256 devices in a mesh: lat: 32 (over z, x_hi, core), lon: 8 (over x_lo, y).
Axes of the slice: x: 4 (x_hi: 2, x_lo: 2; x = x_hi * 2 + x_lo), y: 4, z: 8, core: 2. Of those that a mesh axis runs over, the one named last changes fastest.
Arguments:
- input_field: bfloat16 [128, 2048, 256], P('lat', 'lon'), may hold values from -6 to 6
- grad_out: bfloat16 [128, 2048, 256], P('lat', 'lon'), may hold values from -6 to 6
- weight: bfloat16 [2304, 256], replicated, may hold values from -0.375 to 0.375
- filt: bfloat16 [9, 128, 3, 33], P(None, 'lat'), may hold values from -0.875 to 0.875
- zonal_weight: bfloat16 [9, 128, 3, 2048], P(None, 'lat'), may hold values from -0.078125 to 0.078125
- widths: int32 [128], P('lat'), may hold values from 1 to 16, as said below
- offsets: int32 [128], P('lat'), may hold values from -2 to 0
- polar_rows: int32 [4], replicated, may hold values from 0 to 127, as said below
Outputs:
- input_grad: bfloat16 [128, 2048, 256], P('lat', 'lon')
- weight_grad: float32 [2304, 256], P('lat')
The draws below stay inside these ranges and needn't reach their ends.
Inputs may be any that keep to these rules, and one draw needn't show every extreme that they name: `widths`: every row's half-width is between 1 and 16; the first and last rows have 16. `polar_rows`: four distinct rows: entry 0 is the first row and entry 1 another of the first 4 rows; entry 2 is the last row and entry 3 another of the last 4 rows.
All inputs are finite; a program needn't handle non-finite values.
Results may differ from the reference program's by a relative error of at most 0.0075.
Values may be sent and summed in bfloat16 or wider, within the bound.
A program may use at most 256 MiB of HBM per device.

```python
import math
import jax
import jax.numpy as jnp
from jax import lax

C = 256
K = 9
R = 3
HMAX = 16
ROWS = 4
LONS = 256
NLAT = 128
NLON = 2048
N_LON = 8


def draw_widths(key, part):
    key = jax.random.fold_in(key, 11)
    rows = jnp.arange(NLAT, dtype=jnp.int32)
    distance = jnp.abs(2 * rows + 1 - NLAT)
    base = 1 + (HMAX - 1) * distance // NLAT
    extra = jax.random.randint(key, (NLAT,), 0, 2, dtype=jnp.int32)
    width = jnp.minimum(base + extra, HMAX)
    width = jnp.where((rows == 0) | (rows == NLAT - 1), HMAX, width)
    return width.astype(jnp.int32)


def draw_polar_rows(key, part):
    key = jax.random.fold_in(key, 23)
    picks = jax.random.randint(key, (2,), 1, ROWS, dtype=jnp.int32)
    north = jnp.zeros((1,), jnp.int32)
    south = jnp.full((1,), NLAT - 1, jnp.int32)
    return jnp.concatenate([north, picks[0:1], south, NLAT - 1 - picks[1:2]]).astype(jnp.int32)


def touch_ends(values, stream_key, low, top_value):
    extent = values.shape
    spot = [jax.random.randint(jax.random.fold_in(stream_key, axis), (), 0, extent[axis]) for axis in range(len(extent))]
    values = values.at[tuple(spot)].set(low)
    longest = extent.index(max(extent))
    spot[longest] = (spot[longest] + 1) % extent[longest]
    return values.at[tuple(spot)].set(top_value)


def with_spikes(entries, own_key, source, target, parts, factor):
    def block_of(axis_at):
        return (jnp.arange(entries.shape[axis_at]) // (entries.shape[axis_at] // parts)).reshape((-1,) + (1,) * (entries.ndim - 1 - axis_at))

    one_side = jax.random.permutation(own_key, parts)[block_of(target)]
    second = (block_of(target) + parts // 2) % parts
    return jnp.where((block_of(source) == one_side) | (block_of(source) == second), factor * entries, entries)


def block_scale(key, shape, shards, low, largest):
    def one(dim, shards_of):
        heights = jax.random.uniform(jax.random.fold_in(jax.random.fold_in(key, 6), dim), (shards_of,), jnp.float32, low / len(shards), largest / len(shards))
        return jnp.repeat(jnp.exp(heights), shape[dim] // shards_of).reshape((-1,) + (1,) * (len(shape) - dim - 1))

    loudness = one(*shards[0])
    for cut in shards[1:]:
        loudness = loudness * one(*cut)
    return loudness


def centred(stream_key, extent, scale, bound, split=(), kind=jnp.bfloat16):
    result = jax.random.normal(stream_key, extent, jnp.float32) * scale
    if len(split) > 0:
        result = block_scale(stream_key, extent, split, -0.22, 0.18) * result
    return jnp.clip(result, min=-bound, max=bound).astype(kind)


def heavy_noise(own_key, shape, scale, most, split, heavy, kind=jnp.bfloat16):
    entries = scale * jax.random.normal(own_key, shape, jnp.float32)
    if split:
        entries = entries * block_scale(own_key, shape, split, -0.22, 0.18)
    return jnp.clip(with_spikes(entries, jax.random.fold_in(own_key, 3), *heavy), -most, most).astype(kind)


def setup_inputs(seed: int = 0) -> dict:
    keys = jax.random.split(jax.random.key(seed), 9)
    return {
        "input_field": heavy_noise(keys[0], (NLAT, NLON, C), 1.0, 6.0, ((0, 32), (1, 8)), (0, 2, 32, 2.75)),
        "grad_out": centred(keys[1], (NLAT, NLON, C), 1.0, 6.0, ((0, 32), (1, 8))),
        "weight": centred(keys[2], (K * C, C), C ** -0.5, 0.375),
        "filt": centred(keys[3], (K, NLAT, R, 2 * HMAX + 1), (R * HMAX) ** -0.5, 0.875, ((1, 32),)),
        "zonal_weight": centred(keys[4], (K, NLAT, R, NLON), (R * NLON) ** -0.5, 0.078125, ((1, 32),)),
        "widths": draw_widths(jax.random.fold_in(keys[8], 71), 0),
        "offsets": touch_ends(jax.random.randint(keys[6], (NLAT,), -2, 1), jax.random.fold_in(keys[6], 1), -2, 0).astype(jnp.int32),
        "polar_rows": draw_polar_rows(jax.random.fold_in(keys[8], 71), 0),
    }


def band_matrix(filt_row, width):
    offset_list = jnp.arange(2 * HMAX + 1, dtype=jnp.int32) - HMAX
    keep_mask = jnp.abs(offset_list) <= width
    masked = jnp.where(keep_mask[None, None, :], filt_row.astype(jnp.float32), jnp.zeros((), jnp.float32))
    columns = jnp.arange(LONS + 2 * HMAX, dtype=jnp.int32)
    targets = jnp.arange(LONS, dtype=jnp.int32)
    shifts = jnp.arange(2 * HMAX + 1, dtype=jnp.int32)
    onehot = (columns[None, :, None] - targets[:, None, None] == shifts[None, None, :]).astype(jnp.float32)
    return jnp.einsum('krd,jcd->krjc', masked, onehot)

def reference(input_field, grad_out, weight, filt, zonal_weight, widths, offsets, polar_rows):
    field_pad = jnp.pad(input_field, ((2, 2), (0, 0), (0, 0)))
    field_pad = jnp.concatenate([field_pad[:, NLON - HMAX:], field_pad, field_pad[:, :HMAX]], axis=1)
    starts = jnp.arange(N_LON, dtype=jnp.int32) * LONS
    window = starts[:, None] + jnp.arange(LONS + 2 * HMAX, dtype=jnp.int32)[None, :]
    band_rows = jnp.arange(R, dtype=jnp.int32)
    polar = jnp.any(jnp.arange(NLAT, dtype=jnp.int32)[:, None] == polar_rows[None, :], axis=1).astype(jnp.float32)
    zero_int = jnp.zeros((), jnp.int32)

    def row_step(carry, row_index):
        weight_sum, grad_pad = carry
        source = (row_index + 2 + offsets[row_index] + band_rows).astype(jnp.int32)
        rows_in = jnp.take(field_pad, source, axis=0).astype(jnp.float32)
        bands = band_matrix(filt[:, row_index], widths[row_index])
        windows = rows_in[:, window]
        local = jnp.einsum('krjc,rnch->njkh', bands, windows).reshape(NLON, K * C)
        zonal_w = zonal_weight[:, row_index].astype(jnp.float32)
        zonal_term = jnp.einsum('krj,rjc->kc', zonal_w, rows_in[:, HMAX:HMAX + NLON], precision=lax.Precision.HIGHEST).reshape(K * C)
        field = (local + polar[row_index] * zonal_term[None, :]).astype(jnp.bfloat16)
        grad_row = grad_out[row_index]
        cotangent = jnp.dot(grad_row, weight.T, preferred_element_type=jnp.float32).astype(jnp.bfloat16)
        weight_sum = weight_sum + jnp.dot(field.T, grad_row, preferred_element_type=jnp.float32)
        cot_blocks = cotangent.astype(jnp.float32).reshape(N_LON, LONS, K, C)
        pulled = jnp.einsum('krjc,njkh->rnch', bands, cot_blocks)
        spread = jnp.zeros((R, NLON + 2 * HMAX, C), jnp.float32).at[:, window].add(pulled)
        wrapped_rows = spread[:, HMAX:HMAX + NLON]
        wrapped_rows = wrapped_rows.at[:, NLON - HMAX:].add(spread[:, :HMAX])
        wrapped_rows = wrapped_rows.at[:, :HMAX].add(spread[:, NLON + HMAX:])
        zonal_total = lax.optimization_barrier(jnp.sum(cotangent.astype(jnp.float32), axis=0)).reshape(K, C)
        wrapped_rows = wrapped_rows + polar[row_index] * jnp.einsum('krj,kc->rjc', zonal_w, zonal_total, precision=lax.Precision.HIGHEST)
        first = source[0].astype(jnp.int32)
        current = lax.dynamic_slice(grad_pad, (first, zero_int, zero_int), (R, NLON, C))
        grad_pad = lax.dynamic_update_slice(grad_pad, current + wrapped_rows, (first, zero_int, zero_int))
        return ((weight_sum, grad_pad), None)
    init = (jnp.zeros((K * C, C), jnp.float32), jnp.zeros((NLAT + 4, NLON, C), jnp.float32))
    (weight_sum, grad_pad), _ = lax.scan(row_step, init, jnp.arange(NLAT, dtype=jnp.int32))
    input_grad = grad_pad[2:NLAT + 2].astype(jnp.bfloat16)
    weight_grad = weight_sum * (1.0 / math.sqrt(NLAT * NLON))
    return (input_grad, weight_grad)
```

```python
import functools
import math

import jax
import jax.numpy as jnp
from jax import lax
from jax.experimental import pallas as pl
from jax.experimental.pallas import tpu as pltpu
from jax.sharding import PartitionSpec as P

MESH = pl.DeviceIdType.MESH
F32 = jnp.float32
BF16 = jnp.bfloat16
ROWS = 4
LONS = 256
C = 256
K = 9
REACH = 16
JB = 64
WIN = JB + 2 * REACH
CANDS = 5
DEPTH = 512
N_LAT = 32
N_LON = 8
N_P = 16
GROUPS = ((0, 3), (3, 6), (6, 9))
FACTOR = 1.0 / math.sqrt(128 * 2048)


def dot(a, b, ca=1, cb=0):
    return lax.dot_general(a, b, (((ca,), (cb,)), ((), ())), preferred_element_type=F32)


def kernel(
    g_hbm, x_hbm, w_hbm, v_ref, y_ref, polar_ref,
    ig_hbm, wg_ref,
    gx, xv, xt, wv, wt, vh, yh, vf, tt, hh, yy, ztf, zst, gs_own, gs_buf, gsel,
    wown, wsnd, cx, s1, rb, s2, pr, s3, fin, igv,
    loc_sem, halo_send, halo_recv, vsend, vrecv, ysend, yrecv, gs_send, gs_sem,
    cs_send, cs_recv, ls_send, ls_recv, ps_send, ps_recv, fs_send, fs_recv, out_sem,
):
    lat = lax.axis_index("lat")
    lon = lax.axis_index("lon")
    core = lax.rem(lat, 2)
    p = lax.div(lat, 2)
    twin = lat + 1 - 2 * core

    def lon_at(step):
        return lax.rem(lon + step, N_LON)

    def remote(src, dst, send, recv, to_lat, to_lon):
        return pltpu.make_async_remote_copy(
            src_ref=src, dst_ref=dst, send_sem=send, recv_sem=recv,
            device_id={"lat": to_lat, "lon": to_lon}, device_id_type=MESH,
        )

    g_copy = pltpu.make_async_copy(g_hbm, gx.at[pl.ds(2, ROWS), pl.ds(REACH, LONS)], loc_sem.at[0])
    x_copy = pltpu.make_async_copy(x_hbm, xv, loc_sem.at[1])
    w_copy = pltpu.make_async_copy(w_hbm, wv, loc_sem.at[2])
    g_copy.start()
    x_copy.start()
    w_copy.start()

    barrier = pltpu.get_barrier_semaphore()

    def greet(to_lat, to_lon):
        pl.semaphore_signal(barrier, inc=1, device_id={"lat": to_lat, "lon": to_lon}, device_id_type=MESH)

    outer = lat - 1 + 2 * core
    has_outer = (outer >= 0) & (outer < N_LAT)

    @pl.when(has_outer)
    def _():
        for step in (0, 1, N_LON - 1):
            greet(outer, lon_at(step))

    for step in range(1, N_LON):
        greet(lat, lon_at(step))
    for step in range(N_LON):
        greet(twin, lon_at(step))
    for step in range(1, N_P):
        greet(2 * lax.rem(p + step, N_P) + core, lon)
    pl.semaphore_wait(barrier, 2 * N_LON + N_P - 2 + 3 * has_outer.astype(jnp.int32))

    up, down = lat - 1, lat + 1
    has_up, has_down = lat > 0, lat < N_LAT - 1
    left, right = lon_at(N_LON - 1), lon_at(1)
    rows_of = {-1: (0, 2, 6), 0: (0, ROWS, 2), 1: (2, 2, 0)}
    cols_of = {-1: (0, REACH, REACH + LONS), 0: (0, LONS, REACH), 1: (LONS - REACH, REACH, 0)}
    moves = [(1, 0), (-1, 0), (0, 1), (0, -1), (1, 1), (1, -1), (-1, 1), (-1, -1)]

    def halo(index):
        dlat, dlon = moves[index]
        r0, rn, r_to = rows_of[dlat]
        c0, cn, c_to = cols_of[dlon]
        return remote(
            g_hbm.at[pl.ds(r0, rn), pl.ds(c0, cn)],
            gx.at[pl.ds(r_to, rn), pl.ds(c_to, cn)],
            halo_send.at[index], halo_recv.at[index],
            lat + dlat, lon_at(dlon % N_LON),
        )

    def can_send(index):
        dlat = moves[index][0]
        return has_down if dlat == 1 else has_up

    def can_recv(index):
        dlat = moves[index][0]
        return has_up if dlat == 1 else has_down

    def v_halo(side):
        src = v_ref.at[pl.ds(6, 2)] if side == 0 else v_ref.at[pl.ds(0, 2)]
        return remote(src, vh.at[side], vsend.at[side], vrecv.at[side], down if side == 0 else up, lon)

    for side in range(2):
        @pl.when(has_down if side == 0 else has_up)
        def _():
            v_halo(side).start()

    for index in range(8):
        if moves[index][0] == 0:
            halo(index).start()
        else:
            @pl.when(can_send(index))
            def _():
                halo(index).start()

    north, south = lat == 0, lat == N_LAT - 1
    polar_dev = north | south
    affected = polar_dev | (lat == 1) | (lat == N_LAT - 2)

    def y_halo(first):
        return remote(y_ref.at[pl.ds(first, 2)], yh, ysend, yrecv, twin, lon)

    @pl.when(north)
    def _():
        y_halo(6).start()

    @pl.when(south)
    def _():
        y_halo(0).start()

    g_copy.wait()

    def gs_copy(dc, step):
        return remote(gs_own, gs_buf.at[lon], gs_send.at[dc, step], gs_sem, twin if dc else lat, lon_at(step))

    @pl.when(polar_dev)
    def _():
        gs_own[...] = jnp.zeros_like(gs_own)
        for i in range(ROWS):
            gs_own[pl.ds(i, 1), :] = jnp.sum(
                gx[2 + i, pl.ds(REACH, LONS), :].astype(F32), axis=0, keepdims=True
            )
        for dc in range(2):
            for step in range(N_LON):
                if dc or step:
                    gs_copy(dc, step).start()
        pltpu.make_async_copy(gs_own, gs_buf.at[lon], gs_sem).start()

    @pl.when(lat == 0)
    def _():
        gx[pl.ds(0, 2)] = jnp.zeros((2,) + gx.shape[1:], BF16)
        vh[0] = jnp.zeros(vh.shape[1:], BF16)

    @pl.when(lat == N_LAT - 1)
    def _():
        gx[pl.ds(6, 2)] = jnp.zeros((2,) + gx.shape[1:], BF16)
        vh[1] = jnp.zeros(vh.shape[1:], BF16)

    x_copy.wait()
    for i in range(ROWS):
        xt[:, pl.ds(i * LONS, LONS)] = xv[i].T
    w_copy.wait()

    def turn(k, carry):
        at = pl.ds(pl.multiple_of(k * C, C), C)
        wt[at, :] = wv[at, :].T
        return carry

    lax.fori_loop(0, K, turn, 0)

    for side in range(2):
        @pl.when(has_up if side == 0 else has_down)
        def _():
            v_halo(side).wait_recv()
    for i2 in range(ROWS):
        vf[pl.ds(16 * i2, 16), :] = v_ref[2 + i2].astype(F32) + vh[i2 // 2, i2 % 2].astype(F32)

    def band(index, carry):
        i2, k = lax.div(index, K), lax.rem(index, K)
        row = jnp.broadcast_to(vf[pl.ds(16 * i2 + k, 1), :], (JB, DEPTH))
        rolled = pltpu.roll(row, 0, 1, stride=1, stride_axis=0)
        tt[i2, pl.ds(pl.multiple_of(k * JB, JB), JB), :] = rolled.astype(BF16)
        return carry

    lax.fori_loop(0, ROWS * K, band, 0)

    for i2 in range(ROWS):
        yy[i2] = y_ref[2 + i2]

    @pl.when(lat == 1)
    def _():
        y_halo(6).wait_recv()
        yy[pl.ds(0, 2)] = yh[...]

    @pl.when(lat == N_LAT - 2)
    def _():
        y_halo(0).wait_recv()
        yy[pl.ds(2, 2)] = yh[...]

    circle = jnp.zeros((C, 32), F32)
    for i2 in range(ROWS):
        circle = circle + dot(xt[:, pl.ds(i2 * LONS, LONS)], yy[i2], 1, 1)
    zst[...] = circle * FACTOR

    @pl.when(jnp.logical_not(affected))
    def _():
        gsel[...] = jnp.zeros_like(gsel)

    @pl.when(affected)
    def _():
        pltpu.make_async_copy(gs_buf, gs_buf, gs_sem).wait()
        total = gs_buf[0]
        for step in range(1, N_LON):
            total = total + gs_buf[step]
        pole = lax.div(lat, N_LAT // 2)
        gsel[...] = jnp.zeros_like(gsel)
        for q in range(2):
            mine = polar_ref[2 * pole + q] - pole * (N_LAT - 1) * ROWS
            picked = jnp.zeros((1, C), F32)
            for i in range(ROWS):
                picked = picked + total[i:i + 1] * (mine == i).astype(F32)
            gsel[pl.ds(q, 1), :] = picked

    circle_sum = gsel[...]
    high = circle_sum.astype(BF16)
    low = (circle_sum - high.astype(F32)).astype(BF16)
    parts = jnp.concatenate([high.astype(F32), low.astype(F32)], axis=0).astype(BF16)
    ztf[...] = jnp.zeros_like(ztf)
    for k in range(K):
        mixed = dot(parts, wt[pl.ds(k * C, C), :])
        mixed = mixed[:8] + mixed[8:]
        for q in range(2):
            ztf[pl.ds(16 * q + k, 1), :] = mixed[q:q + 1]

    for index in range(8):
        if moves[index][0] == 0:
            halo(index).wait_recv()
        else:
            @pl.when(can_recv(index))
            def _():
                halo(index).wait_recv()

    def spread(index, carry):
        i2, jb = lax.div(index, LONS // JB), lax.rem(index, LONS // JB)
        at = pl.ds(pl.multiple_of(jb * JB, JB), WIN)
        windows = [gx[i2 + n, at, :] for n in range(CANDS)]
        windows.append(jnp.zeros((DEPTH - CANDS * WIN, C), BF16))
        moved = dot(tt[i2], jnp.concatenate(windows, axis=0)).astype(BF16)
        rows = pl.ds(pl.multiple_of(index * JB, JB), JB)
        for k in range(K):
            hh[rows, pl.ds(k * C, C)] = moved[k * JB:(k + 1) * JB]
        return carry

    lax.fori_loop(0, ROWS * LONS // JB, spread, 0)

    def twin_copy(group):
        k0, k1 = GROUPS[group]
        at = pl.ds(k0, k1 - k0)
        return remote(wsnd.at[at], cx.at[at], cs_send.at[group], cs_recv.at[group], twin, lon)

    def mix(group):
        for k in range(*GROUPS[group]):
            share = dot(xt[...], hh[:, pl.ds(k * C, C)]) * FACTOR
            for q in range(2):
                share = share + zst[:, 16 * q + k:16 * q + k + 1] * gsel[q:q + 1, :]
            first, second = share[:, :128], share[:, 128:]
            wown[k] = jnp.where(core == 0, first, second)
            wsnd[k] = jnp.where(core == 0, second, first).astype(BF16)
        twin_copy(group).start()

    def lon_copy(group, step):
        k0, k1 = GROUPS[group]
        to = lon_at(step)
        at = pl.ds(k0, k1 - k0)
        src = s1.at[at, pl.ds(pl.multiple_of(32 * to, 32), 32)]
        return remote(src, rb.at[lon, at], ls_send.at[group, step], ls_recv.at[group], lat, to)

    def over_lon(group):
        k0, k1 = GROUPS[group]
        at = pl.ds(k0, k1 - k0)
        twin_copy(group).wait_recv()
        for k in range(k0, k1):
            s1[k] = (wown[k] + cx[k].astype(F32)).astype(BF16)
        for step in range(1, N_LON):
            lon_copy(group, step).start()
        own = s1.at[at, pl.ds(pl.multiple_of(32 * lon, 32), 32)]
        pltpu.make_async_copy(own, rb.at[lon, at], ls_recv.at[group]).start()

    def granule(k, b):
        owner = lax.div(16 * k + 2 * lon + b, 9)
        copy = remote(
            s2.at[k, b], pr.at[b, p], ps_send.at[k, b], ps_recv.at[b], 2 * owner + core, lon
        )
        return owner, copy

    def over_lat(group):
        k0, k1 = GROUPS[group]
        slab = rb.at[:, pl.ds(k0, k1 - k0)]
        pltpu.make_async_copy(slab, slab, ls_recv.at[group]).wait()
        for k in range(k0, k1):
            total = rb[0, k].astype(F32)
            for step in range(1, N_LON):
                total = total + rb[step, k].astype(F32)
            total = total.astype(BF16)
            for b in range(2):
                s2[k, b] = total[16 * b:16 * b + 16]
        for k in range(k0, k1):
            for b in range(2):
                owner, copy = granule(k, b)

                @pl.when(owner != p)
                def _():
                    copy.start()

                @pl.when(owner == p)
                def _():
                    pltpu.make_async_copy(s2.at[k, b], pr.at[b, p], ps_recv.at[b]).start()

    def place(b):
        k = lax.div(9 * p - 2 * lon - b + 15, 16)
        e = 16 * k + 2 * lon + b - 9 * p
        return e, e < 9

    def final_copy(b, e, dc, step):
        at = pl.ds(pl.multiple_of(16 * e, 16), 16)
        return remote(
            s3.at[b], fin.at[core, at], fs_send.at[b, dc, step], fs_recv, twin if dc else lat, lon_at(step)
        )

    def needed(e, to_core):
        return ((to_core == 0) & (e <= 4)) | ((to_core == 1) & (e >= 4))

    def spread_out():
        for b in range(2):
            e, valid = place(b)

            @pl.when(valid)
            def _():
                pltpu.make_async_copy(pr.at[b], pr.at[b], ps_recv.at[b]).wait()
                total = pr[b, 0].astype(F32)
                for step in range(1, N_P):
                    total = total + pr[b, step].astype(F32)
                s3[b] = total

            for dc in range(2):
                @pl.when(valid & needed(e, 1 - core if dc else core))
                def _():
                    for step in range(N_LON):
                        if dc or step:
                            final_copy(b, e, dc, step).start()
                        else:
                            at = pl.ds(pl.multiple_of(16 * e, 16), 16)
                            pltpu.make_async_copy(s3.at[b], fin.at[core, at], fs_recv).start()

    def ig_copy(i2):
        return pltpu.make_async_copy(igv.at[i2], ig_hbm.at[i2], out_sem.at[i2])

    circle_total = ztf[...]
    z_high = circle_total.astype(BF16)
    z_low = (circle_total - z_high.astype(F32)).astype(BF16)
    z_parts = jnp.concatenate([z_high, z_low], axis=0)

    def pull(i2):
        grad = dot(hh[pl.ds(i2 * LONS, LONS), :], wt[...])
        twice = jnp.concatenate([yy[i2], yy[i2]], axis=0)
        igv[i2] = (grad + dot(twice, z_parts, 0, 0)).astype(BF16)
        ig_copy(i2).start()

    mix(0)
    mix(1)
    over_lon(0)
    mix(2)
    over_lon(1)
    over_lat(0)
    pull(0)
    over_lon(2)
    over_lat(1)
    pull(1)
    over_lat(2)
    pull(2)
    spread_out()
    pull(3)
    some = fin.at[:, pl.ds(0, 80)]
    pltpu.make_async_copy(some, some, fs_recv).wait()
    rows = pl.ds(pl.multiple_of(72 * core, 8), 72)
    for half in range(2):
        wg_ref[:, pl.ds(128 * half, 128)] = fin[half, rows, :]

    for i2 in range(ROWS):
        ig_copy(i2).wait()
    for index in range(8):
        if moves[index][0] == 0:
            halo(index).wait_send()
        else:
            @pl.when(can_send(index))
            def _():
                halo(index).wait_send()
    for side in range(2):
        @pl.when(has_down if side == 0 else has_up)
        def _():
            v_halo(side).wait_send()

    @pl.when(north)
    def _():
        y_halo(6).wait_send()

    @pl.when(south)
    def _():
        y_halo(0).wait_send()

    @pl.when(polar_dev)
    def _():
        for dc in range(2):
            for step in range(N_LON):
                if dc or step:
                    gs_copy(dc, step).wait_send()

    for group in range(len(GROUPS)):
        twin_copy(group).wait_send()
        for step in range(1, N_LON):
            lon_copy(group, step).wait_send()
    for k in range(K):
        for b in range(2):
            owner, copy = granule(k, b)

            @pl.when(owner != p)
            def _():
                copy.wait_send()
    for b in range(2):
        e, valid = place(b)
        for dc in range(2):
            @pl.when(valid & needed(e, 1 - core if dc else core))
            def _():
                for step in range(N_LON):
                    if dc or step:
                        final_copy(b, e, dc, step).wait_send()


def filter_rows(filt, widths, offsets):
    span = jnp.arange(2 * REACH + 1, dtype=jnp.int32) - REACH
    keep = jnp.abs(span)[None, :] <= widths[:, None]
    masked = jnp.where(keep[None, :, None, :], filt, jnp.zeros_like(filt))[..., ::-1]
    pieces = []
    for n in range(CANDS):
        picked = jnp.zeros((K, ROWS, 2 * REACH + 1), BF16)
        for r in range(3):
            hit = (offsets == 2 - n - r)[None, :, None]
            picked = jnp.where(hit, masked[:, :, r], picked)
        moved = jnp.transpose(picked, (1, 0, 2))
        lanes = WIN - 2 * REACH - 1 + (DEPTH - CANDS * WIN if n == CANDS - 1 else 0)
        pieces.append(jnp.pad(moved, ((4 - n, n), (0, 16 - K), (0, lanes))))
    return jnp.concatenate(pieces, axis=2)


def circle_rows(zonal_weight, offsets, polar_rows):
    lat = lax.axis_index("lat")
    pole = lat // (N_LAT // 2)
    own = lax.dynamic_slice_in_dim(zonal_weight, lax.axis_index("lon") * LONS, LONS, 3)
    mine = lax.dynamic_slice_in_dim(polar_rows, 2 * pole, 2) - lat * ROWS
    slot = jnp.arange(8, dtype=jnp.int32) - 2
    row = jnp.arange(ROWS, dtype=jnp.int32)
    band = jnp.arange(3, dtype=jnp.int32)
    hit = (row[None, :] == mine[:, None])[None, :, :, None] & (
        (slot[:, None] - row[None, :] - offsets[None, :])[:, None, :, None] == band
    )
    picked = jnp.einsum("sqir,kirj->sqkj", hit.astype(BF16), own, preferred_element_type=F32)
    return jnp.pad(picked.astype(BF16), ((0, 0), (0, 0), (0, 16 - K), (0, 0))).reshape(8, 32, LONS)


def body(input_field, grad_out, weight, filt, zonal_weight, widths, offsets, polar_rows):
    values = filter_rows(filt, widths, offsets)
    circle = circle_rows(zonal_weight, offsets, polar_rows)
    dma = pltpu.SemaphoreType.DMA
    anywhere = pl.BlockSpec(memory_space=pl.ANY)
    vmem = pl.BlockSpec(memory_space=pltpu.VMEM)
    groups = len(GROUPS)
    return pl.pallas_call(
        kernel,
        out_shape=(
            jax.ShapeDtypeStruct((ROWS, LONS, C), BF16),
            jax.ShapeDtypeStruct((72, C), F32),
        ),
        in_specs=[anywhere, anywhere, anywhere, vmem, vmem, pl.BlockSpec(memory_space=pltpu.SMEM)],
        out_specs=(anywhere, vmem),
        scratch_shapes=[
            pltpu.VMEM((8, LONS + 2 * REACH, C), BF16),
            pltpu.VMEM((ROWS, LONS, C), BF16),
            pltpu.VMEM((C, ROWS * LONS), BF16),
            pltpu.VMEM((K * C, C), BF16),
            pltpu.VMEM((K * C, C), BF16),
            pltpu.VMEM((2, 2, 16, DEPTH), BF16),
            pltpu.VMEM((2, 32, LONS), BF16),
            pltpu.VMEM((ROWS * 16, DEPTH), F32),
            pltpu.VMEM((ROWS, K * JB, DEPTH), BF16),
            pltpu.VMEM((ROWS * LONS, K * C), BF16),
            pltpu.VMEM((ROWS, 32, LONS), BF16),
            pltpu.VMEM((32, C), F32),
            pltpu.VMEM((C, 32), F32),
            pltpu.VMEM((8, C), F32),
            pltpu.VMEM((N_LON, 8, C), F32),
            pltpu.VMEM((8, C), F32),
            pltpu.VMEM((K, C, 128), F32),
            pltpu.VMEM((K, C, 128), BF16),
            pltpu.VMEM((K, C, 128), BF16),
            pltpu.VMEM((K, C, 128), BF16),
            pltpu.VMEM((N_LON, K, 32, 128), BF16),
            pltpu.VMEM((K, 2, 16, 128), BF16),
            pltpu.VMEM((2, N_P, 16, 128), BF16),
            pltpu.VMEM((2, 16, 128), F32),
            pltpu.VMEM((2, 144, 128), F32),
            pltpu.VMEM((ROWS, LONS, C), BF16),
            dma((3,)), dma((8,)), dma((8,)), dma((2,)), dma((2,)), dma, dma, dma((2, N_LON)), dma,
            dma((groups,)), dma((groups,)), dma((groups, N_LON)), dma((groups,)),
            dma((K, 2)), dma((2,)), dma((2, 2, N_LON)), dma, dma((ROWS,)),
        ],
        compiler_params=pltpu.CompilerParams(
            collective_id=0, has_side_effects=True, vmem_limit_bytes=48 * 1024 * 1024
        ),
        name="sphere_backward",
    )(grad_out, input_field, weight, values, circle, polar_rows)


def solution(mesh):
    in_specs = (
        P("lat", "lon", None),
        P("lat", "lon", None),
        P(),
        P(None, "lat", None, None),
        P(None, "lat", None, None),
        P("lat"),
        P("lat"),
        P(),
    )
    out_specs = (P("lat", "lon", None), P("lat", None))
    return jax.shard_map(body, mesh=mesh, in_specs=in_specs, out_specs=out_specs, check_vma=False)
```

```python
import functools
import math

import jax
import jax.numpy as jnp
from jax import lax
from jax.experimental import pallas as pl
from jax.experimental.pallas import tpu as pltpu
from jax.sharding import PartitionSpec as P

MESH = pl.DeviceIdType.MESH
F32 = jnp.float32
BF16 = jnp.bfloat16
ROWS = 4
LONS = 256
C = 256
K = 9
REACH = 16
JB = 64
WIN = JB + 2 * REACH
CANDS = 5
DEPTH = 512
N_LAT = 32
N_LON = 8
N_P = 16
GROUPS = ((0, 3), (3, 6), (6, 9))
FACTOR = 1.0 / math.sqrt(128 * 2048)


def dot(a, b, ca=1, cb=0):
    return lax.dot_general(a, b, (((ca,), (cb,)), ((), ())), preferred_element_type=F32)


def kernel(
    g_hbm, x_hbm, w_hbm, filt_ref, z_hbm, width_ref, offset_ref, polar_ref,
    ig_hbm, wg_ref,
    gx, xv, xt, wv, wt, lv, vown, vh, vf, tt, hh, zv, zs, yf, yown, yh, yy, ztf, zst, gs_own, gs_buf, gsel,
    wown, wsnd, cx, s1, rb, s2, pr, s3, fin, igv,
    loc_sem, halo_send, halo_recv, vsend, vrecv, ysend, yrecv, gs_send, gs_sem,
    cs_send, cs_recv, ls_send, ls_recv, ps_send, ps_recv, fs_send, fs_recv, out_sem,
):
    lat = lax.axis_index("lat")
    lon = lax.axis_index("lon")
    core = lax.rem(lat, 2)
    p = lax.div(lat, 2)
    twin = lat + 1 - 2 * core

    def lon_at(step):
        return lax.rem(lon + step, N_LON)

    def remote(src, dst, send, recv, to_lat, to_lon, tag="rs"):
        return pltpu.make_async_remote_copy(
            src_ref=src, dst_ref=dst, send_sem=send, recv_sem=recv,
            device_id={"lat": to_lat, "lon": to_lon}, device_id_type=MESH,
        )

    north, south = lat == 0, lat == N_LAT - 1
    polar_dev = north | south
    affected = polar_dev | (lat == 1) | (lat == N_LAT - 2)

    g_copy = pltpu.make_async_copy(g_hbm, gx.at[pl.ds(2, ROWS), pl.ds(REACH, LONS)], loc_sem.at[0])
    x_copy = pltpu.make_async_copy(x_hbm, xv, loc_sem.at[1])
    w_copy = pltpu.make_async_copy(w_hbm, wv, loc_sem.at[2])
    z_copy = pltpu.make_async_copy(
        z_hbm.at[:, :, :, pl.ds(pl.multiple_of(lon * LONS, LONS), LONS)], zv, loc_sem.at[3]
    )
    g_copy.start()
    x_copy.start()
    w_copy.start()

    @pl.when(polar_dev)
    def _():
        z_copy.start()

    barrier = pltpu.get_barrier_semaphore()

    def greet(to_lat, to_lon):
        pl.semaphore_signal(barrier, inc=1, device_id={"lat": to_lat, "lon": to_lon}, device_id_type=MESH)

    outer = lat - 1 + 2 * core
    has_outer = (outer >= 0) & (outer < N_LAT)

    @pl.when(has_outer)
    def _():
        for step in (0, 1, N_LON - 1):
            greet(outer, lon_at(step))

    for step in range(1, N_P):
        greet(2 * lax.rem(p + step, N_P) + core, lon)
    for step in range(1, N_LON):
        greet(lat, lon_at(step))
    for step in range(N_LON):
        greet(twin, lon_at(step))

    span = 2 * REACH + 1
    row_i = lax.broadcasted_iota(jnp.int32, (ROWS, span), 0)
    tap = lax.broadcasted_iota(jnp.int32, (ROWS, span), 1)
    offset_v = jnp.zeros((ROWS, span), jnp.int32)
    width_v = jnp.zeros((ROWS, span), jnp.int32)
    for i in range(ROWS):
        offset_v = jnp.where(row_i == i, offset_ref[i], offset_v)
        width_v = jnp.where(row_i == i, width_ref[i], width_v)
    keep = jnp.abs(tap - REACH) <= width_v
    choose = {m: jnp.where(keep & (offset_v == 2 - m), 1.0, 0.0) for m in (2, 3, 4)}
    lv[...] = jnp.zeros_like(lv)
    for k in range(K):
        values = [filt_ref[k, r].astype(F32) for r in range(3)]
        for n in range(CANDS):
            terms = [choose[n + r] * values[r] for r in range(3) if n + r in choose]
            lv[n, pl.ds((4 - n) * 16 + k, ROWS, stride=16), :] = functools.reduce(jnp.add, terms)
    tap = lax.broadcasted_iota(jnp.int32, (span, DEPTH), 0)
    lane = lax.broadcasted_iota(jnp.int32, (span, DEPTH), 1)
    placed = jnp.zeros((128, DEPTH), F32)
    for n in range(CANDS):
        where = jnp.where(lane + tap == WIN * n + 2 * REACH, 1.0, 0.0).astype(BF16)
        placed = placed + dot(lv[n].astype(BF16), where)
    vown[...] = placed.astype(BF16).reshape(8, 16, DEPTH)

    pl.semaphore_wait(barrier, 2 * N_LON + N_P - 2 + 3 * has_outer.astype(jnp.int32))

    up, down = lat - 1, lat + 1
    has_up, has_down = lat > 0, lat < N_LAT - 1
    rows_of = {-1: (0, 2, 6), 0: (0, ROWS, 2), 1: (2, 2, 0)}
    cols_of = {-1: (0, REACH, REACH + LONS), 0: (0, LONS, REACH), 1: (LONS - REACH, REACH, 0)}
    moves = [(1, 0), (-1, 0), (1, 1), (1, -1), (-1, 1), (-1, -1), (0, 1), (0, -1)]
    from_up = [index for index in range(8) if moves[index][0] == 1]
    from_down = [index for index in range(8) if moves[index][0] == -1]
    level = [index for index in range(8) if moves[index][0] == 0]

    def halo(index):
        dlat, dlon = moves[index]
        r0, rn, r_to = rows_of[dlat]
        c0, cn, c_to = cols_of[dlon]
        return remote(
            g_hbm.at[pl.ds(r0, rn), pl.ds(c0, cn)],
            gx.at[pl.ds(r_to, rn), pl.ds(c_to, cn)],
            halo_send.at[index], halo_recv.at[index],
            lat + dlat, lon_at(dlon % N_LON), "halo",
        )

    def v_halo(side):
        src = vown.at[pl.ds(6, 2)] if side == 0 else vown.at[pl.ds(0, 2)]
        return remote(src, vh.at[side], vsend.at[side], vrecv.at[side], down if side == 0 else up, lon, "halo")

    @pl.when(has_down)
    def _():
        v_halo(0).start()
        for index in from_up:
            halo(index).start()

    @pl.when(has_up)
    def _():
        v_halo(1).start()
        for index in from_down:
            halo(index).start()

    for index in level:
        halo(index).start()

    g_copy.wait()

    def gs_copy(dc, step):
        return remote(
            gs_own, gs_buf.at[lon], gs_send.at[dc, step], gs_sem, twin if dc else lat, lon_at(step), "halo"
        )

    def y_halo(first):
        return remote(yown.at[pl.ds(first, 2)], yh, ysend, yrecv, twin, lon, "halo")

    @pl.when(jnp.logical_not(polar_dev))
    def _():
        yown[...] = jnp.zeros_like(yown)

    @pl.when(polar_dev)
    def _():
        gs_own[...] = jnp.zeros_like(gs_own)
        for i in range(ROWS):
            gs_own[pl.ds(i, 1), :] = jnp.sum(
                gx[2 + i, pl.ds(REACH, LONS), :].astype(F32), axis=0, keepdims=True
            )
        for dc in range(2):
            for step in range(N_LON):
                if dc or step:
                    gs_copy(dc, step).start()
        pltpu.make_async_copy(gs_own, gs_buf.at[lon], gs_sem).start()
        pole = lax.div(lat, N_LAT // 2)
        entry = lax.broadcasted_iota(jnp.int32, (16, 16), 0)
        source = lax.broadcasted_iota(jnp.int32, (16, 16), 1)
        row = source & 3
        first_q = polar_ref[2 * pole] - lat * ROWS
        second_q = polar_ref[2 * pole + 1] - lat * ROWS
        polar_row = jnp.where((entry & 1) == 0, first_q, second_q)
        moved = row + (source >> 2)
        for i in range(ROWS):
            moved = moved + jnp.where(row == i, offset_ref[i], 0)
        hit = (row == polar_row) & (moved == (entry >> 1) - 2) & (source < 12)
        z_copy.wait()
        zs[pl.ds(8, 8), :] = jnp.zeros((8, K * LONS), F32)
        for k in range(K):
            for r in range(3):
                zs[pl.ds(4 * r, 4), pl.ds(k * LONS, LONS)] = zv[k, r].astype(F32)
        picked = dot(jnp.where(hit, 1.0, 0.0).astype(BF16), zs[...].astype(BF16))
        yf[...] = jnp.zeros_like(yf)
        for k in range(K):
            for half in range(2):
                yf[half, pl.ds(k, 16, stride=16), :] = picked[:, k * LONS + 128 * half:k * LONS + 128 * half + 128]
        for half in range(2):
            yown[:, :, pl.ds(128 * half, 128)] = yf[half].astype(BF16).reshape(8, 32, 128)

    @pl.when(north)
    def _():
        y_halo(6).start()

    @pl.when(south)
    def _():
        y_halo(0).start()

    @pl.when(north)
    def _():
        gx[pl.ds(0, 2)] = jnp.zeros((2,) + gx.shape[1:], BF16)
        vh[0] = jnp.zeros(vh.shape[1:], BF16)

    @pl.when(south)
    def _():
        gx[pl.ds(6, 2)] = jnp.zeros((2,) + gx.shape[1:], BF16)
        vh[1] = jnp.zeros(vh.shape[1:], BF16)

    x_copy.wait()
    for i in range(ROWS):
        xt[:, pl.ds(i * LONS, LONS)] = xv[i].T
    w_copy.wait()

    def turn(k, carry):
        at = pl.ds(pl.multiple_of(k * C, C), C)
        wt[at, :] = wv[at, :].T
        return carry

    lax.fori_loop(0, K, turn, 0)

    def band_rows(base, side):
        for a in range(2):
            vf[pl.ds(16 * a, 16), :] = vown[2 + base + a].astype(F32) + vh[side, a].astype(F32)

        def band(k, carry):
            for a in range(2):
                row = jnp.broadcast_to(vf[pl.ds(16 * a + k, 1), :], (JB, DEPTH))
                rolled = pltpu.roll(row, 0, 1, stride=1, stride_axis=0)
                tt[base + a, pl.ds(pl.multiple_of(k * JB, JB), JB), :] = rolled.astype(BF16)
            return carry

        lax.fori_loop(0, K, band, 0)

    def spread_rows(base, k0, k1):
        def spread(step, carry):
            for half in range(2):
                index = 2 * step + half
                i2, jb = base + lax.div(index, LONS // JB), lax.rem(index, LONS // JB)
                at = pl.ds(pl.multiple_of(jb * JB, JB), WIN)
                windows = [gx[i2 + n, at, :] for n in range(CANDS)]
                windows.append(jnp.zeros((DEPTH - CANDS * WIN, C), BF16))
                moved = dot(tt[i2, pl.ds(k0 * JB, (k1 - k0) * JB)], jnp.concatenate(windows, axis=0)).astype(BF16)
                rows = pl.ds(pl.multiple_of(i2 * LONS + jb * JB, JB), JB)
                for k in range(k0, k1):
                    hh[rows, pl.ds(k * C, C)] = moved[(k - k0) * JB:(k - k0 + 1) * JB]
            return carry

        lax.fori_loop(0, LONS // JB, spread, 0)

    near, far = 2 - 2 * core, 2 * core

    def arrive(index_list):
        for index in index_list:
            halo(index).wait_recv()

    arrive(level)

    @pl.when(core == 0)
    def _():
        v_halo(1).wait_recv()
        arrive(from_down)

    @pl.when(core == 1)
    def _():
        v_halo(0).wait_recv()
        arrive(from_up)

    band_rows(near, 1 - core)
    spread_rows(near, 0, K)

    @pl.when((core == 0) & has_up)
    def _():
        v_halo(0).wait_recv()

    @pl.when((core == 1) & has_down)
    def _():
        v_halo(1).wait_recv()

    band_rows(far, core)

    for i2 in range(ROWS):
        yy[i2] = yown[2 + i2]

    @pl.when(lat == 1)
    def _():
        y_halo(6).wait_recv()
        yy[pl.ds(0, 2)] = yh[...]

    @pl.when(lat == N_LAT - 2)
    def _():
        y_halo(0).wait_recv()
        yy[pl.ds(2, 2)] = yh[...]

    circle = jnp.zeros((C, 32), F32)
    for i2 in range(ROWS):
        circle = circle + dot(xt[:, pl.ds(i2 * LONS, LONS)], yy[i2], 1, 1)
    zst[...] = circle * FACTOR

    @pl.when(jnp.logical_not(affected))
    def _():
        gsel[...] = jnp.zeros_like(gsel)

    @pl.when(affected)
    def _():
        pltpu.make_async_copy(gs_buf, gs_buf, gs_sem).wait()
        total = gs_buf[0]
        for step in range(1, N_LON):
            total = total + gs_buf[step]
        pole = lax.div(lat, N_LAT // 2)
        gsel[...] = jnp.zeros_like(gsel)
        for q in range(2):
            mine = polar_ref[2 * pole + q] - pole * (N_LAT - 1) * ROWS
            picked = jnp.zeros((1, C), F32)
            for i in range(ROWS):
                picked = picked + total[i:i + 1] * (mine == i).astype(F32)
            gsel[pl.ds(q, 1), :] = picked

    circle_sum = gsel[...]
    high = circle_sum.astype(BF16)
    low = (circle_sum - high.astype(F32)).astype(BF16)
    parts = jnp.concatenate([high.astype(F32), low.astype(F32)], axis=0).astype(BF16)
    ztf[...] = jnp.zeros_like(ztf)
    for k in range(K):
        mixed = dot(parts, wt[pl.ds(k * C, C), :])
        mixed = mixed[:8] + mixed[8:]
        for q in range(2):
            ztf[pl.ds(16 * q + k, 1), :] = mixed[q:q + 1]

    @pl.when((core == 0) & has_up)
    def _():
        arrive(from_up)

    @pl.when((core == 1) & has_down)
    def _():
        arrive(from_down)

    def twin_copy(group):
        k0, k1 = GROUPS[group]
        at = pl.ds(k0, k1 - k0)
        return remote(wsnd.at[at], cx.at[at], cs_send.at[group], cs_recv.at[group], twin, lon)

    def mix(group):
        for k in range(*GROUPS[group]):
            share = dot(xt[...], hh[:, pl.ds(k * C, C)]) * FACTOR
            for q in range(2):
                share = share + zst[:, 16 * q + k:16 * q + k + 1] * gsel[q:q + 1, :]
            first, second = share[:, :128], share[:, 128:]
            wown[k] = jnp.where(core == 0, first, second)
            wsnd[k] = jnp.where(core == 0, second, first).astype(BF16)
        twin_copy(group).start()

    def lon_copy(group, step):
        k0, k1 = GROUPS[group]
        to = lon_at(step)
        at = pl.ds(k0, k1 - k0)
        src = s1.at[at, pl.ds(pl.multiple_of(32 * to, 32), 32)]
        return remote(src, rb.at[lon, at], ls_send.at[group, step], ls_recv.at[group], lat, to)

    def over_lon(group):
        k0, k1 = GROUPS[group]
        at = pl.ds(k0, k1 - k0)
        twin_copy(group).wait_recv()
        for k in range(k0, k1):
            s1[k] = (wown[k] + cx[k].astype(F32)).astype(BF16)
        for step in range(1, N_LON):
            lon_copy(group, step).start()
        own = s1.at[at, pl.ds(pl.multiple_of(32 * lon, 32), 32)]
        pltpu.make_async_copy(own, rb.at[lon, at], ls_recv.at[group]).start()

    def granule(k, b):
        owner = lax.div(16 * k + 2 * lon + b, 9)
        copy = remote(
            s2.at[k, b], pr.at[b, p], ps_send.at[k, b], ps_recv.at[b], 2 * owner + core, lon
        )
        return owner, copy

    def over_lat(group):
        k0, k1 = GROUPS[group]
        slab = rb.at[:, pl.ds(k0, k1 - k0)]
        pltpu.make_async_copy(slab, slab, ls_recv.at[group]).wait()
        for k in range(k0, k1):
            total = rb[0, k].astype(F32)
            for step in range(1, N_LON):
                total = total + rb[step, k].astype(F32)
            total = total.astype(BF16)
            for b in range(2):
                s2[k, b] = total[16 * b:16 * b + 16]
        for k in range(k0, k1):
            for b in range(2):
                owner, copy = granule(k, b)

                @pl.when(owner != p)
                def _():
                    copy.start()

                @pl.when(owner == p)
                def _():
                    pltpu.make_async_copy(s2.at[k, b], pr.at[b, p], ps_recv.at[b]).start()

    def place(b):
        k = lax.div(9 * p - 2 * lon - b + 15, 16)
        e = 16 * k + 2 * lon + b - 9 * p
        return e, e < 9

    def final_copy(b, e, dc, step):
        at = pl.ds(pl.multiple_of(16 * e, 16), 16)
        return remote(
            s3.at[b], fin.at[core, at], fs_send.at[b, dc, step], fs_recv, twin if dc else lat, lon_at(step)
        )

    def needed(e, to_core):
        return ((to_core == 0) & (e <= 4)) | ((to_core == 1) & (e >= 4))

    def spread_out():
        for b in range(2):
            e, valid = place(b)

            @pl.when(valid)
            def _():
                pltpu.make_async_copy(pr.at[b], pr.at[b], ps_recv.at[b]).wait()
                total = pr[b, 0].astype(F32)
                for step in range(1, N_P):
                    total = total + pr[b, step].astype(F32)
                s3[b] = total

            for dc in range(2):
                @pl.when(valid & needed(e, 1 - core if dc else core))
                def _():
                    for step in range(N_LON):
                        if dc or step:
                            final_copy(b, e, dc, step).start()
                        else:
                            at = pl.ds(pl.multiple_of(16 * e, 16), 16)
                            pltpu.make_async_copy(s3.at[b], fin.at[core, at], fs_recv).start()

    def ig_copy(i2):
        return pltpu.make_async_copy(igv.at[i2], ig_hbm.at[i2], out_sem.at[i2])

    circle_total = ztf[...]
    z_high = circle_total.astype(BF16)
    z_low = (circle_total - z_high.astype(F32)).astype(BF16)
    z_parts = jnp.concatenate([z_high, z_low], axis=0)

    def pull(half):
        grad = dot(hh[pl.ds(half * 2 * LONS, 2 * LONS), :], wt[...])
        for a in range(2):
            i2 = 2 * half + a
            twice = jnp.concatenate([yy[i2], yy[i2]], axis=0)
            igv[i2] = (grad[a * LONS:(a + 1) * LONS] + dot(twice, z_parts, 0, 0)).astype(BF16)
            ig_copy(i2).start()

    spread_rows(far, *GROUPS[0])
    mix(0)
    spread_rows(far, *GROUPS[1])
    mix(1)
    over_lon(0)
    spread_rows(far, *GROUPS[2])
    mix(2)
    over_lon(1)
    over_lat(0)
    over_lon(2)
    over_lat(1)
    pull(0)
    over_lat(2)
    pull(1)
    spread_out()
    for index in level:
        halo(index).wait_send()

    @pl.when(has_down)
    def _():
        v_halo(0).wait_send()
        for index in from_up:
            halo(index).wait_send()

    @pl.when(has_up)
    def _():
        v_halo(1).wait_send()
        for index in from_down:
            halo(index).wait_send()

    @pl.when(north)
    def _():
        y_halo(6).wait_send()

    @pl.when(south)
    def _():
        y_halo(0).wait_send()

    @pl.when(polar_dev)
    def _():
        for dc in range(2):
            for step in range(N_LON):
                if dc or step:
                    gs_copy(dc, step).wait_send()

    for group in range(len(GROUPS)):
        twin_copy(group).wait_send()
        for step in range(1, N_LON):
            lon_copy(group, step).wait_send()
    for k in range(K):
        for b in range(2):
            owner, copy = granule(k, b)

            @pl.when(owner != p)
            def _():
                copy.wait_send()
    some = fin.at[:, pl.ds(0, 80)]
    pltpu.make_async_copy(some, some, fs_recv).wait()
    rows = pl.ds(pl.multiple_of(72 * core, 8), 72)
    for half in range(2):
        wg_ref[:, pl.ds(128 * half, 128)] = fin[half, rows, :]

    for b in range(2):
        e, valid = place(b)
        for dc in range(2):
            @pl.when(valid & needed(e, 1 - core if dc else core))
            def _():
                for step in range(N_LON):
                    if dc or step:
                        final_copy(b, e, dc, step).wait_send()
    for i2 in range(ROWS):
        ig_copy(i2).wait()


def body(input_field, grad_out, weight, filt, zonal_weight, widths, offsets, polar_rows):
    dma = pltpu.SemaphoreType.DMA
    hbm = pl.BlockSpec(memory_space=pltpu.HBM)
    vmem = pl.BlockSpec(memory_space=pltpu.VMEM)
    smem = pl.BlockSpec(memory_space=pltpu.SMEM)
    groups = len(GROUPS)
    return pl.pallas_call(
        kernel,
        out_shape=(
            jax.ShapeDtypeStruct((ROWS, LONS, C), BF16),
            jax.ShapeDtypeStruct((72, C), F32),
        ),
        in_specs=[hbm, hbm, hbm, vmem, hbm, smem, smem, smem],
        out_specs=(pl.BlockSpec(memory_space=pl.ANY), vmem),
        scratch_shapes=[
            pltpu.VMEM((8, LONS + 2 * REACH, C), BF16),
            pltpu.VMEM((ROWS, LONS, C), BF16),
            pltpu.VMEM((C, ROWS * LONS), BF16),
            pltpu.VMEM((K * C, C), BF16),
            pltpu.VMEM((K * C, C), BF16),
            pltpu.VMEM((CANDS, 128, 2 * REACH + 1), F32),
            pltpu.VMEM((8, 16, DEPTH), BF16),
            pltpu.VMEM((2, 2, 16, DEPTH), BF16),
            pltpu.VMEM((32, DEPTH), F32),
            pltpu.VMEM((ROWS, K * JB, DEPTH), BF16),
            pltpu.VMEM((ROWS * LONS, K * C), BF16),
            pltpu.VMEM((K, 3, ROWS, LONS), BF16),
            pltpu.VMEM((16, K * LONS), F32),
            pltpu.VMEM((2, 256, 128), F32),
            pltpu.VMEM((8, 32, LONS), BF16),
            pltpu.VMEM((2, 32, LONS), BF16),
            pltpu.VMEM((ROWS, 32, LONS), BF16),
            pltpu.VMEM((32, C), F32),
            pltpu.VMEM((C, 32), F32),
            pltpu.VMEM((8, C), F32),
            pltpu.VMEM((N_LON, 8, C), F32),
            pltpu.VMEM((8, C), F32),
            pltpu.VMEM((K, C, 128), F32),
            pltpu.VMEM((K, C, 128), BF16),
            pltpu.VMEM((K, C, 128), BF16),
            pltpu.VMEM((K, C, 128), BF16),
            pltpu.VMEM((N_LON, K, 32, 128), BF16),
            pltpu.VMEM((K, 2, 16, 128), BF16),
            pltpu.VMEM((2, N_P, 16, 128), BF16),
            pltpu.VMEM((2, 16, 128), F32),
            pltpu.VMEM((2, 144, 128), F32),
            pltpu.VMEM((ROWS, LONS, C), BF16),
            dma((4,)), dma((8,)), dma((8,)), dma((2,)), dma((2,)), dma, dma, dma((2, N_LON)), dma,
            dma((groups,)), dma((groups,)), dma((groups, N_LON)), dma((groups,)),
            dma((K, 2)), dma((2,)), dma((2, 2, N_LON)), dma, dma((ROWS,)),
        ],
        compiler_params=pltpu.CompilerParams(
            collective_id=0, has_side_effects=True, vmem_limit_bytes=60 * 1024 * 1024
        ),
        name="sphere_backward",
    )(
        grad_out, input_field, weight, jnp.transpose(filt, (0, 2, 1, 3)),
        jnp.transpose(zonal_weight, (0, 2, 1, 3)), widths, offsets, polar_rows,
    )


def solution(mesh):
    in_specs = (
        P("lat", "lon", None),
        P("lat", "lon", None),
        P(),
        P(None, "lat", None, None),
        P(None, "lat", None, None),
        P("lat"),
        P("lat"),
        P(),
    )
    out_specs = (P("lat", "lon", None), P("lat", None))
    return jax.shard_map(body, mesh=mesh, in_specs=in_specs, out_specs=out_specs, check_vma=False)
```

```python
import functools
import math

import jax
import jax.numpy as jnp
from jax import lax
from jax.experimental import pallas as pl
from jax.experimental.pallas import tpu as pltpu
from jax.sharding import PartitionSpec as P

MESH = pl.DeviceIdType.MESH
F32 = jnp.float32
BF16 = jnp.bfloat16
ROWS = 4
LONS = 256
C = 256
K = 9
REACH = 16
JB = 64
WIN = JB + 2 * REACH
CANDS = 5
DEPTH = 512
N_LAT = 32
N_LON = 8
N_Z = 8
GROUPS = ((0, 3), (3, 6), (6, 9))
RUNS = ((0, 3, "y"), (3, 6, "x"), (6, 8, "y"), (8, 9, "x"))
GROUP_RUNS = ((0,), (1,), (2, 3))
FACTOR = 1.0 / math.sqrt(128 * 2048)


def dot(a, b, ca=1, cb=0):
    return lax.dot_general(a, b, (((ca,), (cb,)), ((), ())), preferred_element_type=F32)


def kernel(
    g_hbm, x_hbm, w_hbm, filt_ref, z_hbm, width_ref, offset_ref, polar_ref,
    ig_ref, wg_ref,
    gx, xv, xt, wv, wt, lv, vown, vh, vf, tt, hh, zv, zs, yf, yown, yh, yy, ztf, zst, gs_own, gs_buf, gsel,
    wown, wsnd, cx, s1, r1, s2, r2, s3, r3, s4, fin,
    loc_sem, halo_send, halo_recv, vsend, vrecv, ysend, yrecv, gs_send, gs_sem,
    cs_send, cs_recv, send1, recv1, send2, recv2, send3, recv3, fs_send, fs_recv,
):
    lat = lax.axis_index("lat")
    lon = lax.axis_index("lon")
    core = lax.rem(lat, 2)
    twin = lat + 1 - 2 * core
    z, in_plane = lax.div(lat, 4), lax.rem(lat, 4)
    x_high, x_low, y = lax.div(in_plane, 2), lax.div(lon, 4), lax.rem(lon, 4)
    place = {"x": 2 * x_high + x_low, "y": y}

    def lon_at(step):
        return lax.rem(lon + step, N_LON)

    def remote(src, dst, send, recv, to_lat, to_lon, tag="rs"):
        return pltpu.make_async_remote_copy(
            src_ref=src, dst_ref=dst, send_sem=send, recv_sem=recv,
            device_id={"lat": to_lat, "lon": to_lon}, device_id_type=MESH,
        )

    north, south = lat == 0, lat == N_LAT - 1
    polar_dev = north | south
    affected = polar_dev | (lat == 1) | (lat == N_LAT - 2)

    g_copy = pltpu.make_async_copy(g_hbm, gx.at[pl.ds(2, ROWS), pl.ds(REACH, LONS)], loc_sem.at[0])
    x_copy = pltpu.make_async_copy(x_hbm, xv, loc_sem.at[1])
    w_copy = pltpu.make_async_copy(w_hbm, wv, loc_sem.at[2])
    z_copy = pltpu.make_async_copy(
        z_hbm.at[:, :, :, pl.ds(pl.multiple_of(lon * LONS, LONS), LONS)], zv, loc_sem.at[3]
    )
    g_copy.start()
    x_copy.start()
    w_copy.start()

    @pl.when(polar_dev)
    def _():
        z_copy.start()

    barrier = pltpu.get_barrier_semaphore()

    def greet(to_lat, to_lon):
        pl.semaphore_signal(barrier, inc=1, device_id={"lat": to_lat, "lon": to_lon}, device_id_type=MESH)

    outer = lat - 1 + 2 * core
    to_next = (core == 1) & (x_high == 1) & (z < N_Z - 1)
    to_last = (core == 0) & (x_high == 0) & (z > 0)
    crosses = to_next | to_last

    @pl.when(crosses)
    def _():
        for step in (0, 1, N_LON - 1):
            greet(outer, lon_at(step))

    def lat_at(step):
        return 4 * lax.rem(z + step, N_Z) + in_plane

    for step in range(1, N_Z):
        greet(lat_at(step), lon)
    for turn_lat in range(4):
        for step in range(N_LON):
            if turn_lat or step:
                greet(4 * z + lax.rem(in_plane + turn_lat, 4), lon_at(step))

    span = 2 * REACH + 1
    row_i = lax.broadcasted_iota(jnp.int32, (ROWS, span), 0)
    tap = lax.broadcasted_iota(jnp.int32, (ROWS, span), 1)
    offset_v = jnp.zeros((ROWS, span), jnp.int32)
    width_v = jnp.zeros((ROWS, span), jnp.int32)
    for i in range(ROWS):
        offset_v = jnp.where(row_i == i, offset_ref[i], offset_v)
        width_v = jnp.where(row_i == i, width_ref[i], width_v)
    keep = jnp.abs(tap - REACH) <= width_v
    choose = {m: jnp.where(keep & (offset_v == 2 - m), 1.0, 0.0) for m in (2, 3, 4)}
    lv[...] = jnp.zeros_like(lv)
    for k in range(K):
        values = [filt_ref[k, r].astype(F32) for r in range(3)]
        for n in range(CANDS):
            terms = [choose[n + r] * values[r] for r in range(3) if n + r in choose]
            lv[n, pl.ds((4 - n) * 16 + k, ROWS, stride=16), :] = functools.reduce(jnp.add, terms)
    tap = lax.broadcasted_iota(jnp.int32, (span, DEPTH), 0)
    lane = lax.broadcasted_iota(jnp.int32, (span, DEPTH), 1)
    placed = jnp.zeros((128, DEPTH), F32)
    for n in range(CANDS):
        where = jnp.where(lane + tap == WIN * n + 2 * REACH, 1.0, 0.0).astype(BF16)
        placed = placed + dot(lv[n].astype(BF16), where)
    vown[...] = placed.astype(BF16).reshape(8, 16, DEPTH)

    pl.semaphore_wait(barrier, 4 * N_LON + N_Z - 2 + 3 * crosses.astype(jnp.int32))

    up, down = lat - 1, lat + 1
    has_up, has_down = lat > 0, lat < N_LAT - 1
    rows_of = {-1: (0, 2, 6), 0: (0, ROWS, 2), 1: (2, 2, 0)}
    cols_of = {-1: (0, REACH, REACH + LONS), 0: (0, LONS, REACH), 1: (LONS - REACH, REACH, 0)}
    moves = [(1, 0), (-1, 0), (1, 1), (1, -1), (-1, 1), (-1, -1), (0, 1), (0, -1)]
    from_up = [index for index in range(8) if moves[index][0] == 1]
    from_down = [index for index in range(8) if moves[index][0] == -1]
    level = [index for index in range(8) if moves[index][0] == 0]

    def halo(index):
        dlat, dlon = moves[index]
        r0, rn, r_to = rows_of[dlat]
        c0, cn, c_to = cols_of[dlon]
        return remote(
            g_hbm.at[pl.ds(r0, rn), pl.ds(c0, cn)],
            gx.at[pl.ds(r_to, rn), pl.ds(c_to, cn)],
            halo_send.at[index], halo_recv.at[index],
            lat + dlat, lon_at(dlon % N_LON), "halo",
        )

    def v_halo(side):
        src = vown.at[pl.ds(6, 2)] if side == 0 else vown.at[pl.ds(0, 2)]
        return remote(src, vh.at[side], vsend.at[side], vrecv.at[side], down if side == 0 else up, lon, "halo")

    @pl.when(has_down)
    def _():
        v_halo(0).start()
        for index in from_up:
            halo(index).start()

    @pl.when(has_up)
    def _():
        v_halo(1).start()
        for index in from_down:
            halo(index).start()

    for index in level:
        halo(index).start()

    g_copy.wait()

    def gs_copy(dc, step):
        return remote(
            gs_own, gs_buf.at[lon], gs_send.at[dc, step], gs_sem, twin if dc else lat, lon_at(step), "halo"
        )

    def y_halo(first):
        return remote(yown.at[pl.ds(first, 2)], yh, ysend, yrecv, twin, lon, "halo")

    @pl.when(jnp.logical_not(polar_dev))
    def _():
        yown[...] = jnp.zeros_like(yown)

    @pl.when(polar_dev)
    def _():
        gs_own[...] = jnp.zeros_like(gs_own)
        for i in range(ROWS):
            gs_own[pl.ds(i, 1), :] = jnp.sum(
                gx[2 + i, pl.ds(REACH, LONS), :].astype(F32), axis=0, keepdims=True
            )
        for dc in range(2):
            for step in range(N_LON):
                if dc or step:
                    gs_copy(dc, step).start()
        pltpu.make_async_copy(gs_own, gs_buf.at[lon], gs_sem).start()
        pole = lax.div(lat, N_LAT // 2)
        entry = lax.broadcasted_iota(jnp.int32, (16, 16), 0)
        source = lax.broadcasted_iota(jnp.int32, (16, 16), 1)
        row = source & 3
        first_q = polar_ref[2 * pole] - lat * ROWS
        second_q = polar_ref[2 * pole + 1] - lat * ROWS
        polar_row = jnp.where((entry & 1) == 0, first_q, second_q)
        moved = row + (source >> 2)
        for i in range(ROWS):
            moved = moved + jnp.where(row == i, offset_ref[i], 0)
        hit = (row == polar_row) & (moved == (entry >> 1) - 2) & (source < 12)
        z_copy.wait()
        zs[pl.ds(8, 8), :] = jnp.zeros((8, K * LONS), F32)
        for k in range(K):
            for r in range(3):
                zs[pl.ds(4 * r, 4), pl.ds(k * LONS, LONS)] = zv[k, r].astype(F32)
        picked = dot(jnp.where(hit, 1.0, 0.0).astype(BF16), zs[...].astype(BF16))
        yf[...] = jnp.zeros_like(yf)
        for k in range(K):
            for half in range(2):
                yf[half, pl.ds(k, 16, stride=16), :] = picked[:, k * LONS + 128 * half:k * LONS + 128 * half + 128]
        for half in range(2):
            yown[:, :, pl.ds(128 * half, 128)] = yf[half].astype(BF16).reshape(8, 32, 128)

    @pl.when(north)
    def _():
        y_halo(6).start()

    @pl.when(south)
    def _():
        y_halo(0).start()

    @pl.when(north)
    def _():
        gx[pl.ds(0, 2)] = jnp.zeros((2,) + gx.shape[1:], BF16)
        vh[0] = jnp.zeros(vh.shape[1:], BF16)

    @pl.when(south)
    def _():
        gx[pl.ds(6, 2)] = jnp.zeros((2,) + gx.shape[1:], BF16)
        vh[1] = jnp.zeros(vh.shape[1:], BF16)

    x_copy.wait()
    for i in range(ROWS):
        xt[:, pl.ds(i * LONS, LONS)] = xv[i].T
    w_copy.wait()

    def turn(k, carry):
        at = pl.ds(pl.multiple_of(k * C, C), C)
        wt[at, :] = wv[at, :].T
        return carry

    lax.fori_loop(0, K, turn, 0)

    def band_rows(base, side):
        for a in range(2):
            vf[pl.ds(16 * a, 16), :] = vown[2 + base + a].astype(F32) + vh[side, a].astype(F32)

        def band(k, carry):
            for a in range(2):
                row = jnp.broadcast_to(vf[pl.ds(16 * a + k, 1), :], (JB, DEPTH))
                rolled = pltpu.roll(row, 0, 1, stride=1, stride_axis=0)
                tt[base + a, pl.ds(pl.multiple_of(k * JB, JB), JB), :] = rolled.astype(BF16)
            return carry

        lax.fori_loop(0, K, band, 0)

    def spread_rows(base, k0, k1):
        def spread(step, carry):
            for half in range(2):
                index = 2 * step + half
                i2, jb = base + lax.div(index, LONS // JB), lax.rem(index, LONS // JB)
                at = pl.ds(pl.multiple_of(jb * JB, JB), WIN)
                windows = [gx[i2 + n, at, :] for n in range(CANDS)]
                windows.append(jnp.zeros((DEPTH - CANDS * WIN, C), BF16))
                moved = dot(tt[i2, pl.ds(k0 * JB, (k1 - k0) * JB)], jnp.concatenate(windows, axis=0)).astype(BF16)
                rows = pl.ds(pl.multiple_of(i2 * LONS + jb * JB, JB), JB)
                for k in range(k0, k1):
                    hh[rows, pl.ds(k * C, C)] = moved[(k - k0) * JB:(k - k0 + 1) * JB]
            return carry

        lax.fori_loop(0, LONS // JB, spread, 0)

    near, far = 2 - 2 * core, 2 * core

    def arrive(index_list):
        for index in index_list:
            halo(index).wait_recv()

    arrive(level)

    @pl.when(core == 0)
    def _():
        v_halo(1).wait_recv()
        arrive(from_down)

    @pl.when(core == 1)
    def _():
        v_halo(0).wait_recv()
        arrive(from_up)

    band_rows(near, 1 - core)
    spread_rows(near, 0, K)

    @pl.when((core == 0) & has_up)
    def _():
        v_halo(0).wait_recv()

    @pl.when((core == 1) & has_down)
    def _():
        v_halo(1).wait_recv()

    band_rows(far, core)

    for i2 in range(ROWS):
        yy[i2] = yown[2 + i2]

    @pl.when(lat == 1)
    def _():
        y_halo(6).wait_recv()
        yy[pl.ds(0, 2)] = yh[...]

    @pl.when(lat == N_LAT - 2)
    def _():
        y_halo(0).wait_recv()
        yy[pl.ds(2, 2)] = yh[...]

    circle = jnp.zeros((C, 32), F32)
    for i2 in range(ROWS):
        circle = circle + dot(xt[:, pl.ds(i2 * LONS, LONS)], yy[i2], 1, 1)
    zst[...] = circle * FACTOR

    @pl.when(jnp.logical_not(affected))
    def _():
        gsel[...] = jnp.zeros_like(gsel)

    @pl.when(affected)
    def _():
        pltpu.make_async_copy(gs_buf, gs_buf, gs_sem).wait()
        total = gs_buf[0]
        for step in range(1, N_LON):
            total = total + gs_buf[step]
        pole = lax.div(lat, N_LAT // 2)
        gsel[...] = jnp.zeros_like(gsel)
        for q in range(2):
            mine = polar_ref[2 * pole + q] - pole * (N_LAT - 1) * ROWS
            picked = jnp.zeros((1, C), F32)
            for i in range(ROWS):
                picked = picked + total[i:i + 1] * (mine == i).astype(F32)
            gsel[pl.ds(q, 1), :] = picked

    circle_sum = gsel[...]
    high = circle_sum.astype(BF16)
    low = (circle_sum - high.astype(F32)).astype(BF16)
    parts = jnp.concatenate([high.astype(F32), low.astype(F32)], axis=0).astype(BF16)
    ztf[...] = jnp.zeros_like(ztf)
    for k in range(K):
        mixed = dot(parts, wt[pl.ds(k * C, C), :])
        mixed = mixed[:8] + mixed[8:]
        for q in range(2):
            ztf[pl.ds(16 * q + k, 1), :] = mixed[q:q + 1]

    @pl.when((core == 0) & has_up)
    def _():
        arrive(from_up)

    @pl.when((core == 1) & has_down)
    def _():
        arrive(from_down)

    def twin_copy(group):
        k0, k1 = GROUPS[group]
        at = pl.ds(k0, k1 - k0)
        return remote(wsnd.at[at], cx.at[at], cs_send.at[group], cs_recv.at[group], twin, lon)

    def mix(group):
        for k in range(*GROUPS[group]):
            share = dot(xt[...], hh[:, pl.ds(k * C, C)]) * FACTOR
            for q in range(2):
                share = share + zst[:, 16 * q + k:16 * q + k + 1] * gsel[q:q + 1, :]
            first, second = share[:, :128], share[:, 128:]
            wown[k] = jnp.where(core == 0, first, second)
            wsnd[k] = jnp.where(core == 0, second, first).astype(BF16)
        twin_copy(group).start()

    def along(axis, step):
        to = lax.rem(place[axis] + step, 4)
        if axis == "y":
            return to, lat, lon + to - y
        return to, lat + 2 * (lax.div(to, 2) - x_high), lon + 4 * (lax.rem(to, 2) - x_low)

    def first_piece(run, to):
        k0, k1, axis = RUNS[run]
        at = pl.ds(k0, k1 - k0)
        return s1.at[at, to] if axis == "y" else s1.at[at, :, to]

    def first_copy(run, step):
        k0, k1, axis = RUNS[run]
        to, to_lat, to_lon = along(axis, step)
        dst = r1.at[place[axis], pl.ds(k0, k1 - k0)]
        return remote(first_piece(run, to), dst, send1.at[run, step], recv1.at[run], to_lat, to_lon, "r2")

    def second_copy(run, step):
        k0, k1, axis = RUNS[run]
        axis = "x" if axis == "y" else "y"
        to, to_lat, to_lon = along(axis, step)
        at = pl.ds(k0, k1 - k0)
        return remote(
            s2.at[at, to], r2.at[place[axis], at], send2.at[run, step], recv2.at[run], to_lat, to_lon, "r2"
        )

    def first(group):
        twin_copy(group).wait_recv()
        for k in range(*GROUPS[group]):
            s1[k] = (wown[k] + cx[k].astype(F32)).astype(BF16).reshape(4, 4, 16, 128)
        for run in GROUP_RUNS[group]:
            for step in range(1, 4):
                first_copy(run, step).start()

    def arrived(buffer, semaphore):
        pltpu.make_async_copy(buffer, buffer, semaphore).wait()

    def second(run):
        k0, k1, axis = RUNS[run]
        arrived(r1.at[pl.ds(0, 3), pl.ds(k0, k1 - k0)], recv1.at[run])
        for k in range(k0, k1):
            total = (s1[k, place[axis]] if axis == "y" else s1[k, :, place[axis]]).astype(F32)
            for step in range(1, 4):
                total = total + r1[lax.rem(place[axis] + step, 4), k].astype(F32)
            s2[k] = total.astype(BF16)
        for step in range(1, 4):
            second_copy(run, step).start()

    part = 4 * y + place["x"]

    def granule(k):
        q = 16 * k + part
        to_z = lax.div(q, 18)
        b = lax.div(q - 18 * to_z, 16)
        copy = remote(
            s3.at[k], r3.at[b, z], send3.at[k], recv3.at[b], 4 * to_z + in_plane, lon, "r3"
        )
        return to_z, b, copy

    def third(run):
        k0, k1, axis = RUNS[run]
        axis = "x" if axis == "y" else "y"
        arrived(r2.at[pl.ds(0, 3), pl.ds(k0, k1 - k0)], recv2.at[run])
        for k in range(k0, k1):
            total = s2[k, place[axis]].astype(F32)
            for step in range(1, 4):
                total = total + r2[lax.rem(place[axis] + step, 4), k].astype(F32)
            s3[k] = total.astype(BF16)
        for k in range(k0, k1):
            to_z, b, copy = granule(k)

            @pl.when(to_z != z)
            def _():
                copy.start()

            @pl.when(to_z == z)
            def _():
                pltpu.make_async_copy(s3.at[k], r3.at[b, z], recv3.at[b]).start()

    def owned(b):
        q = 16 * lax.div(18 * z - part + 15, 16) + part + 16 * b
        owner = lax.div(q, 9)
        return q <= 18 * z + 17, owner - 2 * z, q - 9 * owner

    def final_copy(b, to_high, e, dc, step):
        at = pl.ds(pl.multiple_of(16 * e, 16), 16)
        to_lat = 4 * z + 2 * to_high + (1 - core if dc else core)
        return remote(s4.at[b], fin.at[core, at], fs_send.at[b, dc, step], fs_recv, to_lat, lon_at(step), "r4")

    def needed(e, to_core):
        return ((to_core == 0) & (e <= 4)) | ((to_core == 1) & (e >= 4))

    def spread_out():
        for b in range(2):
            valid, to_high, e = owned(b)

            @pl.when(valid)
            def _():
                arrived(r3.at[b], recv3.at[b])
                total = r3[b, 0].astype(F32)
                for step in range(1, N_Z):
                    total = total + r3[b, step].astype(F32)
                s4[b] = total

            for dc in range(2):
                @pl.when(valid & needed(e, 1 - core if dc else core))
                def _():
                    for step in range(N_LON):
                        if dc or step:
                            final_copy(b, to_high, e, dc, step).start()
                        else:
                            @pl.when(to_high == x_high)
                            def _():
                                at = pl.ds(pl.multiple_of(16 * e, 16), 16)
                                pltpu.make_async_copy(s4.at[b], fin.at[core, at], fs_recv).start()

                            @pl.when(to_high != x_high)
                            def _():
                                final_copy(b, to_high, e, 0, 0).start()

    circle_total = ztf[...]
    z_high = circle_total.astype(BF16)
    z_low = (circle_total - z_high.astype(F32)).astype(BF16)
    z_parts = jnp.concatenate([z_high, z_low], axis=0)

    def pull(half):
        grad = dot(hh[pl.ds(half * 2 * LONS, 2 * LONS), :], wt[...])
        for a in range(2):
            i2 = 2 * half + a
            twice = jnp.concatenate([yy[i2], yy[i2]], axis=0)
            ig_ref[i2] = (grad[a * LONS:(a + 1) * LONS] + dot(twice, z_parts, 0, 0)).astype(BF16)

    spread_rows(far, *GROUPS[0])
    mix(0)
    spread_rows(far, *GROUPS[1])
    mix(1)
    first(0)
    spread_rows(far, *GROUPS[2])
    mix(2)
    first(1)
    second(0)
    first(2)
    second(1)
    third(0)
    pull(0)
    second(2)
    second(3)
    third(1)
    pull(1)
    third(2)
    third(3)
    spread_out()
    for index in level:
        halo(index).wait_send()

    @pl.when(has_down)
    def _():
        v_halo(0).wait_send()
        for index in from_up:
            halo(index).wait_send()

    @pl.when(has_up)
    def _():
        v_halo(1).wait_send()
        for index in from_down:
            halo(index).wait_send()

    @pl.when(north)
    def _():
        y_halo(6).wait_send()

    @pl.when(south)
    def _():
        y_halo(0).wait_send()

    @pl.when(polar_dev)
    def _():
        for dc in range(2):
            for step in range(N_LON):
                if dc or step:
                    gs_copy(dc, step).wait_send()

    for group in range(len(GROUPS)):
        twin_copy(group).wait_send()
    for run in range(len(RUNS)):
        for step in range(1, 4):
            first_copy(run, step).wait_send()
            second_copy(run, step).wait_send()
    for k in range(K):
        to_z, b, copy = granule(k)

        @pl.when(to_z != z)
        def _():
            copy.wait_send()

    some = fin.at[:, pl.ds(0, 80)]
    pltpu.make_async_copy(some, some, fs_recv).wait()
    rows = pl.ds(pl.multiple_of(72 * core, 8), 72)
    for half in range(2):
        wg_ref[:, pl.ds(128 * half, 128)] = fin[half, rows, :]

    for b in range(2):
        valid, to_high, e = owned(b)
        for dc in range(2):
            @pl.when(valid & needed(e, 1 - core if dc else core))
            def _():
                for step in range(N_LON):
                    if dc or step:
                        final_copy(b, to_high, e, dc, step).wait_send()
                    else:
                        @pl.when(to_high != x_high)
                        def _():
                            final_copy(b, to_high, e, 0, 0).wait_send()


def body(input_field, grad_out, weight, filt, zonal_weight, widths, offsets, polar_rows):
    dma = pltpu.SemaphoreType.DMA
    hbm = pl.BlockSpec(memory_space=pltpu.HBM)
    vmem = pl.BlockSpec(memory_space=pltpu.VMEM)
    smem = pl.BlockSpec(memory_space=pltpu.SMEM)
    groups, runs = len(GROUPS), len(RUNS)
    return pl.pallas_call(
        kernel,
        out_shape=(pltpu.VMEM((ROWS, LONS, C), BF16), pltpu.VMEM((72, C), F32)),
        in_specs=[hbm, hbm, hbm, vmem, hbm, smem, smem, smem],
        out_specs=(vmem, vmem),
        scratch_shapes=[
            pltpu.VMEM((8, LONS + 2 * REACH, C), BF16),
            pltpu.VMEM((ROWS, LONS, C), BF16),
            pltpu.VMEM((C, ROWS * LONS), BF16),
            pltpu.VMEM((K * C, C), BF16),
            pltpu.VMEM((K * C, C), BF16),
            pltpu.VMEM((CANDS, 128, 2 * REACH + 1), F32),
            pltpu.VMEM((8, 16, DEPTH), BF16),
            pltpu.VMEM((2, 2, 16, DEPTH), BF16),
            pltpu.VMEM((32, DEPTH), F32),
            pltpu.VMEM((ROWS, K * JB, DEPTH), BF16),
            pltpu.VMEM((ROWS * LONS, K * C), BF16),
            pltpu.VMEM((K, 3, ROWS, LONS), BF16),
            pltpu.VMEM((16, K * LONS), F32),
            pltpu.VMEM((2, 256, 128), F32),
            pltpu.VMEM((8, 32, LONS), BF16),
            pltpu.VMEM((2, 32, LONS), BF16),
            pltpu.VMEM((ROWS, 32, LONS), BF16),
            pltpu.VMEM((32, C), F32),
            pltpu.VMEM((C, 32), F32),
            pltpu.VMEM((8, C), F32),
            pltpu.VMEM((N_LON, 8, C), F32),
            pltpu.VMEM((8, C), F32),
            pltpu.VMEM((K, C, 128), F32),
            pltpu.VMEM((K, C, 128), BF16),
            pltpu.VMEM((K, C, 128), BF16),
            pltpu.VMEM((K, 4, 4, 16, 128), BF16),
            pltpu.VMEM((4, K, 4, 16, 128), BF16),
            pltpu.VMEM((K, 4, 16, 128), BF16),
            pltpu.VMEM((4, K, 16, 128), BF16),
            pltpu.VMEM((K, 16, 128), BF16),
            pltpu.VMEM((2, N_Z, 16, 128), BF16),
            pltpu.VMEM((2, 16, 128), F32),
            pltpu.VMEM((2, 144, 128), F32),
            dma((4,)), dma((8,)), dma((8,)), dma((2,)), dma((2,)), dma, dma, dma((2, N_LON)), dma,
            dma((groups,)), dma((groups,)), dma((runs, 4)), dma((runs,)), dma((runs, 4)), dma((runs,)),
            dma((K,)), dma((2,)), dma((2, 2, N_LON)), dma,
        ],
        compiler_params=pltpu.CompilerParams(
            collective_id=0, has_side_effects=True, vmem_limit_bytes=48 * 1024 * 1024
        ),
        name="sphere_backward",
    )(*[
        pltpu.with_memory_space_constraint(array, pltpu.HBM)
        for array in (
            grad_out, input_field, weight, jnp.transpose(filt, (0, 2, 1, 3)),
            jnp.transpose(zonal_weight, (0, 2, 1, 3)), widths, offsets, polar_rows,
        )
    ])


def solution(mesh):
    in_specs = (
        P("lat", "lon", None),
        P("lat", "lon", None),
        P(),
        P(None, "lat", None, None),
        P(None, "lat", None, None),
        P("lat"),
        P("lat"),
        P(),
    )
    out_specs = (P("lat", "lon", None), P("lat", None))
    return jax.shard_map(body, mesh=mesh, in_specs=in_specs, out_specs=out_specs, check_vma=False)
```

```python
import functools
import math

import jax
import jax.numpy as jnp
from jax import lax
from jax.experimental import pallas as pl
from jax.experimental.pallas import tpu as pltpu
from jax.sharding import PartitionSpec as P

MESH = pl.DeviceIdType.MESH
F32 = jnp.float32
BF16 = jnp.bfloat16
ROWS = 4
LONS = 256
C = 256
K = 9
REACH = 16
JB = 64
WIN = JB + 2 * REACH
CANDS = 5
DEPTH = 512
N_LAT = 32
N_LON = 8
N_Z = 8
GROUPS = ((0, 3), (3, 6), (6, 9))
RUNS = ((0, 3, "y"), (3, 6, "x"), (6, 8, "y"), (8, 9, "x"))
GROUP_RUNS = ((0,), (1,), (2, 3))
FACTOR = 1.0 / math.sqrt(128 * 2048)


def dot(a, b, ca=1, cb=0):
    return lax.dot_general(a, b, (((ca,), (cb,)), ((), ())), preferred_element_type=F32)


def kernel(
    g_hbm, x_hbm, w_hbm, filt_ref, z_hbm, width_ref, offset_ref, polar_ref,
    ig_ref, wg_ref,
    gx, xv, xt, wv, wt, lv, vown, vh, vf, tt, hh, zv, zs, yf, yown, yh, yy, ztf, zst, gs_own, gs_buf, gsel,
    wown, wsnd, cx, s1, r1, s2, r2, s3, r3, s4, fin,
    loc_sem, halo_send, halo_recv, vsend, vrecv, ysend, yrecv, gs_send, gs_sem,
    cs_send, cs_recv, send1, recv1, send2, recv2, send3, recv3, fs_send, fs_recv,
):
    lat = lax.axis_index("lat")
    lon = lax.axis_index("lon")
    core = lax.rem(lat, 2)
    twin = lat + 1 - 2 * core
    z, in_plane = lax.div(lat, 4), lax.rem(lat, 4)
    x_high, x_low, y = lax.div(in_plane, 2), lax.div(lon, 4), lax.rem(lon, 4)
    place = {"x": 2 * x_high + x_low, "y": y}

    def lon_at(step):
        return lax.rem(lon + step, N_LON)

    def remote(src, dst, send, recv, to_lat, to_lon, tag="rs"):
        return pltpu.make_async_remote_copy(
            src_ref=src, dst_ref=dst, send_sem=send, recv_sem=recv,
            device_id={"lat": to_lat, "lon": to_lon}, device_id_type=MESH,
        )

    north, south = lat == 0, lat == N_LAT - 1
    polar_dev = north | south
    affected = polar_dev | (lat == 1) | (lat == N_LAT - 2)

    g_copy = pltpu.make_async_copy(g_hbm, gx.at[pl.ds(2, ROWS), pl.ds(REACH, LONS)], loc_sem.at[0])
    x_copy = pltpu.make_async_copy(x_hbm, xv, loc_sem.at[1])
    w_copy = pltpu.make_async_copy(w_hbm, wv, loc_sem.at[2])
    z_copy = pltpu.make_async_copy(
        z_hbm.at[:, :, :, pl.ds(pl.multiple_of(lon * LONS, LONS), LONS)], zv, loc_sem.at[3]
    )
    g_copy.start()
    x_copy.start()
    w_copy.start()

    @pl.when(polar_dev)
    def _():
        z_copy.start()

    barrier = pltpu.get_barrier_semaphore()

    def greet(to_lat, to_lon):
        pl.semaphore_signal(barrier, inc=1, device_id={"lat": to_lat, "lon": to_lon}, device_id_type=MESH)

    outer = lat - 1 + 2 * core
    to_next = (core == 1) & (x_high == 1) & (z < N_Z - 1)
    to_last = (core == 0) & (x_high == 0) & (z > 0)
    crosses = to_next | to_last

    @pl.when(crosses)
    def _():
        for step in (0, 1, N_LON - 1):
            greet(outer, lon_at(step))

    def lat_at(step):
        return 4 * lax.rem(z + step, N_Z) + in_plane

    for step in range(1, N_Z):
        greet(lat_at(step), lon)
    for turn_lat in range(4):
        for step in range(N_LON):
            if turn_lat or step:
                greet(4 * z + lax.rem(in_plane + turn_lat, 4), lon_at(step))

    span = 2 * REACH + 1
    row_i = lax.broadcasted_iota(jnp.int32, (ROWS, span), 0)
    tap = lax.broadcasted_iota(jnp.int32, (ROWS, span), 1)
    offset_v = jnp.zeros((ROWS, span), jnp.int32)
    width_v = jnp.zeros((ROWS, span), jnp.int32)
    for i in range(ROWS):
        offset_v = jnp.where(row_i == i, offset_ref[i], offset_v)
        width_v = jnp.where(row_i == i, width_ref[i], width_v)
    keep = jnp.abs(tap - REACH) <= width_v
    choose = {m: jnp.where(keep & (offset_v == 2 - m), 1.0, 0.0) for m in (2, 3, 4)}
    lv[...] = jnp.zeros_like(lv)
    for k in range(K):
        values = [filt_ref[k, r].astype(F32) for r in range(3)]
        for n in range(CANDS):
            terms = [choose[n + r] * values[r] for r in range(3) if n + r in choose]
            lv[n, pl.ds((4 - n) * 16 + k, ROWS, stride=16), :] = functools.reduce(jnp.add, terms)
    tap = lax.broadcasted_iota(jnp.int32, (span, DEPTH), 0)
    lane = lax.broadcasted_iota(jnp.int32, (span, DEPTH), 1)
    placed = jnp.zeros((128, DEPTH), F32)
    for n in range(CANDS):
        where = jnp.where(lane + tap == WIN * n + 2 * REACH, 1.0, 0.0).astype(BF16)
        placed = placed + dot(lv[n].astype(BF16), where)
    vown[...] = placed.astype(BF16).reshape(8, 16, DEPTH)

    pl.semaphore_wait(barrier, 4 * N_LON + N_Z - 2 + 3 * crosses.astype(jnp.int32))

    up, down = lat - 1, lat + 1
    has_up, has_down = lat > 0, lat < N_LAT - 1
    rows_of = {-1: (0, 2, 6), 0: (0, ROWS, 2), 1: (2, 2, 0)}
    cols_of = {-1: (0, REACH, REACH + LONS), 0: (0, LONS, REACH), 1: (LONS - REACH, REACH, 0)}
    moves = [(1, 0), (-1, 0), (1, 1), (1, -1), (-1, 1), (-1, -1), (0, 1), (0, -1)]
    from_up = [index for index in range(8) if moves[index][0] == 1]
    from_down = [index for index in range(8) if moves[index][0] == -1]
    level = [index for index in range(8) if moves[index][0] == 0]

    def halo(index):
        dlat, dlon = moves[index]
        r0, rn, r_to = rows_of[dlat]
        c0, cn, c_to = cols_of[dlon]
        return remote(
            g_hbm.at[pl.ds(r0, rn), pl.ds(c0, cn)],
            gx.at[pl.ds(r_to, rn), pl.ds(c_to, cn)],
            halo_send.at[index], halo_recv.at[index],
            lat + dlat, lon_at(dlon % N_LON), "halo",
        )

    def v_halo(side):
        src = vown.at[pl.ds(6, 2)] if side == 0 else vown.at[pl.ds(0, 2)]
        return remote(src, vh.at[side], vsend.at[side], vrecv.at[side], down if side == 0 else up, lon, "halo")

    for index in level:
        halo(index).start()

    @pl.when(has_down)
    def _():
        v_halo(0).start()
        for index in from_up[1:]:
            halo(index).start()

    @pl.when(has_up)
    def _():
        v_halo(1).start()
        for index in from_down[1:]:
            halo(index).start()

    @pl.when(has_down)
    def _():
        halo(from_up[0]).start()

    @pl.when(has_up)
    def _():
        halo(from_down[0]).start()

    g_copy.wait()

    def gs_copy(dc, step):
        return remote(
            gs_own, gs_buf.at[lon], gs_send.at[dc, step], gs_sem, twin if dc else lat, lon_at(step), "halo"
        )

    def y_halo(first):
        return remote(yown.at[pl.ds(first, 2)], yh, ysend, yrecv, twin, lon, "halo")

    @pl.when(jnp.logical_not(polar_dev))
    def _():
        yown[...] = jnp.zeros_like(yown)

    @pl.when(polar_dev)
    def _():
        gs_own[...] = jnp.zeros_like(gs_own)
        for i in range(ROWS):
            gs_own[pl.ds(i, 1), :] = jnp.sum(
                gx[2 + i, pl.ds(REACH, LONS), :].astype(F32), axis=0, keepdims=True
            )
        for dc in range(2):
            for step in range(N_LON):
                if dc or step:
                    gs_copy(dc, step).start()
        pltpu.make_async_copy(gs_own, gs_buf.at[lon], gs_sem).start()
        pole = lax.div(lat, N_LAT // 2)
        entry = lax.broadcasted_iota(jnp.int32, (16, 16), 0)
        source = lax.broadcasted_iota(jnp.int32, (16, 16), 1)
        row = source & 3
        first_q = polar_ref[2 * pole] - lat * ROWS
        second_q = polar_ref[2 * pole + 1] - lat * ROWS
        polar_row = jnp.where((entry & 1) == 0, first_q, second_q)
        moved = row + (source >> 2)
        for i in range(ROWS):
            moved = moved + jnp.where(row == i, offset_ref[i], 0)
        hit = (row == polar_row) & (moved == (entry >> 1) - 2) & (source < 12)
        z_copy.wait()
        zs[pl.ds(8, 8), :] = jnp.zeros((8, K * LONS), F32)
        for k in range(K):
            for r in range(3):
                zs[pl.ds(4 * r, 4), pl.ds(k * LONS, LONS)] = zv[k, r].astype(F32)
        picked = dot(jnp.where(hit, 1.0, 0.0).astype(BF16), zs[...].astype(BF16))
        yf[...] = jnp.zeros_like(yf)
        for k in range(K):
            for half in range(2):
                yf[half, pl.ds(k, 16, stride=16), :] = picked[:, k * LONS + 128 * half:k * LONS + 128 * half + 128]
        for half in range(2):
            yown[:, :, pl.ds(128 * half, 128)] = yf[half].astype(BF16).reshape(8, 32, 128)

    @pl.when(north)
    def _():
        y_halo(6).start()

    @pl.when(south)
    def _():
        y_halo(0).start()

    @pl.when(north)
    def _():
        gx[pl.ds(0, 2)] = jnp.zeros((2,) + gx.shape[1:], BF16)
        vh[0] = jnp.zeros(vh.shape[1:], BF16)

    @pl.when(south)
    def _():
        gx[pl.ds(6, 2)] = jnp.zeros((2,) + gx.shape[1:], BF16)
        vh[1] = jnp.zeros(vh.shape[1:], BF16)

    x_copy.wait()
    for i in range(ROWS):
        xt[:, pl.ds(i * LONS, LONS)] = xv[i].T
    w_copy.wait()

    def turn(k, carry):
        at = pl.ds(pl.multiple_of(k * C, C), C)
        wt[at, :] = wv[at, :].T
        return carry

    lax.fori_loop(0, K, turn, 0)

    def band_rows(base, side):
        for a in range(2):
            vf[pl.ds(16 * a, 16), :] = vown[2 + base + a].astype(F32) + vh[side, a].astype(F32)

        def band(k, carry):
            for a in range(2):
                row = jnp.broadcast_to(vf[pl.ds(16 * a + k, 1), :], (JB, DEPTH))
                rolled = pltpu.roll(row, 0, 1, stride=1, stride_axis=0)
                tt[base + a, pl.ds(pl.multiple_of(k * JB, JB), JB), :] = rolled.astype(BF16)
            return carry

        lax.fori_loop(0, K, band, 0)

    def spread_rows(base, k0, k1, blocks):
        def spread(step, carry):
            for jb in blocks:
                i2 = base + step
                at = pl.ds(jb * JB, WIN)
                windows = [gx[i2 + n, at, :] for n in range(CANDS)]
                windows.append(jnp.zeros((DEPTH - CANDS * WIN, C), BF16))
                moved = dot(tt[i2, pl.ds(k0 * JB, (k1 - k0) * JB)], jnp.concatenate(windows, axis=0)).astype(BF16)
                rows = pl.ds(pl.multiple_of(i2 * LONS + jb * JB, JB), JB)
                for k in range(k0, k1):
                    hh[rows, pl.ds(k * C, C)] = moved[(k - k0) * JB:(k - k0 + 1) * JB]
            return carry

        lax.fori_loop(0, 2, spread, 0)

    near, far = 2 - 2 * core, 2 * core

    def arrive(index_list):
        for index in index_list:
            halo(index).wait_recv()

    @pl.when(core == 0)
    def _():
        v_halo(1).wait_recv()
        arrive(from_down[:1])

    @pl.when(core == 1)
    def _():
        v_halo(0).wait_recv()
        arrive(from_up[:1])

    band_rows(near, 1 - core)
    spread_rows(near, 0, K, (1, 2))

    @pl.when((core == 0) & has_up)
    def _():
        v_halo(0).wait_recv()

    @pl.when((core == 1) & has_down)
    def _():
        v_halo(1).wait_recv()

    band_rows(far, core)

    for i2 in range(ROWS):
        yy[i2] = yown[2 + i2]

    @pl.when(lat == 1)
    def _():
        y_halo(6).wait_recv()
        yy[pl.ds(0, 2)] = yh[...]

    @pl.when(lat == N_LAT - 2)
    def _():
        y_halo(0).wait_recv()
        yy[pl.ds(2, 2)] = yh[...]

    circle = jnp.zeros((C, 32), F32)
    for i2 in range(ROWS):
        circle = circle + dot(xt[:, pl.ds(i2 * LONS, LONS)], yy[i2], 1, 1)
    zst[...] = circle * FACTOR

    @pl.when(jnp.logical_not(affected))
    def _():
        gsel[...] = jnp.zeros_like(gsel)

    @pl.when(affected)
    def _():
        pltpu.make_async_copy(gs_buf, gs_buf, gs_sem).wait()
        total = gs_buf[0]
        for step in range(1, N_LON):
            total = total + gs_buf[step]
        pole = lax.div(lat, N_LAT // 2)
        gsel[...] = jnp.zeros_like(gsel)
        for q in range(2):
            mine = polar_ref[2 * pole + q] - pole * (N_LAT - 1) * ROWS
            picked = jnp.zeros((1, C), F32)
            for i in range(ROWS):
                picked = picked + total[i:i + 1] * (mine == i).astype(F32)
            gsel[pl.ds(q, 1), :] = picked

    circle_sum = gsel[...]
    high = circle_sum.astype(BF16)
    low = (circle_sum - high.astype(F32)).astype(BF16)
    parts = jnp.concatenate([high.astype(F32), low.astype(F32)], axis=0).astype(BF16)
    ztf[...] = jnp.zeros_like(ztf)
    for k in range(K):
        mixed = dot(parts, wt[pl.ds(k * C, C), :])
        mixed = mixed[:8] + mixed[8:]
        for q in range(2):
            ztf[pl.ds(16 * q + k, 1), :] = mixed[q:q + 1]

    arrive(level)

    @pl.when(core == 0)
    def _():
        arrive(from_down[1:])

    @pl.when(core == 1)
    def _():
        arrive(from_up[1:])

    spread_rows(near, 0, K, (0, 3))

    @pl.when((core == 0) & has_up)
    def _():
        arrive(from_up)

    @pl.when((core == 1) & has_down)
    def _():
        arrive(from_down)

    def twin_copy(group):
        k0, k1 = GROUPS[group]
        at = pl.ds(k0, k1 - k0)
        return remote(wsnd.at[at], cx.at[at], cs_send.at[group], cs_recv.at[group], twin, lon)

    def mix(group):
        for k in range(*GROUPS[group]):
            share = dot(xt[...], hh[:, pl.ds(k * C, C)]) * FACTOR
            for q in range(2):
                share = share + zst[:, 16 * q + k:16 * q + k + 1] * gsel[q:q + 1, :]
            first, second = share[:, :128], share[:, 128:]
            wown[k] = jnp.where(core == 0, first, second)
            wsnd[k] = jnp.where(core == 0, second, first).astype(BF16)
        twin_copy(group).start()

    def along(axis, step):
        to = lax.rem(place[axis] + step, 4)
        if axis == "y":
            return to, lat, lon + to - y
        return to, lat + 2 * (lax.div(to, 2) - x_high), lon + 4 * (lax.rem(to, 2) - x_low)

    def first_piece(run, to):
        k0, k1, axis = RUNS[run]
        at = pl.ds(k0, k1 - k0)
        return s1.at[at, to] if axis == "y" else s1.at[at, :, to]

    def first_copy(run, step):
        k0, k1, axis = RUNS[run]
        to, to_lat, to_lon = along(axis, step)
        dst = r1.at[place[axis], pl.ds(k0, k1 - k0)]
        return remote(first_piece(run, to), dst, send1.at[run, step], recv1.at[run], to_lat, to_lon, "r2")

    def second_copy(run, step):
        k0, k1, axis = RUNS[run]
        axis = "x" if axis == "y" else "y"
        to, to_lat, to_lon = along(axis, step)
        at = pl.ds(k0, k1 - k0)
        return remote(
            s2.at[at, to], r2.at[place[axis], at], send2.at[run, step], recv2.at[run], to_lat, to_lon, "r2"
        )

    def first(group):
        twin_copy(group).wait_recv()
        for k in range(*GROUPS[group]):
            s1[k] = (wown[k] + cx[k].astype(F32)).astype(BF16).reshape(4, 4, 16, 128)
        for run in GROUP_RUNS[group]:
            for step in range(1, 4):
                first_copy(run, step).start()

    def arrived(buffer, semaphore):
        pltpu.make_async_copy(buffer, buffer, semaphore).wait()

    def second(run):
        k0, k1, axis = RUNS[run]
        arrived(r1.at[pl.ds(0, 3), pl.ds(k0, k1 - k0)], recv1.at[run])
        for k in range(k0, k1):
            total = (s1[k, place[axis]] if axis == "y" else s1[k, :, place[axis]]).astype(F32)
            for step in range(1, 4):
                total = total + r1[lax.rem(place[axis] + step, 4), k].astype(F32)
            s2[k] = total.astype(BF16)
        for step in range(1, 4):
            second_copy(run, step).start()

    part = 4 * y + place["x"]

    def granule(k):
        q = 16 * k + part
        to_z = lax.div(q, 18)
        b = lax.div(q - 18 * to_z, 16)
        copy = remote(
            s3.at[k], r3.at[b, z], send3.at[k], recv3.at[b], 4 * to_z + in_plane, lon, "r3"
        )
        return to_z, b, copy

    def third(run):
        k0, k1, axis = RUNS[run]
        axis = "x" if axis == "y" else "y"
        arrived(r2.at[pl.ds(0, 3), pl.ds(k0, k1 - k0)], recv2.at[run])
        for k in range(k0, k1):
            total = s2[k, place[axis]].astype(F32)
            for step in range(1, 4):
                total = total + r2[lax.rem(place[axis] + step, 4), k].astype(F32)
            s3[k] = total.astype(BF16)
        for k in range(k0, k1):
            to_z, b, copy = granule(k)

            @pl.when(to_z != z)
            def _():
                copy.start()

            @pl.when(to_z == z)
            def _():
                pltpu.make_async_copy(s3.at[k], r3.at[b, z], recv3.at[b]).start()

    def owned(b):
        q = 16 * lax.div(18 * z - part + 15, 16) + part + 16 * b
        owner = lax.div(q, 9)
        return q <= 18 * z + 17, owner - 2 * z, q - 9 * owner

    def final_copy(b, to_high, e, dc, step):
        at = pl.ds(pl.multiple_of(16 * e, 16), 16)
        to_lat = 4 * z + 2 * to_high + (1 - core if dc else core)
        return remote(s4.at[b], fin.at[core, at], fs_send.at[b, dc, step], fs_recv, to_lat, lon_at(step), "r4")

    def needed(e, to_core):
        return ((to_core == 0) & (e <= 4)) | ((to_core == 1) & (e >= 4))

    def spread_out():
        for b in range(2):
            valid, to_high, e = owned(b)

            @pl.when(valid)
            def _():
                arrived(r3.at[b], recv3.at[b])
                total = r3[b, 0].astype(F32)
                for step in range(1, N_Z):
                    total = total + r3[b, step].astype(F32)
                s4[b] = total

            for dc in range(2):
                @pl.when(valid & needed(e, 1 - core if dc else core))
                def _():
                    for step in range(N_LON):
                        if dc or step:
                            final_copy(b, to_high, e, dc, step).start()
                        else:
                            @pl.when(to_high == x_high)
                            def _():
                                at = pl.ds(pl.multiple_of(16 * e, 16), 16)
                                pltpu.make_async_copy(s4.at[b], fin.at[core, at], fs_recv).start()

                            @pl.when(to_high != x_high)
                            def _():
                                final_copy(b, to_high, e, 0, 0).start()

    circle_total = ztf[...]
    z_high = circle_total.astype(BF16)
    z_low = (circle_total - z_high.astype(F32)).astype(BF16)
    z_parts = jnp.concatenate([z_high, z_low], axis=0)

    def pull(half):
        grad = dot(hh[pl.ds(half * 2 * LONS, 2 * LONS), :], wt[...])
        for a in range(2):
            i2 = 2 * half + a
            twice = jnp.concatenate([yy[i2], yy[i2]], axis=0)
            ig_ref[i2] = (grad[a * LONS:(a + 1) * LONS] + dot(twice, z_parts, 0, 0)).astype(BF16)

    spread_rows(far, *GROUPS[0], range(4))
    mix(0)
    spread_rows(far, *GROUPS[1], range(4))
    mix(1)
    first(0)
    spread_rows(far, *GROUPS[2], range(4))
    mix(2)
    first(1)
    first(2)
    second(0)
    second(1)
    pull(0)
    third(0)
    second(2)
    second(3)
    pull(1)
    third(1)
    third(2)
    third(3)
    spread_out()
    for index in level:
        halo(index).wait_send()

    @pl.when(has_down)
    def _():
        v_halo(0).wait_send()
        for index in from_up:
            halo(index).wait_send()

    @pl.when(has_up)
    def _():
        v_halo(1).wait_send()
        for index in from_down:
            halo(index).wait_send()

    @pl.when(north)
    def _():
        y_halo(6).wait_send()

    @pl.when(south)
    def _():
        y_halo(0).wait_send()

    @pl.when(polar_dev)
    def _():
        for dc in range(2):
            for step in range(N_LON):
                if dc or step:
                    gs_copy(dc, step).wait_send()

    for group in range(len(GROUPS)):
        twin_copy(group).wait_send()
    for run in range(len(RUNS)):
        for step in range(1, 4):
            first_copy(run, step).wait_send()
            second_copy(run, step).wait_send()
    for k in range(K):
        to_z, b, copy = granule(k)

        @pl.when(to_z != z)
        def _():
            copy.wait_send()

    some = fin.at[:, pl.ds(0, 80)]
    pltpu.make_async_copy(some, some, fs_recv).wait()
    rows = pl.ds(pl.multiple_of(72 * core, 8), 72)
    for half in range(2):
        wg_ref[:, pl.ds(128 * half, 128)] = fin[half, rows, :]

    for b in range(2):
        valid, to_high, e = owned(b)
        for dc in range(2):
            @pl.when(valid & needed(e, 1 - core if dc else core))
            def _():
                for step in range(N_LON):
                    if dc or step:
                        final_copy(b, to_high, e, dc, step).wait_send()
                    else:
                        @pl.when(to_high != x_high)
                        def _():
                            final_copy(b, to_high, e, 0, 0).wait_send()


def body(input_field, grad_out, weight, filt, zonal_weight, widths, offsets, polar_rows):
    dma = pltpu.SemaphoreType.DMA
    hbm = pl.BlockSpec(memory_space=pltpu.HBM)
    vmem = pl.BlockSpec(memory_space=pltpu.VMEM)
    smem = pl.BlockSpec(memory_space=pltpu.SMEM)
    groups, runs = len(GROUPS), len(RUNS)
    return pl.pallas_call(
        kernel,
        out_shape=(pltpu.VMEM((ROWS, LONS, C), BF16), pltpu.VMEM((72, C), F32)),
        in_specs=[hbm, hbm, hbm, vmem, hbm, smem, smem, smem],
        out_specs=(vmem, vmem),
        scratch_shapes=[
            pltpu.VMEM((8, LONS + 2 * REACH, C), BF16),
            pltpu.VMEM((ROWS, LONS, C), BF16),
            pltpu.VMEM((C, ROWS * LONS), BF16),
            pltpu.VMEM((K * C, C), BF16),
            pltpu.VMEM((K * C, C), BF16),
            pltpu.VMEM((CANDS, 128, 2 * REACH + 1), F32),
            pltpu.VMEM((8, 16, DEPTH), BF16),
            pltpu.VMEM((2, 2, 16, DEPTH), BF16),
            pltpu.VMEM((32, DEPTH), F32),
            pltpu.VMEM((ROWS, K * JB, DEPTH), BF16),
            pltpu.VMEM((ROWS * LONS, K * C), BF16),
            pltpu.VMEM((K, 3, ROWS, LONS), BF16),
            pltpu.VMEM((16, K * LONS), F32),
            pltpu.VMEM((2, 256, 128), F32),
            pltpu.VMEM((8, 32, LONS), BF16),
            pltpu.VMEM((2, 32, LONS), BF16),
            pltpu.VMEM((ROWS, 32, LONS), BF16),
            pltpu.VMEM((32, C), F32),
            pltpu.VMEM((C, 32), F32),
            pltpu.VMEM((8, C), F32),
            pltpu.VMEM((N_LON, 8, C), F32),
            pltpu.VMEM((8, C), F32),
            pltpu.VMEM((K, C, 128), F32),
            pltpu.VMEM((K, C, 128), BF16),
            pltpu.VMEM((K, C, 128), BF16),
            pltpu.VMEM((K, 4, 4, 16, 128), BF16),
            pltpu.VMEM((4, K, 4, 16, 128), BF16),
            pltpu.VMEM((K, 4, 16, 128), BF16),
            pltpu.VMEM((4, K, 16, 128), BF16),
            pltpu.VMEM((K, 16, 128), BF16),
            pltpu.VMEM((2, N_Z, 16, 128), BF16),
            pltpu.VMEM((2, 16, 128), F32),
            pltpu.VMEM((2, 144, 128), F32),
            dma((4,)), dma((8,)), dma((8,)), dma((2,)), dma((2,)), dma, dma, dma((2, N_LON)), dma,
            dma((groups,)), dma((groups,)), dma((runs, 4)), dma((runs,)), dma((runs, 4)), dma((runs,)),
            dma((K,)), dma((2,)), dma((2, 2, N_LON)), dma,
        ],
        compiler_params=pltpu.CompilerParams(
            collective_id=0, has_side_effects=True, vmem_limit_bytes=48 * 1024 * 1024
        ),
        name="sphere_backward",
    )(*[
        pltpu.with_memory_space_constraint(array, pltpu.HBM)
        for array in (
            grad_out, input_field, weight, jnp.transpose(filt, (0, 2, 1, 3)),
            jnp.transpose(zonal_weight, (0, 2, 1, 3)), widths, offsets, polar_rows,
        )
    ])


def solution(mesh):
    in_specs = (
        P("lat", "lon", None),
        P("lat", "lon", None),
        P(),
        P(None, "lat", None, None),
        P(None, "lat", None, None),
        P("lat"),
        P("lat"),
        P(),
    )
    out_specs = (P("lat", "lon", None), P("lat", None))
    return jax.shard_map(body, mesh=mesh, in_specs=in_specs, out_specs=out_specs, check_vma=False)
```

```python
import functools
import math

import jax
import jax.numpy as jnp
from jax import lax
from jax.experimental import pallas as pl
from jax.experimental.pallas import tpu as pltpu
from jax.sharding import PartitionSpec as P

MESH = pl.DeviceIdType.MESH
F32 = jnp.float32
BF16 = jnp.bfloat16
ROWS = 4
LONS = 256
C = 256
K = 9
REACH = 16
JB = 64
WIN = JB + 2 * REACH
CANDS = 5
DEPTH = 512
N_LAT = 32
N_LON = 8
N_Z = 8
GROUPS = ((0, 4), (4, 7), (7, 9))
RUNS = ((0, 2, "y"), (2, 4, "x"), (4, 6, "x"), (6, 7, "y"), (7, 8, "y"), (8, 9, "x"))
GROUP_RUNS = ((0, 1), (2, 3), (4, 5))
FACTOR = 1.0 / math.sqrt(128 * 2048)


def dot(a, b, ca=1, cb=0):
    return lax.dot_general(a, b, (((ca,), (cb,)), ((), ())), preferred_element_type=F32)


def kernel(
    g_hbm, x_hbm, w_hbm, filt_hbm, z_hbm, width_hbm, offset_hbm, polar_hbm,
    ig_ref, wg_ref,
    filt_ref, width_ref, offset_ref, polar_ref,
    gx, gfar, xv, xt, wv, wt, lv, vown, vtwin, vfar, vf, vfh, tt, tth, facc, hh, wnear, zv, zs, yf, yown, yh, yy, ztf, zparts, zst, gs_own, gs_buf, gsel,
    wown, wsnd, cx, s1, r1, s2, r2, s3, r3, s4, fin,
    loc_sem, halo_send, halo_recv, vsend, vrecv, ysend, yrecv, gs_send, gs_sem,
    cs_send, cs_recv, send1, recv1, send2, recv2, send3, recv3, fs_send, fs_recv,
):
    lat = lax.axis_index("lat")
    lon = lax.axis_index("lon")
    core = lax.rem(lat, 2)
    twin = lat + 1 - 2 * core
    z, in_plane = lax.div(lat, 4), lax.rem(lat, 4)
    x_high, x_low, y = lax.div(in_plane, 2), lax.div(lon, 4), lax.rem(lon, 4)
    place = {"x": 2 * x_high + x_low, "y": y}

    def lon_at(step):
        return lax.rem(lon + step, N_LON)

    def remote(src, dst, send, recv, to_lat, to_lon, tag="rs"):
        return pltpu.make_async_remote_copy(
            src_ref=src, dst_ref=dst, send_sem=send, recv_sem=recv,
            device_id={"lat": to_lat, "lon": to_lon}, device_id_type=MESH,
        )

    north, south = lat == 0, lat == N_LAT - 1
    polar_dev = north | south
    affected = polar_dev | (lat == 1) | (lat == N_LAT - 2)

    barrier = pltpu.get_barrier_semaphore()

    def greet(to_lat, to_lon):
        pl.semaphore_signal(barrier, inc=1, device_id={"lat": to_lat, "lon": to_lon}, device_id_type=MESH)

    outer = lat - 1 + 2 * core
    to_next = (core == 1) & (x_high == 1) & (z < N_Z - 1)
    to_last = (core == 0) & (x_high == 0) & (z > 0)
    crosses = to_next | to_last

    @pl.when(crosses)
    def _():
        for step in (0, 1, N_LON - 1):
            greet(outer, lon_at(step))

    def lat_at(step):
        return 4 * lax.rem(z + step, N_Z) + in_plane

    for step in range(1, N_Z):
        greet(lat_at(step), lon)
    for turn_lat in range(4):
        for step in range(N_LON):
            if turn_lat or step:
                greet(4 * z + lax.rem(in_plane + turn_lat, 4), lon_at(step))

    g_copy = pltpu.make_async_copy(g_hbm, gx.at[pl.ds(2, ROWS), pl.ds(REACH, LONS)], loc_sem.at[0])
    x_copy = pltpu.make_async_copy(x_hbm, xv, loc_sem.at[1])
    w_copy = pltpu.make_async_copy(w_hbm, wv, loc_sem.at[2])
    z_copy = pltpu.make_async_copy(
        z_hbm.at[:, :, :, pl.ds(pl.multiple_of(lon * LONS, LONS), LONS)], zv, loc_sem.at[3]
    )
    small = [
        pltpu.make_async_copy(src, dst, loc_sem.at[4 + index])
        for index, (src, dst) in enumerate(
            ((filt_hbm, filt_ref), (width_hbm, width_ref), (offset_hbm, offset_ref), (polar_hbm, polar_ref))
        )
    ]
    for copy in small:
        copy.start()
    g_copy.start()
    x_copy.start()
    w_copy.start()

    @pl.when(polar_dev)
    def _():
        z_copy.start()

    for copy in small:
        copy.wait()
    span = 2 * REACH + 1
    row_i = lax.broadcasted_iota(jnp.int32, (ROWS, span), 0)
    tap = lax.broadcasted_iota(jnp.int32, (ROWS, span), 1)
    offset_v = jnp.zeros((ROWS, span), jnp.int32)
    width_v = jnp.zeros((ROWS, span), jnp.int32)
    for i in range(ROWS):
        offset_v = jnp.where(row_i == i, offset_ref[i], offset_v)
        width_v = jnp.where(row_i == i, width_ref[i], width_v)
    keep = jnp.abs(tap - REACH) <= width_v
    choose = {m: jnp.where(keep & (offset_v == 2 - m), 1.0, 0.0) for m in (2, 3, 4)}
    lv[...] = jnp.zeros_like(lv)
    for k in range(K):
        values = [filt_ref[k, r].astype(F32) for r in range(3)]
        for n in range(CANDS):
            terms = [choose[n + r] * values[r] for r in range(3) if n + r in choose]
            lv[n, pl.ds((4 - n) * 16 + k, ROWS, stride=16), :] = functools.reduce(jnp.add, terms)
    tap = lax.broadcasted_iota(jnp.int32, (span, DEPTH), 0)
    lane = lax.broadcasted_iota(jnp.int32, (span, DEPTH), 1)
    placed = jnp.zeros((128, DEPTH), F32)
    for n in range(CANDS):
        where = jnp.where(lane + tap == WIN * n + 2 * REACH, 1.0, 0.0).astype(BF16)
        placed = placed + dot(lv[n].astype(BF16), where)
    vown[...] = placed.astype(BF16).reshape(8, 16, DEPTH)

    g_copy.wait()
    pl.semaphore_wait(barrier, 4 * N_LON + N_Z - 2 + 3 * crosses.astype(jnp.int32))

    has_far = (outer >= 0) & (outer < N_LAT)
    near, far = 2 - 2 * core, 2 * core
    cols_of = {-1: (0, REACH, REACH + LONS), 0: (0, LONS, REACH), 1: (LONS - REACH, REACH, 0)}
    level, to_twin, to_far = ((0, 1), (1, -1)), ((2, 0), (3, 1), (4, -1)), ((5, 0), (6, 1), (7, -1))

    def halo(kind, index, dlon):
        c0, cn, c_to = cols_of[dlon]
        cols, to_cols = pl.ds(REACH + c0, cn), pl.ds(c_to, cn)
        if kind == "level":
            src, dst, to_lat = gx.at[pl.ds(2, ROWS), cols], gx.at[pl.ds(2, ROWS), to_cols], lat
        elif kind == "twin":
            src, dst, to_lat = gx.at[pl.ds(2 + near, 2), cols], gx.at[pl.ds(6 * core, 2), to_cols], twin
        else:
            src, dst, to_lat = gx.at[pl.ds(2 + far, 2), cols], gfar.at[:, to_cols], outer
        return remote(
            src, dst, halo_send.at[index], halo_recv.at[index], to_lat, lon_at(dlon % N_LON),
            "big" if kind == "far" and dlon == 0 else "halo",
        )

    def arrived(buffer, semaphore):
        pltpu.make_async_copy(buffer, buffer, semaphore).wait()

    def arrive(kind, moves):
        for index, dlon in moves:
            c0, cn, c_to = cols_of[dlon]
            cols = pl.ds(c_to, cn)
            if kind == "level":
                place_of = gx.at[pl.ds(2, ROWS), cols]
            elif kind == "twin":
                place_of = gx.at[pl.ds(6 - 6 * core, 2), cols]
            else:
                place_of = gfar.at[:, cols]
            arrived(place_of, halo_recv.at[index])

    def v_twin():
        return remote(vown.at[pl.ds(6 - 6 * core, 2)], vtwin, vsend.at[0], vrecv.at[0], twin, lon, "halo")

    def v_far():
        return remote(vown.at[pl.ds(6 * core, 2)], vfar, vsend.at[1], vrecv.at[1], outer, lon, "halo")

    for move in level:
        halo("level", *move).start()
    v_twin().start()
    for move in to_twin:
        halo("twin", *move).start()

    @pl.when(has_far)
    def _():
        v_far().start()
        for move in to_far[1:] + to_far[:1]:
            halo("far", *move).start()

    gx[pl.ds(6 * core, 2)] = jnp.zeros((2,) + gx.shape[1:], BF16)

    @pl.when(jnp.logical_not(has_far))
    def _():
        gfar[...] = jnp.zeros_like(gfar)
        vfar[...] = jnp.zeros_like(vfar)

    def gs_copy(dc, step):
        return remote(
            gs_own, gs_buf.at[lon], gs_send.at[dc, step], gs_sem, twin if dc else lat, lon_at(step), "halo"
        )

    def y_halo(first):
        return remote(yown.at[pl.ds(first, 2)], yh, ysend, yrecv, twin, lon, "halo")

    @pl.when(jnp.logical_not(polar_dev))
    def _():
        yown[...] = jnp.zeros_like(yown)

    @pl.when(polar_dev)
    def _():
        gs_own[...] = jnp.zeros_like(gs_own)
        for i in range(ROWS):
            gs_own[pl.ds(i, 1), :] = jnp.sum(
                gx[2 + i, pl.ds(REACH, LONS), :].astype(F32), axis=0, keepdims=True
            )
        for dc in range(2):
            for step in range(N_LON):
                if dc or step:
                    gs_copy(dc, step).start()
        pltpu.make_async_copy(gs_own, gs_buf.at[lon], gs_sem).start()
        pole = lax.div(lat, N_LAT // 2)
        entry = lax.broadcasted_iota(jnp.int32, (16, 16), 0)
        source = lax.broadcasted_iota(jnp.int32, (16, 16), 1)
        row = source & 3
        first_q = polar_ref[2 * pole] - lat * ROWS
        second_q = polar_ref[2 * pole + 1] - lat * ROWS
        polar_row = jnp.where((entry & 1) == 0, first_q, second_q)
        moved = row + (source >> 2)
        for i in range(ROWS):
            moved = moved + jnp.where(row == i, offset_ref[i], 0)
        hit = (row == polar_row) & (moved == (entry >> 1) - 2) & (source < 12)
        z_copy.wait()
        zs[pl.ds(8, 8), :] = jnp.zeros((8, K * LONS), F32)
        for k in range(K):
            for r in range(3):
                zs[pl.ds(4 * r, 4), pl.ds(k * LONS, LONS)] = zv[k, r].astype(F32)
        picked = dot(jnp.where(hit, 1.0, 0.0).astype(BF16), zs[...].astype(BF16))
        yf[...] = jnp.zeros_like(yf)
        for k in range(K):
            for half in range(2):
                yf[half, pl.ds(k, 16, stride=16), :] = picked[:, k * LONS + 128 * half:k * LONS + 128 * half + 128]
        for half in range(2):
            yown[:, :, pl.ds(128 * half, 128)] = yf[half].astype(BF16).reshape(8, 32, 128)

    @pl.when(north)
    def _():
        y_halo(6).start()

    @pl.when(south)
    def _():
        y_halo(0).start()

    x_copy.wait()
    for i in range(ROWS):
        xt[:, pl.ds(i * LONS, LONS)] = xv[i].T
    def band_rows(rows, lanes, put):
        def band(step, carry):
            for k in (3 * step, 3 * step + 1, 3 * step + 2):
                for a in range(2):
                    row = jnp.broadcast_to(rows[pl.ds(16 * a + k, 1), :], (JB, lanes))
                    rolled = pltpu.roll(row, 0, 1, stride=1, stride_axis=0)
                    put(a)[pl.ds(pl.multiple_of(k * JB, JB), JB), :] = rolled.astype(BF16)
            return carry

        lax.fori_loop(0, K // 3, band, 0)

    def own_windows(i2, jb):
        windows = [gx[i2 + n, pl.ds(jb * JB, WIN), :] for n in range(CANDS)]
        windows.append(jnp.zeros((DEPTH - CANDS * WIN, C), BF16))
        return jnp.concatenate(windows, axis=0)

    def put_rows(i2, jb, k0, k1, moved):
        rows = pl.ds(pl.multiple_of(i2 * LONS + jb * JB, JB), JB)
        for k in range(k0, k1):
            hh[rows, pl.ds(k * C, C)] = moved[(k - k0) * JB:(k - k0 + 1) * JB]

    def spread_near(blocks):
        def spread(step, carry):
            for jb in blocks:
                i2 = near + step
                put_rows(i2, jb, 0, K, dot(tt[i2], own_windows(i2, jb)).astype(BF16))
            return carry

        lax.fori_loop(0, 2, spread, 0)

    def spread_far_own():
        def spread(step, carry):
            for jb in range(4):
                facc[4 * step + jb] = dot(tt[far + step], own_windows(far + step, jb))
            return carry

        lax.fori_loop(0, 2, spread, 0)

    def spread_far(k0, k1):
        at = pl.ds(k0 * JB, (k1 - k0) * JB)

        def spread(step, carry):
            for jb in range(4):
                windows = [gfar[n, pl.ds(jb * JB, WIN), :] for n in range(2)]
                windows.append(jnp.zeros((256 - 2 * WIN, C), BF16))
                moved = facc[4 * step + jb, at] + dot(tth[step, at], jnp.concatenate(windows, axis=0))
                put_rows(far + step, jb, k0, k1, moved.astype(BF16))
            return carry

        lax.fori_loop(0, 2, spread, 0)

    v_twin().wait_recv()
    arrive("twin", to_twin[:1])
    for a in range(2):
        vf[pl.ds(16 * a, 16), :] = vown[2 + near + a].astype(F32) + vtwin[a].astype(F32)
    band_rows(vf, DEPTH, lambda a: tt.at[near + a])
    spread_near((1, 2))
    for a in range(2):
        vf[pl.ds(16 * a, 16), :] = vown[2 + far + a].astype(F32)
    band_rows(vf, DEPTH, lambda a: tt.at[far + a])

    for i2 in range(ROWS):
        yy[i2] = yown[2 + i2]

    @pl.when(lat == 1)
    def _():
        y_halo(6).wait_recv()
        yy[pl.ds(0, 2)] = yh[...]

    @pl.when(lat == N_LAT - 2)
    def _():
        y_halo(0).wait_recv()
        yy[pl.ds(2, 2)] = yh[...]

    circle = jnp.zeros((C, 32), F32)
    for i2 in range(ROWS):
        circle = circle + dot(xt[:, pl.ds(i2 * LONS, LONS)], yy[i2], 1, 1)
    zst[...] = circle * FACTOR

    @pl.when(jnp.logical_not(affected))
    def _():
        gsel[...] = jnp.zeros_like(gsel)

    @pl.when(affected)
    def _():
        pltpu.make_async_copy(gs_buf, gs_buf, gs_sem).wait()
        total = gs_buf[0]
        for step in range(1, N_LON):
            total = total + gs_buf[step]
        pole = lax.div(lat, N_LAT // 2)
        gsel[...] = jnp.zeros_like(gsel)
        for q in range(2):
            mine = polar_ref[2 * pole + q] - pole * (N_LAT - 1) * ROWS
            picked = jnp.zeros((1, C), F32)
            for i in range(ROWS):
                picked = picked + total[i:i + 1] * (mine == i).astype(F32)
            gsel[pl.ds(q, 1), :] = picked

    arrive("level", level)
    arrive("twin", to_twin[1:])
    spread_near((0, 3))
    spread_far_own()
    near_lons = pl.ds(pl.multiple_of(near * LONS, 2 * LONS), 2 * LONS)
    far_lons = pl.ds(pl.multiple_of(far * LONS, 2 * LONS), 2 * LONS)
    for k in range(K):
        share = dot(xt[:, near_lons], hh[near_lons, pl.ds(k * C, C)]) * FACTOR
        for q in range(2):
            share = share + zst[:, 16 * q + k:16 * q + k + 1] * gsel[q:q + 1, :]
        wnear[k] = share

    @pl.when(has_far)
    def _():
        arrived(vfar, vrecv.at[1])

    for a in range(2):
        values = vfar[a].astype(F32)
        low_side = pltpu.roll(values, WIN * a, 1) if a else values
        high_side = pltpu.roll(values, 128 + WIN * a, 1)
        vfh[pl.ds(16 * a, 16), :] = jnp.where(core == 0, low_side, high_side)[:, :256]
    band_rows(vfh, 256, lambda a: tth.at[a])

    @pl.when(has_far)
    def _():
        arrive("far", to_far)

    def twin_copy(group):
        k0, k1 = GROUPS[group]
        at = pl.ds(k0, k1 - k0)
        return remote(wsnd.at[at], cx.at[at], cs_send.at[group], cs_recv.at[group], twin, lon)

    def mix(group):
        for k in range(*GROUPS[group]):
            share = wnear[k] + dot(xt[:, far_lons], hh[far_lons, pl.ds(k * C, C)]) * FACTOR
            first, second = share[:, :128], share[:, 128:]
            wown[k] = jnp.where(core == 0, first, second)
            wsnd[k] = jnp.where(core == 0, second, first).astype(BF16)
        twin_copy(group).start()

    def along(axis, step):
        to = lax.rem(place[axis] + step, 4)
        if axis == "y":
            return to, lat, lon + to - y
        return to, lat + 2 * (lax.div(to, 2) - x_high), lon + 4 * (lax.rem(to, 2) - x_low)

    def first_piece(run, to):
        k0, k1, axis = RUNS[run]
        at = pl.ds(k0, k1 - k0)
        return s1.at[at, to] if axis == "y" else s1.at[at, :, to]

    def first_copy(run, step):
        k0, k1, axis = RUNS[run]
        to, to_lat, to_lon = along(axis, step)
        dst = r1.at[place[axis], pl.ds(k0, k1 - k0)]
        return remote(first_piece(run, to), dst, send1.at[run, step], recv1.at[run], to_lat, to_lon, "r2")

    def second_copy(run, step):
        k0, k1, axis = RUNS[run]
        axis = "x" if axis == "y" else "y"
        to, to_lat, to_lon = along(axis, step)
        at = pl.ds(k0, k1 - k0)
        return remote(
            s2.at[at, to], r2.at[place[axis], at], send2.at[run, step], recv2.at[run], to_lat, to_lon, "r2"
        )

    def first(group):
        twin_copy(group).wait_recv()
        for k in range(*GROUPS[group]):
            s1[k] = (wown[k] + cx[k].astype(F32)).astype(BF16).reshape(4, 4, 16, 128)
        for run in GROUP_RUNS[group]:
            for step in range(1, 4):
                first_copy(run, step).start()

    def second(run):
        k0, k1, axis = RUNS[run]
        arrived(r1.at[pl.ds(0, 3), pl.ds(k0, k1 - k0)], recv1.at[run])
        for k in range(k0, k1):
            total = (s1[k, place[axis]] if axis == "y" else s1[k, :, place[axis]]).astype(F32)
            for step in range(1, 4):
                total = total + r1[lax.rem(place[axis] + step, 4), k].astype(F32)
            s2[k] = total.astype(BF16)
        for step in range(1, 4):
            second_copy(run, step).start()

    part = 4 * y + place["x"]

    def granule(k):
        q = 16 * k + part
        to_z = lax.div(q, 18)
        b = lax.div(q - 18 * to_z, 16)
        copy = remote(
            s3.at[k], r3.at[b, z], send3.at[k], recv3.at[b], 4 * to_z + in_plane, lon, "r3"
        )
        return to_z, b, copy

    def third(run):
        k0, k1, axis = RUNS[run]
        axis = "x" if axis == "y" else "y"
        arrived(r2.at[pl.ds(0, 3), pl.ds(k0, k1 - k0)], recv2.at[run])
        for k in range(k0, k1):
            total = s2[k, place[axis]].astype(F32)
            for step in range(1, 4):
                total = total + r2[lax.rem(place[axis] + step, 4), k].astype(F32)
            s3[k] = total.astype(BF16)
        for k in range(k0, k1):
            to_z, b, copy = granule(k)

            @pl.when(to_z != z)
            def _():
                copy.start()

            @pl.when(to_z == z)
            def _():
                pltpu.make_async_copy(s3.at[k], r3.at[b, z], recv3.at[b]).start()

    def owned(b):
        q = 16 * lax.div(18 * z - part + 15, 16) + part + 16 * b
        owner = lax.div(q, 9)
        return q <= 18 * z + 17, owner - 2 * z, q - 9 * owner

    def final_copy(b, to_high, e, dc, step):
        at = pl.ds(pl.multiple_of(16 * e, 16), 16)
        to_lat = 4 * z + 2 * to_high + (1 - core if dc else core)
        return remote(s4.at[b], fin.at[core, at], fs_send.at[b, dc, step], fs_recv, to_lat, lon_at(step), "r4")

    def needed(e, to_core):
        return ((to_core == 0) & (e <= 4)) | ((to_core == 1) & (e >= 4))

    def spread_out():
        for b in range(2):
            valid, to_high, e = owned(b)

            @pl.when(valid)
            def _():
                arrived(r3.at[b], recv3.at[b])
                total = r3[b, 0].astype(F32)
                for step in range(1, N_Z):
                    total = total + r3[b, step].astype(F32)
                s4[b] = total

            for dc in range(2):
                @pl.when(valid & needed(e, 1 - core if dc else core))
                def _():
                    for step in range(N_LON):
                        if dc or step:
                            final_copy(b, to_high, e, dc, step).start()
                        else:
                            @pl.when(to_high == x_high)
                            def _():
                                at = pl.ds(pl.multiple_of(16 * e, 16), 16)
                                pltpu.make_async_copy(s4.at[b], fin.at[core, at], fs_recv).start()

                            @pl.when(to_high != x_high)
                            def _():
                                final_copy(b, to_high, e, 0, 0).start()

    def prepare_pull():
        w_copy.wait()

        def turn(k, carry):
            at = pl.ds(pl.multiple_of(k * C, C), C)
            wt[at, :] = wv[at, :].T
            return carry

        lax.fori_loop(0, K, turn, 0)

        circle_sum = gsel[...]
        high = circle_sum.astype(BF16)
        low = (circle_sum - high.astype(F32)).astype(BF16)
        parts = jnp.concatenate([high.astype(F32), low.astype(F32)], axis=0).astype(BF16)
        ztf[...] = jnp.zeros_like(ztf)
        for k in range(K):
            mixed = dot(parts, wt[pl.ds(k * C, C), :])
            mixed = mixed[:8] + mixed[8:]
            for q in range(2):
                ztf[pl.ds(16 * q + k, 1), :] = mixed[q:q + 1]

        circle_total = ztf[...]
        z_high = circle_total.astype(BF16)
        z_low = (circle_total - z_high.astype(F32)).astype(BF16)
        z_parts = jnp.concatenate([z_high, z_low], axis=0)
        zparts[...] = z_parts

    def pull(half):
        z_parts = zparts[...]
        grad = dot(hh[pl.ds(half * 2 * LONS, 2 * LONS), :], wt[...])
        for a in range(2):
            i2 = 2 * half + a
            twice = jnp.concatenate([yy[i2], yy[i2]], axis=0)
            ig_ref[i2] = (grad[a * LONS:(a + 1) * LONS] + dot(twice, z_parts, 0, 0)).astype(BF16)

    spread_far(*GROUPS[0])
    mix(0)
    spread_far(*GROUPS[1])
    mix(1)
    first(0)
    spread_far(*GROUPS[2])
    mix(2)
    first(1)
    first(2)
    second(0)
    second(1)
    prepare_pull()
    pull(0)
    second(2)
    second(3)
    third(0)
    third(1)
    second(4)
    second(5)
    pull(1)
    third(2)
    third(3)
    third(4)
    third(5)
    spread_out()
    for move in level:
        halo("level", *move).wait_send()
    v_twin().wait_send()
    for move in to_twin:
        halo("twin", *move).wait_send()

    @pl.when(has_far)
    def _():
        v_far().wait_send()
        for move in to_far:
            halo("far", *move).wait_send()

    @pl.when(north)
    def _():
        y_halo(6).wait_send()

    @pl.when(south)
    def _():
        y_halo(0).wait_send()

    @pl.when(polar_dev)
    def _():
        for dc in range(2):
            for step in range(N_LON):
                if dc or step:
                    gs_copy(dc, step).wait_send()

    for group in range(len(GROUPS)):
        twin_copy(group).wait_send()
    for run in range(len(RUNS)):
        for step in range(1, 4):
            first_copy(run, step).wait_send()
            second_copy(run, step).wait_send()
    for k in range(K):
        to_z, b, copy = granule(k)

        @pl.when(to_z != z)
        def _():
            copy.wait_send()

    some = fin.at[:, pl.ds(0, 80)]
    pltpu.make_async_copy(some, some, fs_recv).wait()
    rows = pl.ds(pl.multiple_of(72 * core, 8), 72)
    for half in range(2):
        wg_ref[:, pl.ds(128 * half, 128)] = fin[half, rows, :]

    for b in range(2):
        valid, to_high, e = owned(b)
        for dc in range(2):
            @pl.when(valid & needed(e, 1 - core if dc else core))
            def _():
                for step in range(N_LON):
                    if dc or step:
                        final_copy(b, to_high, e, dc, step).wait_send()
                    else:
                        @pl.when(to_high != x_high)
                        def _():
                            final_copy(b, to_high, e, 0, 0).wait_send()


def store(ig_ref, wg_ref, ig_hbm, wg_hbm, sem):
    copies = [
        pltpu.make_async_copy(ig_ref, ig_hbm, sem.at[0]),
        pltpu.make_async_copy(wg_ref, wg_hbm, sem.at[1]),
    ]
    for copy in copies:
        copy.start()
    for copy in copies:
        copy.wait()


def body(input_field, grad_out, weight, filt, zonal_weight, widths, offsets, polar_rows):
    dma = pltpu.SemaphoreType.DMA
    hbm = pl.BlockSpec(memory_space=pltpu.HBM)
    vmem = pl.BlockSpec(memory_space=pltpu.VMEM)
    groups, runs = len(GROUPS), len(RUNS)
    grads = pl.pallas_call(
        kernel,
        out_shape=(pltpu.VMEM((ROWS, LONS, C), BF16), pltpu.VMEM((72, C), F32)),
        in_specs=[hbm] * 8,
        out_specs=(vmem, vmem),
        scratch_shapes=[
            pltpu.VMEM((K, 3, ROWS, 2 * REACH + 1), BF16),
            pltpu.SMEM((ROWS,), jnp.int32), pltpu.SMEM((ROWS,), jnp.int32), pltpu.SMEM((4,), jnp.int32),
            pltpu.VMEM((8, LONS + 2 * REACH, C), BF16),
            pltpu.VMEM((2, LONS + 2 * REACH, C), BF16),
            pltpu.VMEM((ROWS, LONS, C), BF16),
            pltpu.VMEM((C, ROWS * LONS), BF16),
            pltpu.VMEM((K * C, C), BF16),
            pltpu.VMEM((K * C, C), BF16),
            pltpu.VMEM((CANDS, 128, 2 * REACH + 1), F32),
            pltpu.VMEM((8, 16, DEPTH), BF16),
            pltpu.VMEM((2, 16, DEPTH), BF16),
            pltpu.VMEM((2, 16, DEPTH), BF16),
            pltpu.VMEM((32, DEPTH), F32),
            pltpu.VMEM((32, 256), F32),
            pltpu.VMEM((ROWS, K * JB, DEPTH), BF16),
            pltpu.VMEM((2, K * JB, 256), BF16),
            pltpu.VMEM((8, K * JB, C), F32),
            pltpu.VMEM((ROWS * LONS, K * C), BF16),
            pltpu.VMEM((K, C, C), F32),
            pltpu.VMEM((K, 3, ROWS, LONS), BF16),
            pltpu.VMEM((16, K * LONS), F32),
            pltpu.VMEM((2, 256, 128), F32),
            pltpu.VMEM((8, 32, LONS), BF16),
            pltpu.VMEM((2, 32, LONS), BF16),
            pltpu.VMEM((ROWS, 32, LONS), BF16),
            pltpu.VMEM((32, C), F32),
            pltpu.VMEM((64, C), BF16),
            pltpu.VMEM((C, 32), F32),
            pltpu.VMEM((8, C), F32),
            pltpu.VMEM((N_LON, 8, C), F32),
            pltpu.VMEM((8, C), F32),
            pltpu.VMEM((K, C, 128), F32),
            pltpu.VMEM((K, C, 128), BF16),
            pltpu.VMEM((K, C, 128), BF16),
            pltpu.VMEM((K, 4, 4, 16, 128), BF16),
            pltpu.VMEM((4, K, 4, 16, 128), BF16),
            pltpu.VMEM((K, 4, 16, 128), BF16),
            pltpu.VMEM((4, K, 16, 128), BF16),
            pltpu.VMEM((K, 16, 128), BF16),
            pltpu.VMEM((2, N_Z, 16, 128), BF16),
            pltpu.VMEM((2, 16, 128), F32),
            pltpu.VMEM((2, 144, 128), F32),
            dma((8,)), dma((8,)), dma((8,)), dma((2,)), dma((2,)), dma, dma, dma((2, N_LON)), dma,
            dma((groups,)), dma((groups,)), dma((runs, 4)), dma((runs,)), dma((runs, 4)), dma((runs,)),
            dma((K,)), dma((2,)), dma((2, 2, N_LON)), dma,
        ],
        compiler_params=pltpu.CompilerParams(
            collective_id=0, has_side_effects=True, vmem_limit_bytes=48 * 1024 * 1024
        ),
        name="sphere_backward",
    )(*[
        pltpu.with_memory_space_constraint(array, pltpu.HBM)
        for array in (
            grad_out, input_field, weight, jnp.transpose(filt, (0, 2, 1, 3)),
            jnp.transpose(zonal_weight, (0, 2, 1, 3)), widths, offsets, polar_rows,
        )
    ])
    return tuple(pl.pallas_call(
        store,
        out_shape=(
            jax.ShapeDtypeStruct((ROWS, LONS, C), BF16),
            jax.ShapeDtypeStruct((72, C), F32),
        ),
        in_specs=[pl.BlockSpec(memory_space=pl.ANY)] * 2,
        out_specs=(pl.BlockSpec(memory_space=pl.ANY),) * 2,
        scratch_shapes=[dma((2,))],
        name="store",
    )(*[pltpu.with_memory_space_constraint(array, pltpu.VMEM) for array in grads]))


def solution(mesh):
    in_specs = (
        P("lat", "lon", None),
        P("lat", "lon", None),
        P(),
        P(None, "lat", None, None),
        P(None, "lat", None, None),
        P("lat"),
        P("lat"),
        P(),
    )
    out_specs = (P("lat", "lon", None), P("lat", None))
    return jax.shard_map(body, mesh=mesh, in_specs=in_specs, out_specs=out_specs, check_vma=False)
```

```python
import functools
import math

import jax
import jax.numpy as jnp
from jax import lax
from jax.experimental import pallas as pl
from jax.experimental.pallas import tpu as pltpu
from jax.sharding import PartitionSpec as P

MESH = pl.DeviceIdType.MESH
F32 = jnp.float32
BF16 = jnp.bfloat16
ROWS = 4
LONS = 256
C = 256
K = 9
REACH = 16
JB = 64
WIN = JB + 2 * REACH
CANDS = 5
DEPTH = 512
N_LAT = 32
N_LON = 8
N_Z = 8
GROUPS = ((0, 2), (2, 5), (5, 9))
FACTOR = 1.0 / math.sqrt(128 * 2048)


def dot(a, b, ca=1, cb=0):
    return lax.dot_general(a, b, (((ca,), (cb,)), ((), ())), preferred_element_type=F32)


def kernel(
    g_hbm, x_hbm, w_hbm, filt_hbm, z_hbm, width_hbm, offset_hbm, polar_hbm,
    ig_ref, wg_ref,
    filt_ref, width_ref, offset_ref, polar_ref,
    gx, gfar, xv, xt, wv, wt, lv, vown, vtwin, vfar, vf, vfh, tt, tth, facc, hh, wnear, zv, zs, yf, yown, yh, yy, ztf, zparts, zst, gs_own, gs_buf, gsel,
    wown, wsnd, cx, s1, rplane, s3, r3, s4, fin,
    loc_sem, halo_send, halo_recv, vsend, vrecv, ysend, yrecv, gs_send, gs_sem,
    cs_send, cs_recv, send_plane, recv_plane, send3, recv3, fs_send, fs_recv,
):
    lat = lax.axis_index("lat")
    lon = lax.axis_index("lon")
    core = lax.rem(lat, 2)
    twin = lat + 1 - 2 * core
    z, in_plane = lax.div(lat, 4), lax.rem(lat, 4)
    x_high, x_low, y = lax.div(in_plane, 2), lax.div(lon, 4), lax.rem(lon, 4)
    x = 2 * x_high + x_low

    def lon_at(step):
        return lax.rem(lon + step, N_LON)

    def remote(src, dst, send, recv, to_lat, to_lon):
        return pltpu.make_async_remote_copy(
            src_ref=src, dst_ref=dst, send_sem=send, recv_sem=recv,
            device_id={"lat": to_lat, "lon": to_lon}, device_id_type=MESH,
        )

    north, south = lat == 0, lat == N_LAT - 1
    polar_dev = north | south
    affected = polar_dev | (lat == 1) | (lat == N_LAT - 2)

    barrier = pltpu.get_barrier_semaphore()

    def greet(to_lat, to_lon):
        pl.semaphore_signal(barrier, inc=1, device_id={"lat": to_lat, "lon": to_lon}, device_id_type=MESH)

    outer = lat - 1 + 2 * core
    to_next = (core == 1) & (x_high == 1) & (z < N_Z - 1)
    to_last = (core == 0) & (x_high == 0) & (z > 0)
    crosses = to_next | to_last

    @pl.when(crosses)
    def _():
        for step in (0, 1, N_LON - 1):
            greet(outer, lon_at(step))

    def lat_at(step):
        return 4 * lax.rem(z + step, N_Z) + in_plane

    for step in range(1, N_Z):
        greet(lat_at(step), lon)
    for turn_lat in range(4):
        for step in range(N_LON):
            if turn_lat or step:
                greet(4 * z + lax.rem(in_plane + turn_lat, 4), lon_at(step))

    g_copy = pltpu.make_async_copy(g_hbm, gx.at[pl.ds(2, ROWS), pl.ds(REACH, LONS)], loc_sem.at[0])
    x_copy = pltpu.make_async_copy(x_hbm, xv, loc_sem.at[1])
    w_copy = pltpu.make_async_copy(w_hbm, wv, loc_sem.at[2])
    z_copy = pltpu.make_async_copy(
        z_hbm.at[:, :, :, pl.ds(pl.multiple_of(lon * LONS, LONS), LONS)], zv, loc_sem.at[3]
    )
    small = [
        pltpu.make_async_copy(src, dst, loc_sem.at[4 + index])
        for index, (src, dst) in enumerate(
            ((filt_hbm, filt_ref), (width_hbm, width_ref), (offset_hbm, offset_ref), (polar_hbm, polar_ref))
        )
    ]
    for copy in small:
        copy.start()
    g_copy.start()
    x_copy.start()
    w_copy.start()

    @pl.when(polar_dev)
    def _():
        z_copy.start()

    for copy in small:
        copy.wait()
    span = 2 * REACH + 1
    row_i = lax.broadcasted_iota(jnp.int32, (ROWS, span), 0)
    tap = lax.broadcasted_iota(jnp.int32, (ROWS, span), 1)
    offset_v = jnp.zeros((ROWS, span), jnp.int32)
    width_v = jnp.zeros((ROWS, span), jnp.int32)
    for i in range(ROWS):
        offset_v = jnp.where(row_i == i, offset_ref[i], offset_v)
        width_v = jnp.where(row_i == i, width_ref[i], width_v)
    keep = jnp.abs(tap - REACH) <= width_v
    choose = {m: jnp.where(keep & (offset_v == 2 - m), 1.0, 0.0) for m in (2, 3, 4)}
    lv[...] = jnp.zeros_like(lv)
    for k in range(K):
        values = [filt_ref[k, r].astype(F32) for r in range(3)]
        for n in range(CANDS):
            terms = [choose[n + r] * values[r] for r in range(3) if n + r in choose]
            lv[n, pl.ds((4 - n) * 16 + k, ROWS, stride=16), :] = functools.reduce(jnp.add, terms)
    tap = lax.broadcasted_iota(jnp.int32, (span, DEPTH), 0)
    lane = lax.broadcasted_iota(jnp.int32, (span, DEPTH), 1)
    placed = jnp.zeros((128, DEPTH), F32)
    for n in range(CANDS):
        where = jnp.where(lane + tap == WIN * n + 2 * REACH, 1.0, 0.0).astype(BF16)
        placed = placed + dot(lv[n].astype(BF16), where)
    vown[...] = placed.astype(BF16).reshape(8, 16, DEPTH)

    g_copy.wait()
    pl.semaphore_wait(barrier, 4 * N_LON + N_Z - 2 + 3 * crosses.astype(jnp.int32))

    has_far = (outer >= 0) & (outer < N_LAT)
    near, far = 2 - 2 * core, 2 * core
    cols_of = {-1: (0, REACH, REACH + LONS), 0: (0, LONS, REACH), 1: (LONS - REACH, REACH, 0)}
    level, to_twin, to_far = ((0, 1), (1, -1)), ((2, 0), (3, 1), (4, -1)), ((5, 0), (6, 1), (7, -1))

    def halo(kind, index, dlon):
        c0, cn, c_to = cols_of[dlon]
        cols, to_cols = pl.ds(REACH + c0, cn), pl.ds(c_to, cn)
        if kind == "level":
            src, dst, to_lat = gx.at[pl.ds(2, ROWS), cols], gx.at[pl.ds(2, ROWS), to_cols], lat
        elif kind == "twin":
            src, dst, to_lat = gx.at[pl.ds(2 + near, 2), cols], gx.at[pl.ds(6 * core, 2), to_cols], twin
        else:
            src, dst, to_lat = gx.at[pl.ds(2 + far, 2), cols], gfar.at[:, to_cols], outer
        return remote(
            src, dst, halo_send.at[index], halo_recv.at[index], to_lat, lon_at(dlon % N_LON),
        )

    def arrived(buffer, semaphore):
        pltpu.make_async_copy(buffer, buffer, semaphore).wait()

    def arrive(kind, moves):
        for index, dlon in moves:
            c0, cn, c_to = cols_of[dlon]
            cols = pl.ds(c_to, cn)
            if kind == "level":
                place_of = gx.at[pl.ds(2, ROWS), cols]
            elif kind == "twin":
                place_of = gx.at[pl.ds(6 - 6 * core, 2), cols]
            else:
                place_of = gfar.at[:, cols]
            arrived(place_of, halo_recv.at[index])

    def v_twin():
        return remote(vown.at[pl.ds(6 - 6 * core, 2)], vtwin, vsend.at[0], vrecv.at[0], twin, lon)

    def v_far():
        return remote(vown.at[pl.ds(6 * core, 2)], vfar, vsend.at[1], vrecv.at[1], outer, lon)

    for move in level:
        halo("level", *move).start()
    v_twin().start()
    for move in to_twin:
        halo("twin", *move).start()

    @pl.when(has_far)
    def _():
        v_far().start()
        for move in to_far[1:] + to_far[:1]:
            halo("far", *move).start()

    gx[pl.ds(6 * core, 2)] = jnp.zeros((2,) + gx.shape[1:], BF16)

    @pl.when(jnp.logical_not(has_far))
    def _():
        gfar[...] = jnp.zeros_like(gfar)
        vfar[...] = jnp.zeros_like(vfar)

    def gs_copy(dc, step):
        return remote(
            gs_own, gs_buf.at[lon], gs_send.at[dc, step], gs_sem, twin if dc else lat, lon_at(step)
        )

    def y_halo(first):
        return remote(yown.at[pl.ds(first, 2)], yh, ysend, yrecv, twin, lon)

    @pl.when(jnp.logical_not(polar_dev))
    def _():
        yown[...] = jnp.zeros_like(yown)

    @pl.when(polar_dev)
    def _():
        gs_own[...] = jnp.zeros_like(gs_own)
        for i in range(ROWS):
            gs_own[pl.ds(i, 1), :] = jnp.sum(
                gx[2 + i, pl.ds(REACH, LONS), :].astype(F32), axis=0, keepdims=True
            )
        for dc in range(2):
            for step in range(N_LON):
                if dc or step:
                    gs_copy(dc, step).start()
        pltpu.make_async_copy(gs_own, gs_buf.at[lon], gs_sem).start()
        pole = lax.div(lat, N_LAT // 2)
        entry = lax.broadcasted_iota(jnp.int32, (16, 16), 0)
        source = lax.broadcasted_iota(jnp.int32, (16, 16), 1)
        row = source & 3
        first_q = polar_ref[2 * pole] - lat * ROWS
        second_q = polar_ref[2 * pole + 1] - lat * ROWS
        polar_row = jnp.where((entry & 1) == 0, first_q, second_q)
        moved = row + (source >> 2)
        for i in range(ROWS):
            moved = moved + jnp.where(row == i, offset_ref[i], 0)
        hit = (row == polar_row) & (moved == (entry >> 1) - 2) & (source < 12)
        z_copy.wait()
        zs[pl.ds(8, 8), :] = jnp.zeros((8, K * LONS), F32)
        for k in range(K):
            for r in range(3):
                zs[pl.ds(4 * r, 4), pl.ds(k * LONS, LONS)] = zv[k, r].astype(F32)
        picked = dot(jnp.where(hit, 1.0, 0.0).astype(BF16), zs[...].astype(BF16))
        yf[...] = jnp.zeros_like(yf)
        for k in range(K):
            for half in range(2):
                yf[half, pl.ds(k, 16, stride=16), :] = picked[:, k * LONS + 128 * half:k * LONS + 128 * half + 128]
        for half in range(2):
            yown[:, :, pl.ds(128 * half, 128)] = yf[half].astype(BF16).reshape(8, 32, 128)

    @pl.when(north)
    def _():
        y_halo(6).start()

    @pl.when(south)
    def _():
        y_halo(0).start()

    x_copy.wait()
    for i in range(ROWS):
        xt[:, pl.ds(i * LONS, LONS)] = xv[i].T
    def band_rows(rows, lanes, put):
        def band(step, carry):
            for k in (3 * step, 3 * step + 1, 3 * step + 2):
                for a in range(2):
                    row = jnp.broadcast_to(rows[pl.ds(16 * a + k, 1), :], (JB, lanes))
                    rolled = pltpu.roll(row, 0, 1, stride=1, stride_axis=0)
                    put(a)[pl.ds(pl.multiple_of(k * JB, JB), JB), :] = rolled.astype(BF16)
            return carry

        lax.fori_loop(0, K // 3, band, 0)

    def own_windows(i2, jb):
        windows = [gx[i2 + n, pl.ds(jb * JB, WIN), :] for n in range(CANDS)]
        windows.append(jnp.zeros((DEPTH - CANDS * WIN, C), BF16))
        return jnp.concatenate(windows, axis=0)

    def put_rows(i2, jb, k0, k1, moved):
        rows = pl.ds(pl.multiple_of(i2 * LONS + jb * JB, JB), JB)
        for k in range(k0, k1):
            hh[rows, pl.ds(k * C, C)] = moved[(k - k0) * JB:(k - k0 + 1) * JB]

    def spread_near(blocks):
        def spread(step, carry):
            for jb in blocks:
                i2 = near + step
                put_rows(i2, jb, 0, K, dot(tt[i2], own_windows(i2, jb)).astype(BF16))
            return carry

        lax.fori_loop(0, 2, spread, 0)

    def spread_far_own():
        def spread(step, carry):
            for jb in range(4):
                facc[4 * step + jb] = dot(tt[far + step], own_windows(far + step, jb))
            return carry

        lax.fori_loop(0, 2, spread, 0)

    def spread_far(k0, k1):
        at = pl.ds(k0 * JB, (k1 - k0) * JB)

        def spread(step, carry):
            for jb in range(4):
                windows = [gfar[n, pl.ds(jb * JB, WIN), :] for n in range(2)]
                windows.append(jnp.zeros((256 - 2 * WIN, C), BF16))
                moved = facc[4 * step + jb, at] + dot(tth[step, at], jnp.concatenate(windows, axis=0))
                put_rows(far + step, jb, k0, k1, moved.astype(BF16))
            return carry

        lax.fori_loop(0, 2, spread, 0)

    v_twin().wait_recv()
    arrive("twin", to_twin[:1])
    for a in range(2):
        vf[pl.ds(16 * a, 16), :] = vown[2 + near + a].astype(F32) + vtwin[a].astype(F32)
    band_rows(vf, DEPTH, lambda a: tt.at[near + a])
    spread_near((1, 2))
    for a in range(2):
        vf[pl.ds(16 * a, 16), :] = vown[2 + far + a].astype(F32)
    band_rows(vf, DEPTH, lambda a: tt.at[far + a])

    arrive("level", level)
    arrive("twin", to_twin[1:])
    spread_near((0, 3))
    spread_far_own()
    for i2 in range(ROWS):
        yy[i2] = yown[2 + i2]

    @pl.when(lat == 1)
    def _():
        y_halo(6).wait_recv()
        yy[pl.ds(0, 2)] = yh[...]

    @pl.when(lat == N_LAT - 2)
    def _():
        y_halo(0).wait_recv()
        yy[pl.ds(2, 2)] = yh[...]

    circle = jnp.zeros((C, 32), F32)
    for i2 in range(ROWS):
        circle = circle + dot(xt[:, pl.ds(i2 * LONS, LONS)], yy[i2], 1, 1)
    zst[...] = circle * FACTOR

    @pl.when(jnp.logical_not(affected))
    def _():
        gsel[...] = jnp.zeros_like(gsel)

    @pl.when(affected)
    def _():
        pltpu.make_async_copy(gs_buf, gs_buf, gs_sem).wait()
        total = gs_buf[0]
        for step in range(1, N_LON):
            total = total + gs_buf[step]
        pole = lax.div(lat, N_LAT // 2)
        gsel[...] = jnp.zeros_like(gsel)
        for q in range(2):
            mine = polar_ref[2 * pole + q] - pole * (N_LAT - 1) * ROWS
            picked = jnp.zeros((1, C), F32)
            for i in range(ROWS):
                picked = picked + total[i:i + 1] * (mine == i).astype(F32)
            gsel[pl.ds(q, 1), :] = picked

    near_lons = pl.ds(pl.multiple_of(near * LONS, 2 * LONS), 2 * LONS)
    far_lons = pl.ds(pl.multiple_of(far * LONS, 2 * LONS), 2 * LONS)
    for k in range(K):
        share = dot(xt[:, near_lons], hh[near_lons, pl.ds(k * C, C)]) * FACTOR
        for q in range(2):
            share = share + zst[:, 16 * q + k:16 * q + k + 1] * gsel[q:q + 1, :]
        wnear[k] = share

    @pl.when(has_far)
    def _():
        arrived(vfar, vrecv.at[1])

    for a in range(2):
        values = vfar[a].astype(F32)
        low_side = pltpu.roll(values, WIN * a, 1) if a else values
        high_side = pltpu.roll(values, 128 + WIN * a, 1)
        vfh[pl.ds(16 * a, 16), :] = jnp.where(core == 0, low_side, high_side)[:, :256]
    band_rows(vfh, 256, lambda a: tth.at[a])

    @pl.when(has_far)
    def _():
        arrive("far", to_far)

    def twin_copy(group):
        k0, k1 = GROUPS[group]
        at = pl.ds(k0, k1 - k0)
        return remote(wsnd.at[at], cx.at[at], cs_send.at[group], cs_recv.at[group], twin, lon)

    def mix(group):
        for k in range(*GROUPS[group]):
            share = wnear[k] + dot(xt[:, far_lons], hh[far_lons, pl.ds(k * C, C)]) * FACTOR
            first, second = share[:, :128], share[:, 128:]
            wown[k] = jnp.where(core == 0, first, second)
            wsnd[k] = jnp.where(core == 0, second, first).astype(BF16)
        twin_copy(group).start()

    def along_x(step):
        to = lax.rem(x + step, 4)
        return to, lat + 2 * (lax.div(to, 2) - x_high), lon + 4 * (lax.rem(to, 2) - x_low)

    def plane_copy(group, dx, dy):
        k0, k1 = GROUPS[group]
        at = pl.ds(k0, k1 - k0)
        to_x, to_lat, to_lon = along_x(dx)
        to_y = lax.rem(y + dy, 4)
        slot = 4 * dx + dy
        return remote(
            s1.at[at, to_y, to_x], rplane.at[slot, at], send_plane.at[group, slot], recv_plane.at[group],
            to_lat, to_lon + to_y - y,
        )

    others = [(dx, dy) for dx in range(4) for dy in range(4) if dx or dy]

    def first(group):
        twin_copy(group).wait_recv()
        for k in range(*GROUPS[group]):
            s1[k] = (wown[k] + cx[k].astype(F32)).astype(BF16).reshape(4, 4, 16, 128)
        for dx, dy in others:
            plane_copy(group, dx, dy).start()

    part = 4 * y + x

    def granule(k):
        q = 16 * k + part
        to_z = lax.div(q, 18)
        b = lax.div(q - 18 * to_z, 16)
        copy = remote(
            s3.at[k], r3.at[b, z], send3.at[k], recv3.at[b], 4 * to_z + in_plane, lon
        )
        return to_z, b, copy

    def second(group):
        k0, k1 = GROUPS[group]
        arrived(rplane.at[pl.ds(1, 15), pl.ds(k0, k1 - k0)], recv_plane.at[group])
        for k in range(k0, k1):
            total = s1[k, y, x].astype(F32)
            for dx, dy in others:
                total = total + rplane[4 * dx + dy, k].astype(F32)
            s3[k] = total.astype(BF16)
        for k in range(k0, k1):
            to_z, b, copy = granule(k)

            @pl.when(to_z != z)
            def _():
                copy.start()

            @pl.when(to_z == z)
            def _():
                pltpu.make_async_copy(s3.at[k], r3.at[b, z], recv3.at[b]).start()

    def owned(b):
        q = 16 * lax.div(18 * z - part + 15, 16) + part + 16 * b
        owner = lax.div(q, 9)
        return q <= 18 * z + 17, owner - 2 * z, q - 9 * owner

    def final_copy(b, to_high, e, dc, step):
        at = pl.ds(pl.multiple_of(16 * e, 16), 16)
        to_lat = 4 * z + 2 * to_high + (1 - core if dc else core)
        return remote(s4.at[b], fin.at[core, at], fs_send.at[b, dc, step], fs_recv, to_lat, lon_at(step))

    def needed(e, to_core):
        return ((to_core == 0) & (e <= 4)) | ((to_core == 1) & (e >= 4))

    def spread_out():
        for b in range(2):
            valid, to_high, e = owned(b)

            @pl.when(valid)
            def _():
                arrived(r3.at[b], recv3.at[b])
                total = r3[b, 0].astype(F32)
                for step in range(1, N_Z):
                    total = total + r3[b, step].astype(F32)
                s4[b] = total

            for dc in range(2):
                @pl.when(valid & needed(e, 1 - core if dc else core))
                def _():
                    for step in range(N_LON):
                        if dc or step:
                            final_copy(b, to_high, e, dc, step).start()
                        else:
                            @pl.when(to_high == x_high)
                            def _():
                                at = pl.ds(pl.multiple_of(16 * e, 16), 16)
                                pltpu.make_async_copy(s4.at[b], fin.at[core, at], fs_recv).start()

                            @pl.when(to_high != x_high)
                            def _():
                                final_copy(b, to_high, e, 0, 0).start()

    def prepare_pull():
        w_copy.wait()

        def turn(k, carry):
            at = pl.ds(pl.multiple_of(k * C, C), C)
            wt[at, :] = wv[at, :].T
            return carry

        lax.fori_loop(0, K, turn, 0)

        circle_sum = gsel[...]
        high = circle_sum.astype(BF16)
        low = (circle_sum - high.astype(F32)).astype(BF16)
        parts = jnp.concatenate([high.astype(F32), low.astype(F32)], axis=0).astype(BF16)
        ztf[...] = jnp.zeros_like(ztf)
        for k in range(K):
            mixed = dot(parts, wt[pl.ds(k * C, C), :])
            mixed = mixed[:8] + mixed[8:]
            for q in range(2):
                ztf[pl.ds(16 * q + k, 1), :] = mixed[q:q + 1]

        circle_total = ztf[...]
        z_high = circle_total.astype(BF16)
        z_low = (circle_total - z_high.astype(F32)).astype(BF16)
        z_parts = jnp.concatenate([z_high, z_low], axis=0)
        zparts[...] = z_parts

    def pull(half):
        z_parts = zparts[...]
        grad = dot(hh[pl.ds(half * 2 * LONS, 2 * LONS), :], wt[...])
        for a in range(2):
            i2 = 2 * half + a
            twice = jnp.concatenate([yy[i2], yy[i2]], axis=0)
            ig_ref[i2] = (grad[a * LONS:(a + 1) * LONS] + dot(twice, z_parts, 0, 0)).astype(BF16)

    spread_far(*GROUPS[0])
    mix(0)
    spread_far(*GROUPS[1])
    mix(1)
    first(0)
    spread_far(*GROUPS[2])
    mix(2)
    first(1)
    first(2)
    prepare_pull()
    pull(0)
    second(0)
    second(1)
    pull(1)
    second(2)
    spread_out()
    for move in level:
        halo("level", *move).wait_send()
    v_twin().wait_send()
    for move in to_twin:
        halo("twin", *move).wait_send()

    @pl.when(has_far)
    def _():
        v_far().wait_send()
        for move in to_far:
            halo("far", *move).wait_send()

    @pl.when(north)
    def _():
        y_halo(6).wait_send()

    @pl.when(south)
    def _():
        y_halo(0).wait_send()

    @pl.when(polar_dev)
    def _():
        for dc in range(2):
            for step in range(N_LON):
                if dc or step:
                    gs_copy(dc, step).wait_send()

    for group in range(len(GROUPS)):
        twin_copy(group).wait_send()
    for group in range(len(GROUPS)):
        for dx, dy in others:
            plane_copy(group, dx, dy).wait_send()
    for k in range(K):
        to_z, b, copy = granule(k)

        @pl.when(to_z != z)
        def _():
            copy.wait_send()

    some = fin.at[:, pl.ds(0, 80)]
    pltpu.make_async_copy(some, some, fs_recv).wait()
    rows = pl.ds(pl.multiple_of(72 * core, 8), 72)
    for half in range(2):
        wg_ref[:, pl.ds(128 * half, 128)] = fin[half, rows, :]

    for b in range(2):
        valid, to_high, e = owned(b)
        for dc in range(2):
            @pl.when(valid & needed(e, 1 - core if dc else core))
            def _():
                for step in range(N_LON):
                    if dc or step:
                        final_copy(b, to_high, e, dc, step).wait_send()
                    else:
                        @pl.when(to_high != x_high)
                        def _():
                            final_copy(b, to_high, e, 0, 0).wait_send()


def store(ig_ref, wg_ref, ig_hbm, wg_hbm, sem):
    copies = [
        pltpu.make_async_copy(ig_ref, ig_hbm, sem.at[0]),
        pltpu.make_async_copy(wg_ref, wg_hbm, sem.at[1]),
    ]
    for copy in copies:
        copy.start()
    for copy in copies:
        copy.wait()


def body(input_field, grad_out, weight, filt, zonal_weight, widths, offsets, polar_rows):
    dma = pltpu.SemaphoreType.DMA
    hbm = pl.BlockSpec(memory_space=pltpu.HBM)
    vmem = pl.BlockSpec(memory_space=pltpu.VMEM)
    groups = len(GROUPS)
    grads = pl.pallas_call(
        kernel,
        out_shape=(pltpu.VMEM((ROWS, LONS, C), BF16), pltpu.VMEM((72, C), F32)),
        in_specs=[hbm] * 8,
        out_specs=(vmem, vmem),
        scratch_shapes=[
            pltpu.VMEM((K, 3, ROWS, 2 * REACH + 1), BF16),
            pltpu.SMEM((ROWS,), jnp.int32), pltpu.SMEM((ROWS,), jnp.int32), pltpu.SMEM((4,), jnp.int32),
            pltpu.VMEM((8, LONS + 2 * REACH, C), BF16),
            pltpu.VMEM((2, LONS + 2 * REACH, C), BF16),
            pltpu.VMEM((ROWS, LONS, C), BF16),
            pltpu.VMEM((C, ROWS * LONS), BF16),
            pltpu.VMEM((K * C, C), BF16),
            pltpu.VMEM((K * C, C), BF16),
            pltpu.VMEM((CANDS, 128, 2 * REACH + 1), F32),
            pltpu.VMEM((8, 16, DEPTH), BF16),
            pltpu.VMEM((2, 16, DEPTH), BF16),
            pltpu.VMEM((2, 16, DEPTH), BF16),
            pltpu.VMEM((32, DEPTH), F32),
            pltpu.VMEM((32, 256), F32),
            pltpu.VMEM((ROWS, K * JB, DEPTH), BF16),
            pltpu.VMEM((2, K * JB, 256), BF16),
            pltpu.VMEM((8, K * JB, C), F32),
            pltpu.VMEM((ROWS * LONS, K * C), BF16),
            pltpu.VMEM((K, C, C), F32),
            pltpu.VMEM((K, 3, ROWS, LONS), BF16),
            pltpu.VMEM((16, K * LONS), F32),
            pltpu.VMEM((2, 256, 128), F32),
            pltpu.VMEM((8, 32, LONS), BF16),
            pltpu.VMEM((2, 32, LONS), BF16),
            pltpu.VMEM((ROWS, 32, LONS), BF16),
            pltpu.VMEM((32, C), F32),
            pltpu.VMEM((64, C), BF16),
            pltpu.VMEM((C, 32), F32),
            pltpu.VMEM((8, C), F32),
            pltpu.VMEM((N_LON, 8, C), F32),
            pltpu.VMEM((8, C), F32),
            pltpu.VMEM((K, C, 128), F32),
            pltpu.VMEM((K, C, 128), BF16),
            pltpu.VMEM((K, C, 128), BF16),
            pltpu.VMEM((K, 4, 4, 16, 128), BF16),
            pltpu.VMEM((16, K, 16, 128), BF16),
            pltpu.VMEM((K, 16, 128), BF16),
            pltpu.VMEM((2, N_Z, 16, 128), BF16),
            pltpu.VMEM((2, 16, 128), F32),
            pltpu.VMEM((2, 144, 128), F32),
            dma((8,)), dma((8,)), dma((8,)), dma((2,)), dma((2,)), dma, dma, dma((2, N_LON)), dma,
            dma((groups,)), dma((groups,)), dma((groups, 16)), dma((groups,)), dma((K,)), dma((2,)), dma((2, 2, N_LON)), dma,
        ],
        compiler_params=pltpu.CompilerParams(
            collective_id=0, has_side_effects=True, vmem_limit_bytes=48 * 1024 * 1024
        ),
        name="sphere_backward",
    )(*[
        pltpu.with_memory_space_constraint(array, pltpu.HBM)
        for array in (
            grad_out, input_field, weight, jnp.transpose(filt, (0, 2, 1, 3)),
            jnp.transpose(zonal_weight, (0, 2, 1, 3)), widths, offsets, polar_rows,
        )
    ])
    return tuple(pl.pallas_call(
        store,
        out_shape=(
            jax.ShapeDtypeStruct((ROWS, LONS, C), BF16),
            jax.ShapeDtypeStruct((72, C), F32),
        ),
        in_specs=[pl.BlockSpec(memory_space=pl.ANY)] * 2,
        out_specs=(pl.BlockSpec(memory_space=pl.ANY),) * 2,
        scratch_shapes=[dma((2,))],
        name="store",
    )(*[pltpu.with_memory_space_constraint(array, pltpu.VMEM) for array in grads]))


def solution(mesh):
    in_specs = (
        P("lat", "lon", None),
        P("lat", "lon", None),
        P(),
        P(None, "lat", None, None),
        P(None, "lat", None, None),
        P("lat"),
        P("lat"),
        P(),
    )
    out_specs = (P("lat", "lon", None), P("lat", None))
    return jax.shard_map(body, mesh=mesh, in_specs=in_specs, out_specs=out_specs, check_vma=False)
```

```python
import functools
import math

import jax
import jax.numpy as jnp
from jax import lax
from jax.experimental import pallas as pl
from jax.experimental.pallas import tpu as pltpu
from jax.sharding import PartitionSpec as P

MESH = pl.DeviceIdType.MESH
F32 = jnp.float32
BF16 = jnp.bfloat16
ROWS = 4
LONS = 256
C = 256
K = 9
REACH = 16
JB = 64
WIN = JB + 2 * REACH
CANDS = 5
DEPTH = 512
N_LAT = 32
N_LON = 8
N_Z = 8
GROUPS = ((0, 2), (2, 5), (5, 9))
FACTOR = 1.0 / math.sqrt(128 * 2048)


def dot(a, b, ca=1, cb=0):
    return lax.dot_general(a, b, (((ca,), (cb,)), ((), ())), preferred_element_type=F32)


def kernel(
    g_hbm, x_hbm, w_hbm, filt_hbm, z_hbm, width_hbm, offset_hbm, polar_hbm,
    ig_ref, wg_ref,
    filt_ref, width_ref, offset_ref, polar_ref,
    gx, gfar, xv, xt, wv, wt, lv, vown, vtwin, vfar, vf, vfh, tt, tth, facc, hh, wnear, zv, zs, yf, yown, yh, yy, ztf, zparts, zst, gs_own, gs_buf, gsel,
    wown, wsnd, cx, s1, rplane, s3, r3, s4, fin,
    loc_sem, halo_send, halo_recv, vsend, vrecv, ysend, yrecv, gs_send, gs_sem,
    cs_send, cs_recv, send_plane, recv_plane, send3, recv3, fs_send, fs_recv,
):
    lat = lax.axis_index("lat")
    lon = lax.axis_index("lon")
    core = lax.rem(lat, 2)
    twin = lat + 1 - 2 * core
    z, in_plane = lax.div(lat, 4), lax.rem(lat, 4)
    x_high, x_low, y = lax.div(in_plane, 2), lax.div(lon, 4), lax.rem(lon, 4)
    x = 2 * x_high + x_low

    def lon_at(step):
        return lax.rem(lon + step, N_LON)

    def remote(src, dst, send, recv, to_lat, to_lon):
        return pltpu.make_async_remote_copy(
            src_ref=src, dst_ref=dst, send_sem=send, recv_sem=recv,
            device_id={"lat": to_lat, "lon": to_lon}, device_id_type=MESH,
        )

    north, south = lat == 0, lat == N_LAT - 1
    polar_dev = north | south
    affected = polar_dev | (lat == 1) | (lat == N_LAT - 2)

    barrier = pltpu.get_barrier_semaphore()

    def greet(to_lat, to_lon):
        pl.semaphore_signal(barrier, inc=1, device_id={"lat": to_lat, "lon": to_lon}, device_id_type=MESH)

    outer = lat - 1 + 2 * core
    to_next = (core == 1) & (x_high == 1) & (z < N_Z - 1)
    to_last = (core == 0) & (x_high == 0) & (z > 0)
    crosses = to_next | to_last

    @pl.when(crosses)
    def _():
        for step in (0, 1, N_LON - 1):
            greet(outer, lon_at(step))

    def lat_at(step):
        return 4 * lax.rem(z + step, N_Z) + in_plane

    for step in range(1, N_Z):
        greet(lat_at(step), lon)
    for turn_lat in range(4):
        for step in range(N_LON):
            if turn_lat or step:
                greet(4 * z + lax.rem(in_plane + turn_lat, 4), lon_at(step))

    g_copy = pltpu.make_async_copy(g_hbm, gx.at[pl.ds(2, ROWS), pl.ds(REACH, LONS)], loc_sem.at[0])
    x_copy = pltpu.make_async_copy(x_hbm, xv, loc_sem.at[1])
    w_copy = pltpu.make_async_copy(w_hbm, wv, loc_sem.at[2])
    z_copy = pltpu.make_async_copy(
        z_hbm.at[:, :, :, pl.ds(pl.multiple_of(lon * LONS, LONS), LONS)], zv, loc_sem.at[3]
    )
    small = [
        pltpu.make_async_copy(src, dst, loc_sem.at[4 + index])
        for index, (src, dst) in enumerate(
            ((filt_hbm, filt_ref), (width_hbm, width_ref), (offset_hbm, offset_ref), (polar_hbm, polar_ref))
        )
    ]
    for copy in small:
        copy.start()
    g_copy.start()
    x_copy.start()
    w_copy.start()

    @pl.when(polar_dev)
    def _():
        z_copy.start()

    for copy in small:
        copy.wait()
    span = 2 * REACH + 1
    row_i = lax.broadcasted_iota(jnp.int32, (ROWS, span), 0)
    tap = lax.broadcasted_iota(jnp.int32, (ROWS, span), 1)
    offset_v = jnp.zeros((ROWS, span), jnp.int32)
    width_v = jnp.zeros((ROWS, span), jnp.int32)
    for i in range(ROWS):
        offset_v = jnp.where(row_i == i, offset_ref[i], offset_v)
        width_v = jnp.where(row_i == i, width_ref[i], width_v)
    keep = jnp.abs(tap - REACH) <= width_v
    choose = {m: jnp.where(keep & (offset_v == 2 - m), 1.0, 0.0) for m in (2, 3, 4)}
    lv[...] = jnp.zeros_like(lv)
    for k in range(K):
        values = [filt_ref[k, r].astype(F32) for r in range(3)]
        for n in range(CANDS):
            terms = [choose[n + r] * values[r] for r in range(3) if n + r in choose]
            lv[n, pl.ds((4 - n) * 16 + k, ROWS, stride=16), :] = functools.reduce(jnp.add, terms)
    tap = lax.broadcasted_iota(jnp.int32, (span, DEPTH), 0)
    lane = lax.broadcasted_iota(jnp.int32, (span, DEPTH), 1)
    placed = jnp.zeros((128, DEPTH), F32)
    for n in range(CANDS):
        where = jnp.where(lane + tap == WIN * n + 2 * REACH, 1.0, 0.0).astype(BF16)
        placed = placed + dot(lv[n].astype(BF16), where)
    vown[...] = placed.astype(BF16).reshape(8, 16, DEPTH)

    g_copy.wait()
    pl.semaphore_wait(barrier, 4 * N_LON + N_Z - 2 + 3 * crosses.astype(jnp.int32))

    has_far = (outer >= 0) & (outer < N_LAT)
    near, far = 2 - 2 * core, 2 * core
    cols_of = {-1: (0, REACH, REACH + LONS), 0: (0, LONS, REACH), 1: (LONS - REACH, REACH, 0)}
    level, to_twin, to_far = ((0, 1), (1, -1)), ((2, 0), (3, 1), (4, -1)), ((5, 0), (6, 1), (7, -1))

    def halo(kind, index, dlon):
        c0, cn, c_to = cols_of[dlon]
        cols, to_cols = pl.ds(REACH + c0, cn), pl.ds(c_to, cn)
        if kind == "level":
            src, dst, to_lat = gx.at[pl.ds(2, ROWS), cols], gx.at[pl.ds(2, ROWS), to_cols], lat
        elif kind == "twin":
            src, dst, to_lat = gx.at[pl.ds(2 + near, 2), cols], gx.at[pl.ds(6 * core, 2), to_cols], twin
        else:
            src, dst, to_lat = gx.at[pl.ds(2 + far, 2), cols], gfar.at[:, to_cols], outer
        return remote(
            src, dst, halo_send.at[index], halo_recv.at[index], to_lat, lon_at(dlon % N_LON),
        )

    def arrived(buffer, semaphore):
        pltpu.make_async_copy(buffer, buffer, semaphore).wait()

    def arrive(kind, moves):
        for index, dlon in moves:
            c0, cn, c_to = cols_of[dlon]
            cols = pl.ds(c_to, cn)
            if kind == "level":
                place_of = gx.at[pl.ds(2, ROWS), cols]
            elif kind == "twin":
                place_of = gx.at[pl.ds(6 - 6 * core, 2), cols]
            else:
                place_of = gfar.at[:, cols]
            arrived(place_of, halo_recv.at[index])

    def v_twin():
        return remote(vown.at[pl.ds(6 - 6 * core, 2)], vtwin, vsend.at[0], vrecv.at[0], twin, lon)

    def v_far():
        return remote(vown.at[pl.ds(6 * core, 2)], vfar, vsend.at[1], vrecv.at[1], outer, lon)

    for move in level:
        halo("level", *move).start()
    v_twin().start()
    for move in to_twin:
        halo("twin", *move).start()

    @pl.when(has_far)
    def _():
        v_far().start()
        for move in to_far[1:] + to_far[:1]:
            halo("far", *move).start()

    gx[pl.ds(6 * core, 2)] = jnp.zeros((2,) + gx.shape[1:], BF16)

    @pl.when(jnp.logical_not(has_far))
    def _():
        gfar[...] = jnp.zeros_like(gfar)
        vfar[...] = jnp.zeros_like(vfar)

    def gs_copy(dc, step):
        return remote(
            gs_own, gs_buf.at[lon], gs_send.at[dc, step], gs_sem, twin if dc else lat, lon_at(step)
        )

    def y_halo(first):
        return remote(yown.at[pl.ds(first, 2)], yh, ysend, yrecv, twin, lon)

    @pl.when(jnp.logical_not(polar_dev))
    def _():
        yown[...] = jnp.zeros_like(yown)

    @pl.when(polar_dev)
    def _():
        gs_own[...] = jnp.zeros_like(gs_own)
        for i in range(ROWS):
            gs_own[pl.ds(i, 1), :] = jnp.sum(
                gx[2 + i, pl.ds(REACH, LONS), :].astype(F32), axis=0, keepdims=True
            )
        for dc in range(2):
            for step in range(N_LON):
                if dc or step:
                    gs_copy(dc, step).start()
        pltpu.make_async_copy(gs_own, gs_buf.at[lon], gs_sem).start()
        pole = lax.div(lat, N_LAT // 2)
        entry = lax.broadcasted_iota(jnp.int32, (16, 16), 0)
        source = lax.broadcasted_iota(jnp.int32, (16, 16), 1)
        row = source & 3
        first_q = polar_ref[2 * pole] - lat * ROWS
        second_q = polar_ref[2 * pole + 1] - lat * ROWS
        polar_row = jnp.where((entry & 1) == 0, first_q, second_q)
        moved = row + (source >> 2)
        for i in range(ROWS):
            moved = moved + jnp.where(row == i, offset_ref[i], 0)
        hit = (row == polar_row) & (moved == (entry >> 1) - 2) & (source < 12)
        z_copy.wait()
        zs[pl.ds(8, 8), :] = jnp.zeros((8, K * LONS), F32)
        for k in range(K):
            for r in range(3):
                zs[pl.ds(4 * r, 4), pl.ds(k * LONS, LONS)] = zv[k, r].astype(F32)
        picked = dot(jnp.where(hit, 1.0, 0.0).astype(BF16), zs[...].astype(BF16))
        yf[...] = jnp.zeros_like(yf)
        for k in range(K):
            for half in range(2):
                yf[half, pl.ds(k, 16, stride=16), :] = picked[:, k * LONS + 128 * half:k * LONS + 128 * half + 128]
        for half in range(2):
            yown[:, :, pl.ds(128 * half, 128)] = yf[half].astype(BF16).reshape(8, 32, 128)

    @pl.when(north)
    def _():
        y_halo(6).start()

    @pl.when(south)
    def _():
        y_halo(0).start()

    x_copy.wait()
    for i in range(ROWS):
        xt[:, pl.ds(i * LONS, LONS)] = xv[i].T
    def band_rows(rows, lanes, put):
        def band(step, carry):
            for k in (3 * step, 3 * step + 1, 3 * step + 2):
                for a in range(2):
                    row = jnp.broadcast_to(rows[pl.ds(16 * a + k, 1), :], (JB, lanes))
                    rolled = pltpu.roll(row, 0, 1, stride=1, stride_axis=0)
                    put(a)[pl.ds(pl.multiple_of(k * JB, JB), JB), :] = rolled.astype(BF16)
            return carry

        lax.fori_loop(0, K // 3, band, 0)

    def own_windows(i2, jb):
        windows = [gx[i2 + n, pl.ds(jb * JB, WIN), :] for n in range(CANDS)]
        windows.append(jnp.zeros((DEPTH - CANDS * WIN, C), BF16))
        return jnp.concatenate(windows, axis=0)

    def put_rows(i2, jb, k0, k1, moved):
        rows = pl.ds(pl.multiple_of(i2 * LONS + jb * JB, JB), JB)
        for k in range(k0, k1):
            hh[rows, pl.ds(k * C, C)] = moved[(k - k0) * JB:(k - k0 + 1) * JB]

    def spread_near(blocks):
        def spread(step, carry):
            for jb in blocks:
                i2 = near + step
                put_rows(i2, jb, 0, K, dot(tt[i2], own_windows(i2, jb)).astype(BF16))
            return carry

        lax.fori_loop(0, 2, spread, 0)

    def spread_far_own():
        def spread(step, carry):
            for jb in range(4):
                facc[4 * step + jb] = dot(tt[far + step], own_windows(far + step, jb))
            return carry

        lax.fori_loop(0, 2, spread, 0)

    def spread_far(k0, k1):
        at = pl.ds(k0 * JB, (k1 - k0) * JB)

        def spread(step, carry):
            for jb in range(4):
                windows = [gfar[n, pl.ds(jb * JB, WIN), :] for n in range(2)]
                windows.append(jnp.zeros((256 - 2 * WIN, C), BF16))
                moved = facc[4 * step + jb, at] + dot(tth[step, at], jnp.concatenate(windows, axis=0))
                put_rows(far + step, jb, k0, k1, moved.astype(BF16))
            return carry

        lax.fori_loop(0, 2, spread, 0)

    v_twin().wait_recv()
    arrive("twin", to_twin[:1])
    for a in range(2):
        vf[pl.ds(16 * a, 16), :] = vown[2 + near + a].astype(F32) + vtwin[a].astype(F32)
    band_rows(vf, DEPTH, lambda a: tt.at[near + a])
    spread_near((1, 2))
    for a in range(2):
        vf[pl.ds(16 * a, 16), :] = vown[2 + far + a].astype(F32)
    band_rows(vf, DEPTH, lambda a: tt.at[far + a])

    arrive("level", level)
    arrive("twin", to_twin[1:])
    spread_near((0, 3))
    spread_far_own()
    for i2 in range(ROWS):
        yy[i2] = yown[2 + i2]

    @pl.when(lat == 1)
    def _():
        y_halo(6).wait_recv()
        yy[pl.ds(0, 2)] = yh[...]

    @pl.when(lat == N_LAT - 2)
    def _():
        y_halo(0).wait_recv()
        yy[pl.ds(2, 2)] = yh[...]

    circle = jnp.zeros((C, 32), F32)
    for i2 in range(ROWS):
        circle = circle + dot(xt[:, pl.ds(i2 * LONS, LONS)], yy[i2], 1, 1)
    zst[...] = circle * FACTOR

    @pl.when(jnp.logical_not(affected))
    def _():
        gsel[...] = jnp.zeros_like(gsel)

    @pl.when(affected)
    def _():
        pltpu.make_async_copy(gs_buf, gs_buf, gs_sem).wait()
        total = gs_buf[0]
        for step in range(1, N_LON):
            total = total + gs_buf[step]
        pole = lax.div(lat, N_LAT // 2)
        gsel[...] = jnp.zeros_like(gsel)
        for q in range(2):
            mine = polar_ref[2 * pole + q] - pole * (N_LAT - 1) * ROWS
            picked = jnp.zeros((1, C), F32)
            for i in range(ROWS):
                picked = picked + total[i:i + 1] * (mine == i).astype(F32)
            gsel[pl.ds(q, 1), :] = picked

    near_lons = pl.ds(pl.multiple_of(near * LONS, 2 * LONS), 2 * LONS)
    far_lons = pl.ds(pl.multiple_of(far * LONS, 2 * LONS), 2 * LONS)
    for k in range(K):
        share = dot(xt[:, near_lons], hh[near_lons, pl.ds(k * C, C)]) * FACTOR
        for q in range(2):
            share = share + zst[:, 16 * q + k:16 * q + k + 1] * gsel[q:q + 1, :]
        wnear[k] = share

    @pl.when(has_far)
    def _():
        arrived(vfar, vrecv.at[1])

    for a in range(2):
        values = vfar[a].astype(F32)
        low_side = pltpu.roll(values, WIN * a, 1) if a else values
        high_side = pltpu.roll(values, 128 + WIN * a, 1)
        vfh[pl.ds(16 * a, 16), :] = jnp.where(core == 0, low_side, high_side)[:, :256]
    band_rows(vfh, 256, lambda a: tth.at[a])

    @pl.when(has_far)
    def _():
        arrive("far", to_far)

    def twin_copy(group):
        k0, k1 = GROUPS[group]
        at = pl.ds(k0, k1 - k0)
        return remote(wsnd.at[at], cx.at[at], cs_send.at[group], cs_recv.at[group], twin, lon)

    def mix(group):
        for k in range(*GROUPS[group]):
            share = wnear[k] + dot(xt[:, far_lons], hh[far_lons, pl.ds(k * C, C)]) * FACTOR
            first, second = share[:, :128], share[:, 128:]
            wown[k] = jnp.where(core == 0, first, second)
            wsnd[k] = jnp.where(core == 0, second, first).astype(BF16)
        twin_copy(group).start()

    def along_x(step):
        to = lax.rem(x + step, 4)
        return to, lat + 2 * (lax.div(to, 2) - x_high), lon + 4 * (lax.rem(to, 2) - x_low)

    def plane_copy(group, dx, dy):
        k0, k1 = GROUPS[group]
        at = pl.ds(k0, k1 - k0)
        to_x, to_lat, to_lon = along_x(dx)
        to_y = lax.rem(y + dy, 4)
        slot = 4 * dx + dy
        return remote(
            s1.at[at, to_y, to_x], rplane.at[slot, at], send_plane.at[group, slot], recv_plane.at[group],
            to_lat, to_lon + to_y - y,
        )

    others = sorted(
        [(dx, dy) for dx in range(4) for dy in range(4) if dx or dy],
        key=lambda move: -min(move[0], 4 - move[0]) - min(move[1], 4 - move[1]),
    )

    def first(group):
        twin_copy(group).wait_recv()
        for k in range(*GROUPS[group]):
            s1[k] = (wown[k] + cx[k].astype(F32)).astype(BF16).reshape(4, 4, 16, 128)
        for dx, dy in others:
            plane_copy(group, dx, dy).start()

    part = 4 * y + x

    def granule(k):
        q = 16 * k + part
        to_z = lax.div(q, 18)
        b = lax.div(q - 18 * to_z, 16)
        copy = remote(
            s3.at[k], r3.at[b, z], send3.at[k], recv3.at[b], 4 * to_z + in_plane, lon
        )
        return to_z, b, copy

    def second(group):
        k0, k1 = GROUPS[group]
        arrived(rplane.at[pl.ds(1, 15), pl.ds(k0, k1 - k0)], recv_plane.at[group])
        for k in range(k0, k1):
            total = s1[k, y, x].astype(F32)
            for dx, dy in others:
                total = total + rplane[4 * dx + dy, k].astype(F32)
            s3[k] = total.astype(BF16)
        for k in range(k0, k1):
            to_z, b, copy = granule(k)

            @pl.when(to_z != z)
            def _():
                copy.start()

            @pl.when(to_z == z)
            def _():
                pltpu.make_async_copy(s3.at[k], r3.at[b, z], recv3.at[b]).start()

    def owned(b):
        q = 16 * lax.div(18 * z - part + 15, 16) + part + 16 * b
        owner = lax.div(q, 9)
        return q <= 18 * z + 17, owner - 2 * z, q - 9 * owner

    def final_copy(b, to_high, e, dc, step):
        at = pl.ds(pl.multiple_of(16 * e, 16), 16)
        to_lat = 4 * z + 2 * to_high + (1 - core if dc else core)
        return remote(s4.at[b], fin.at[core, at], fs_send.at[b, dc, step], fs_recv, to_lat, lon_at(step))

    def needed(e, to_core):
        return ((to_core == 0) & (e <= 4)) | ((to_core == 1) & (e >= 4))

    def spread_out():
        for b in range(2):
            valid, to_high, e = owned(b)

            @pl.when(valid)
            def _():
                arrived(r3.at[b], recv3.at[b])
                total = r3[b, 0].astype(F32)
                for step in range(1, N_Z):
                    total = total + r3[b, step].astype(F32)
                s4[b] = total

            for dc in range(2):
                @pl.when(valid & needed(e, 1 - core if dc else core))
                def _():
                    for step in range(N_LON):
                        if dc or step:
                            final_copy(b, to_high, e, dc, step).start()
                        else:
                            @pl.when(to_high == x_high)
                            def _():
                                at = pl.ds(pl.multiple_of(16 * e, 16), 16)
                                pltpu.make_async_copy(s4.at[b], fin.at[core, at], fs_recv).start()

                            @pl.when(to_high != x_high)
                            def _():
                                final_copy(b, to_high, e, 0, 0).start()

    def prepare_pull():
        w_copy.wait()

        def turn(k, carry):
            at = pl.ds(pl.multiple_of(k * C, C), C)
            wt[at, :] = wv[at, :].T
            return carry

        lax.fori_loop(0, K, turn, 0)

        circle_sum = gsel[...]
        high = circle_sum.astype(BF16)
        low = (circle_sum - high.astype(F32)).astype(BF16)
        parts = jnp.concatenate([high.astype(F32), low.astype(F32)], axis=0).astype(BF16)
        ztf[...] = jnp.zeros_like(ztf)
        for k in range(K):
            mixed = dot(parts, wt[pl.ds(k * C, C), :])
            mixed = mixed[:8] + mixed[8:]
            for q in range(2):
                ztf[pl.ds(16 * q + k, 1), :] = mixed[q:q + 1]

        circle_total = ztf[...]
        z_high = circle_total.astype(BF16)
        z_low = (circle_total - z_high.astype(F32)).astype(BF16)
        z_parts = jnp.concatenate([z_high, z_low], axis=0)
        zparts[...] = z_parts

    def pull(half):
        z_parts = zparts[...]
        grad = dot(hh[pl.ds(half * 2 * LONS, 2 * LONS), :], wt[...])
        for a in range(2):
            i2 = 2 * half + a
            twice = jnp.concatenate([yy[i2], yy[i2]], axis=0)
            ig_ref[i2] = (grad[a * LONS:(a + 1) * LONS] + dot(twice, z_parts, 0, 0)).astype(BF16)

    spread_far(*GROUPS[0])
    mix(0)
    spread_far(*GROUPS[1])
    mix(1)
    first(0)
    spread_far(*GROUPS[2])
    mix(2)
    first(1)
    first(2)
    prepare_pull()
    pull(0)
    second(0)
    second(1)
    pull(1)
    second(2)
    spread_out()
    for move in level:
        halo("level", *move).wait_send()
    v_twin().wait_send()
    for move in to_twin:
        halo("twin", *move).wait_send()

    @pl.when(has_far)
    def _():
        v_far().wait_send()
        for move in to_far:
            halo("far", *move).wait_send()

    @pl.when(north)
    def _():
        y_halo(6).wait_send()

    @pl.when(south)
    def _():
        y_halo(0).wait_send()

    @pl.when(polar_dev)
    def _():
        for dc in range(2):
            for step in range(N_LON):
                if dc or step:
                    gs_copy(dc, step).wait_send()

    for group in range(len(GROUPS)):
        twin_copy(group).wait_send()
    for group in range(len(GROUPS)):
        for dx, dy in others:
            plane_copy(group, dx, dy).wait_send()
    for k in range(K):
        to_z, b, copy = granule(k)

        @pl.when(to_z != z)
        def _():
            copy.wait_send()

    some = fin.at[:, pl.ds(0, 80)]
    pltpu.make_async_copy(some, some, fs_recv).wait()
    rows = pl.ds(pl.multiple_of(72 * core, 8), 72)
    for half in range(2):
        wg_ref[:, pl.ds(128 * half, 128)] = fin[half, rows, :]

    for b in range(2):
        valid, to_high, e = owned(b)
        for dc in range(2):
            @pl.when(valid & needed(e, 1 - core if dc else core))
            def _():
                for step in range(N_LON):
                    if dc or step:
                        final_copy(b, to_high, e, dc, step).wait_send()
                    else:
                        @pl.when(to_high != x_high)
                        def _():
                            final_copy(b, to_high, e, 0, 0).wait_send()


def store(ig_ref, wg_ref, ig_hbm, wg_hbm, sem):
    copies = [
        pltpu.make_async_copy(ig_ref, ig_hbm, sem.at[0]),
        pltpu.make_async_copy(wg_ref, wg_hbm, sem.at[1]),
    ]
    for copy in copies:
        copy.start()
    for copy in copies:
        copy.wait()


def body(input_field, grad_out, weight, filt, zonal_weight, widths, offsets, polar_rows):
    dma = pltpu.SemaphoreType.DMA
    hbm = pl.BlockSpec(memory_space=pltpu.HBM)
    vmem = pl.BlockSpec(memory_space=pltpu.VMEM)
    groups = len(GROUPS)
    grads = pl.pallas_call(
        kernel,
        out_shape=(pltpu.VMEM((ROWS, LONS, C), BF16), pltpu.VMEM((72, C), F32)),
        in_specs=[hbm] * 8,
        out_specs=(vmem, vmem),
        scratch_shapes=[
            pltpu.VMEM((K, 3, ROWS, 2 * REACH + 1), BF16),
            pltpu.SMEM((ROWS,), jnp.int32), pltpu.SMEM((ROWS,), jnp.int32), pltpu.SMEM((4,), jnp.int32),
            pltpu.VMEM((8, LONS + 2 * REACH, C), BF16),
            pltpu.VMEM((2, LONS + 2 * REACH, C), BF16),
            pltpu.VMEM((ROWS, LONS, C), BF16),
            pltpu.VMEM((C, ROWS * LONS), BF16),
            pltpu.VMEM((K * C, C), BF16),
            pltpu.VMEM((K * C, C), BF16),
            pltpu.VMEM((CANDS, 128, 2 * REACH + 1), F32),
            pltpu.VMEM((8, 16, DEPTH), BF16),
            pltpu.VMEM((2, 16, DEPTH), BF16),
            pltpu.VMEM((2, 16, DEPTH), BF16),
            pltpu.VMEM((32, DEPTH), F32),
            pltpu.VMEM((32, 256), F32),
            pltpu.VMEM((ROWS, K * JB, DEPTH), BF16),
            pltpu.VMEM((2, K * JB, 256), BF16),
            pltpu.VMEM((8, K * JB, C), F32),
            pltpu.VMEM((ROWS * LONS, K * C), BF16),
            pltpu.VMEM((K, C, C), F32),
            pltpu.VMEM((K, 3, ROWS, LONS), BF16),
            pltpu.VMEM((16, K * LONS), F32),
            pltpu.VMEM((2, 256, 128), F32),
            pltpu.VMEM((8, 32, LONS), BF16),
            pltpu.VMEM((2, 32, LONS), BF16),
            pltpu.VMEM((ROWS, 32, LONS), BF16),
            pltpu.VMEM((32, C), F32),
            pltpu.VMEM((64, C), BF16),
            pltpu.VMEM((C, 32), F32),
            pltpu.VMEM((8, C), F32),
            pltpu.VMEM((N_LON, 8, C), F32),
            pltpu.VMEM((8, C), F32),
            pltpu.VMEM((K, C, 128), F32),
            pltpu.VMEM((K, C, 128), BF16),
            pltpu.VMEM((K, C, 128), BF16),
            pltpu.VMEM((K, 4, 4, 16, 128), BF16),
            pltpu.VMEM((16, K, 16, 128), BF16),
            pltpu.VMEM((K, 16, 128), BF16),
            pltpu.VMEM((2, N_Z, 16, 128), BF16),
            pltpu.VMEM((2, 16, 128), F32),
            pltpu.VMEM((2, 144, 128), F32),
            dma((8,)), dma((8,)), dma((8,)), dma((2,)), dma((2,)), dma, dma, dma((2, N_LON)), dma,
            dma((groups,)), dma((groups,)), dma((groups, 16)), dma((groups,)), dma((K,)), dma((2,)), dma((2, 2, N_LON)), dma,
        ],
        compiler_params=pltpu.CompilerParams(
            collective_id=0, has_side_effects=True, vmem_limit_bytes=48 * 1024 * 1024
        ),
        name="sphere_backward",
    )(*[
        pltpu.with_memory_space_constraint(array, pltpu.HBM)
        for array in (
            grad_out, input_field, weight, jnp.transpose(filt, (0, 2, 1, 3)),
            jnp.transpose(zonal_weight, (0, 2, 1, 3)), widths, offsets, polar_rows,
        )
    ])
    return tuple(pl.pallas_call(
        store,
        out_shape=(
            jax.ShapeDtypeStruct((ROWS, LONS, C), BF16),
            jax.ShapeDtypeStruct((72, C), F32),
        ),
        in_specs=[pl.BlockSpec(memory_space=pl.ANY)] * 2,
        out_specs=(pl.BlockSpec(memory_space=pl.ANY),) * 2,
        scratch_shapes=[dma((2,))],
        name="store",
    )(*[pltpu.with_memory_space_constraint(array, pltpu.VMEM) for array in grads]))


def solution(mesh):
    in_specs = (
        P("lat", "lon", None),
        P("lat", "lon", None),
        P(),
        P(None, "lat", None, None),
        P(None, "lat", None, None),
        P("lat"),
        P("lat"),
        P(),
    )
    out_specs = (P("lat", "lon", None), P("lat", None))
    return jax.shard_map(body, mesh=mesh, in_specs=in_specs, out_specs=out_specs, check_vma=False)
```

```python
import functools
import math

import jax
import jax.numpy as jnp
from jax import lax
from jax.experimental import pallas as pl
from jax.experimental.pallas import tpu as pltpu
from jax.sharding import PartitionSpec as P

MESH = pl.DeviceIdType.MESH
F32 = jnp.float32
BF16 = jnp.bfloat16
ROWS = 4
LONS = 256
C = 256
K = 9
REACH = 16
JB = 64
WIN = JB + 2 * REACH
CANDS = 5
DEPTH = 512
N_LAT = 32
N_LON = 8
N_Z = 8
GROUPS = ((0, 2), (2, 4), (4, 6), (6, 9))
FACTOR = 1.0 / math.sqrt(128 * 2048)


def dot(a, b, ca=1, cb=0):
    return lax.dot_general(a, b, (((ca,), (cb,)), ((), ())), preferred_element_type=F32)


def kernel(
    g_hbm, x_hbm, w_hbm, filt_hbm, z_hbm, width_hbm, offset_hbm, polar_hbm,
    ig_ref, wg_ref,
    filt_ref, width_ref, offset_ref, polar_ref,
    gx, gfar, xv, xt, wv, wt, lv, vown, vtwin, vfar, vf, vfh, tt, tth, facc, hh, wnear, zv, zs, yf, yown, yh, yy, ztf, zparts, zst, gs_own, gs_buf, gsel,
    wown, wsnd, cx, s1, rplane, s3, r3, s4, fin,
    loc_sem, halo_send, halo_recv, vsend, vrecv, ysend, yrecv, gs_send, gs_sem,
    cs_send, cs_recv, send_plane, recv_plane, send3, recv3, fs_send, fs_recv,
):
    lat = lax.axis_index("lat")
    lon = lax.axis_index("lon")
    core = lax.rem(lat, 2)
    twin = lat + 1 - 2 * core
    z, in_plane = lax.div(lat, 4), lax.rem(lat, 4)
    x_high, x_low, y = lax.div(in_plane, 2), lax.div(lon, 4), lax.rem(lon, 4)
    x = 2 * x_high + x_low

    def lon_at(step):
        return lax.rem(lon + step, N_LON)

    def remote(src, dst, send, recv, to_lat, to_lon):
        return pltpu.make_async_remote_copy(
            src_ref=src, dst_ref=dst, send_sem=send, recv_sem=recv,
            device_id={"lat": to_lat, "lon": to_lon}, device_id_type=MESH,
        )

    north, south = lat == 0, lat == N_LAT - 1
    polar_dev = north | south
    affected = polar_dev | (lat == 1) | (lat == N_LAT - 2)

    barrier = pltpu.get_barrier_semaphore()

    def greet(to_lat, to_lon):
        pl.semaphore_signal(barrier, inc=1, device_id={"lat": to_lat, "lon": to_lon}, device_id_type=MESH)

    outer = lat - 1 + 2 * core
    to_next = (core == 1) & (x_high == 1) & (z < N_Z - 1)
    to_last = (core == 0) & (x_high == 0) & (z > 0)
    crosses = to_next | to_last

    @pl.when(crosses)
    def _():
        for step in (0, 1, N_LON - 1):
            greet(outer, lon_at(step))

    def lat_at(step):
        return 4 * lax.rem(z + step, N_Z) + in_plane

    for step in range(1, N_Z):
        greet(lat_at(step), lon)
    for turn_lat in range(4):
        for step in range(N_LON):
            if turn_lat or step:
                greet(4 * z + lax.rem(in_plane + turn_lat, 4), lon_at(step))

    g_copy = pltpu.make_async_copy(g_hbm, gx.at[pl.ds(2, ROWS), pl.ds(REACH, LONS)], loc_sem.at[0])
    x_copy = pltpu.make_async_copy(x_hbm, xv, loc_sem.at[1])
    w_copy = pltpu.make_async_copy(w_hbm, wv, loc_sem.at[2])
    z_copy = pltpu.make_async_copy(
        z_hbm.at[:, :, :, pl.ds(pl.multiple_of(lon * LONS, LONS), LONS)], zv, loc_sem.at[3]
    )
    small = [
        pltpu.make_async_copy(src, dst, loc_sem.at[4 + index])
        for index, (src, dst) in enumerate(
            ((filt_hbm, filt_ref), (width_hbm, width_ref), (offset_hbm, offset_ref), (polar_hbm, polar_ref))
        )
    ]
    for copy in small:
        copy.start()
    g_copy.start()
    x_copy.start()
    w_copy.start()

    @pl.when(polar_dev)
    def _():
        z_copy.start()

    for copy in small:
        copy.wait()
    span = 2 * REACH + 1
    row_i = lax.broadcasted_iota(jnp.int32, (ROWS, span), 0)
    tap = lax.broadcasted_iota(jnp.int32, (ROWS, span), 1)
    offset_v = jnp.zeros((ROWS, span), jnp.int32)
    width_v = jnp.zeros((ROWS, span), jnp.int32)
    for i in range(ROWS):
        offset_v = jnp.where(row_i == i, offset_ref[i], offset_v)
        width_v = jnp.where(row_i == i, width_ref[i], width_v)
    keep = jnp.abs(tap - REACH) <= width_v
    choose = {m: jnp.where(keep & (offset_v == 2 - m), 1.0, 0.0) for m in (2, 3, 4)}
    lv[...] = jnp.zeros_like(lv)
    for k in range(K):
        values = [filt_ref[k, r].astype(F32) for r in range(3)]
        for n in range(CANDS):
            terms = [choose[n + r] * values[r] for r in range(3) if n + r in choose]
            lv[n, pl.ds((4 - n) * 16 + k, ROWS, stride=16), :] = functools.reduce(jnp.add, terms)
    tap = lax.broadcasted_iota(jnp.int32, (span, DEPTH), 0)
    lane = lax.broadcasted_iota(jnp.int32, (span, DEPTH), 1)
    placed = jnp.zeros((128, DEPTH), F32)
    for n in range(CANDS):
        where = jnp.where(lane + tap == WIN * n + 2 * REACH, 1.0, 0.0).astype(BF16)
        placed = placed + dot(lv[n].astype(BF16), where)
    vown[...] = placed.astype(BF16).reshape(8, 16, DEPTH)

    g_copy.wait()
    pl.semaphore_wait(barrier, 4 * N_LON + N_Z - 2 + 3 * crosses.astype(jnp.int32))

    has_far = (outer >= 0) & (outer < N_LAT)
    near, far = 2 - 2 * core, 2 * core
    cols_of = {-1: (0, REACH, REACH + LONS), 0: (0, LONS, REACH), 1: (LONS - REACH, REACH, 0)}
    level, to_twin, to_far = ((0, 1), (1, -1)), ((2, 0), (3, 1), (4, -1)), ((5, 0), (6, 1), (7, -1))

    def halo(kind, index, dlon):
        c0, cn, c_to = cols_of[dlon]
        cols, to_cols = pl.ds(REACH + c0, cn), pl.ds(c_to, cn)
        if kind == "level":
            src, dst, to_lat = gx.at[pl.ds(2, ROWS), cols], gx.at[pl.ds(2, ROWS), to_cols], lat
        elif kind == "twin":
            src, dst, to_lat = gx.at[pl.ds(2 + near, 2), cols], gx.at[pl.ds(6 * core, 2), to_cols], twin
        else:
            src, dst, to_lat = gx.at[pl.ds(2 + far, 2), cols], gfar.at[:, to_cols], outer
        return remote(
            src, dst, halo_send.at[index], halo_recv.at[index], to_lat, lon_at(dlon % N_LON),
        )

    def arrived(buffer, semaphore):
        pltpu.make_async_copy(buffer, buffer, semaphore).wait()

    def arrive(kind, moves):
        for index, dlon in moves:
            c0, cn, c_to = cols_of[dlon]
            cols = pl.ds(c_to, cn)
            if kind == "level":
                place_of = gx.at[pl.ds(2, ROWS), cols]
            elif kind == "twin":
                place_of = gx.at[pl.ds(6 - 6 * core, 2), cols]
            else:
                place_of = gfar.at[:, cols]
            arrived(place_of, halo_recv.at[index])

    def v_twin():
        return remote(vown.at[pl.ds(6 - 6 * core, 2)], vtwin, vsend.at[0], vrecv.at[0], twin, lon)

    def v_far():
        return remote(vown.at[pl.ds(6 * core, 2)], vfar, vsend.at[1], vrecv.at[1], outer, lon)

    for move in level:
        halo("level", *move).start()
    v_twin().start()
    for move in to_twin:
        halo("twin", *move).start()

    @pl.when(has_far)
    def _():
        v_far().start()
        for move in to_far[1:] + to_far[:1]:
            halo("far", *move).start()

    gx[pl.ds(6 * core, 2)] = jnp.zeros((2,) + gx.shape[1:], BF16)

    @pl.when(jnp.logical_not(has_far))
    def _():
        gfar[...] = jnp.zeros_like(gfar)
        vfar[...] = jnp.zeros_like(vfar)

    def gs_copy(dc, step):
        return remote(
            gs_own, gs_buf.at[lon], gs_send.at[dc, step], gs_sem, twin if dc else lat, lon_at(step)
        )

    def y_halo(first):
        return remote(yown.at[pl.ds(first, 2)], yh, ysend, yrecv, twin, lon)

    @pl.when(jnp.logical_not(polar_dev))
    def _():
        yown[...] = jnp.zeros_like(yown)

    @pl.when(polar_dev)
    def _():
        gs_own[...] = jnp.zeros_like(gs_own)
        for i in range(ROWS):
            gs_own[pl.ds(i, 1), :] = jnp.sum(
                gx[2 + i, pl.ds(REACH, LONS), :].astype(F32), axis=0, keepdims=True
            )
        for dc in range(2):
            for step in range(N_LON):
                if dc or step:
                    gs_copy(dc, step).start()
        pltpu.make_async_copy(gs_own, gs_buf.at[lon], gs_sem).start()
        pole = lax.div(lat, N_LAT // 2)
        entry = lax.broadcasted_iota(jnp.int32, (16, 16), 0)
        source = lax.broadcasted_iota(jnp.int32, (16, 16), 1)
        row = source & 3
        first_q = polar_ref[2 * pole] - lat * ROWS
        second_q = polar_ref[2 * pole + 1] - lat * ROWS
        polar_row = jnp.where((entry & 1) == 0, first_q, second_q)
        moved = row + (source >> 2)
        for i in range(ROWS):
            moved = moved + jnp.where(row == i, offset_ref[i], 0)
        hit = (row == polar_row) & (moved == (entry >> 1) - 2) & (source < 12)
        z_copy.wait()
        zs[pl.ds(8, 8), :] = jnp.zeros((8, K * LONS), F32)
        for k in range(K):
            for r in range(3):
                zs[pl.ds(4 * r, 4), pl.ds(k * LONS, LONS)] = zv[k, r].astype(F32)
        picked = dot(jnp.where(hit, 1.0, 0.0).astype(BF16), zs[...].astype(BF16))
        yf[...] = jnp.zeros_like(yf)
        for k in range(K):
            for half in range(2):
                yf[half, pl.ds(k, 16, stride=16), :] = picked[:, k * LONS + 128 * half:k * LONS + 128 * half + 128]
        for half in range(2):
            yown[:, :, pl.ds(128 * half, 128)] = yf[half].astype(BF16).reshape(8, 32, 128)

    @pl.when(north)
    def _():
        y_halo(6).start()

    @pl.when(south)
    def _():
        y_halo(0).start()

    x_copy.wait()
    for i in range(ROWS):
        xt[:, pl.ds(i * LONS, LONS)] = xv[i].T
    def band_rows(rows, lanes, put):
        def band(step, carry):
            for k in (3 * step, 3 * step + 1, 3 * step + 2):
                for a in range(2):
                    row = jnp.broadcast_to(rows[pl.ds(16 * a + k, 1), :], (JB, lanes))
                    rolled = pltpu.roll(row, 0, 1, stride=1, stride_axis=0)
                    put(a)[pl.ds(pl.multiple_of(k * JB, JB), JB), :] = rolled.astype(BF16)
            return carry

        lax.fori_loop(0, K // 3, band, 0)

    def own_windows(i2, jb):
        windows = [gx[i2 + n, pl.ds(jb * JB, WIN), :] for n in range(CANDS)]
        windows.append(jnp.zeros((DEPTH - CANDS * WIN, C), BF16))
        return jnp.concatenate(windows, axis=0)

    def put_rows(i2, jb, k0, k1, moved):
        rows = pl.ds(pl.multiple_of(i2 * LONS + jb * JB, JB), JB)
        for k in range(k0, k1):
            hh[rows, pl.ds(k * C, C)] = moved[(k - k0) * JB:(k - k0 + 1) * JB]

    def spread_near(blocks):
        def spread(step, carry):
            for jb in blocks:
                i2 = near + step
                put_rows(i2, jb, 0, K, dot(tt[i2], own_windows(i2, jb)).astype(BF16))
            return carry

        lax.fori_loop(0, 2, spread, 0)

    def spread_far_own():
        def spread(step, carry):
            for jb in range(4):
                facc[4 * step + jb] = dot(tt[far + step], own_windows(far + step, jb))
            return carry

        lax.fori_loop(0, 2, spread, 0)

    def spread_far(k0, k1):
        at = pl.ds(k0 * JB, (k1 - k0) * JB)

        def spread(step, carry):
            for jb in range(4):
                windows = [gfar[n, pl.ds(jb * JB, WIN), :] for n in range(2)]
                windows.append(jnp.zeros((256 - 2 * WIN, C), BF16))
                moved = facc[4 * step + jb, at] + dot(tth[step, at], jnp.concatenate(windows, axis=0))
                put_rows(far + step, jb, k0, k1, moved.astype(BF16))
            return carry

        lax.fori_loop(0, 2, spread, 0)

    v_twin().wait_recv()
    arrive("twin", to_twin[:1])
    for a in range(2):
        vf[pl.ds(16 * a, 16), :] = vown[2 + near + a].astype(F32) + vtwin[a].astype(F32)
    band_rows(vf, DEPTH, lambda a: tt.at[near + a])
    spread_near((1, 2))
    for a in range(2):
        vf[pl.ds(16 * a, 16), :] = vown[2 + far + a].astype(F32)
    band_rows(vf, DEPTH, lambda a: tt.at[far + a])

    arrive("level", level)
    arrive("twin", to_twin[1:])
    spread_near((0, 3))
    spread_far_own()
    for i2 in range(ROWS):
        yy[i2] = yown[2 + i2]

    @pl.when(lat == 1)
    def _():
        y_halo(6).wait_recv()
        yy[pl.ds(0, 2)] = yh[...]

    @pl.when(lat == N_LAT - 2)
    def _():
        y_halo(0).wait_recv()
        yy[pl.ds(2, 2)] = yh[...]

    circle = jnp.zeros((C, 32), F32)
    for i2 in range(ROWS):
        circle = circle + dot(xt[:, pl.ds(i2 * LONS, LONS)], yy[i2], 1, 1)
    zst[...] = circle * FACTOR

    @pl.when(jnp.logical_not(affected))
    def _():
        gsel[...] = jnp.zeros_like(gsel)

    @pl.when(affected)
    def _():
        pltpu.make_async_copy(gs_buf, gs_buf, gs_sem).wait()
        total = gs_buf[0]
        for step in range(1, N_LON):
            total = total + gs_buf[step]
        pole = lax.div(lat, N_LAT // 2)
        gsel[...] = jnp.zeros_like(gsel)
        for q in range(2):
            mine = polar_ref[2 * pole + q] - pole * (N_LAT - 1) * ROWS
            picked = jnp.zeros((1, C), F32)
            for i in range(ROWS):
                picked = picked + total[i:i + 1] * (mine == i).astype(F32)
            gsel[pl.ds(q, 1), :] = picked

    near_lons = pl.ds(pl.multiple_of(near * LONS, 2 * LONS), 2 * LONS)
    far_lons = pl.ds(pl.multiple_of(far * LONS, 2 * LONS), 2 * LONS)
    for k in range(K):
        share = dot(xt[:, near_lons], hh[near_lons, pl.ds(k * C, C)]) * FACTOR
        for q in range(2):
            share = share + zst[:, 16 * q + k:16 * q + k + 1] * gsel[q:q + 1, :]
        wnear[k] = share

    @pl.when(has_far)
    def _():
        arrived(vfar, vrecv.at[1])

    for a in range(2):
        values = vfar[a].astype(F32)
        low_side = pltpu.roll(values, WIN * a, 1) if a else values
        high_side = pltpu.roll(values, 128 + WIN * a, 1)
        vfh[pl.ds(16 * a, 16), :] = jnp.where(core == 0, low_side, high_side)[:, :256]
    band_rows(vfh, 256, lambda a: tth.at[a])

    @pl.when(has_far)
    def _():
        arrive("far", to_far)

    def twin_copy(group):
        k0, k1 = GROUPS[group]
        at = pl.ds(k0, k1 - k0)
        return remote(wsnd.at[at], cx.at[at], cs_send.at[group], cs_recv.at[group], twin, lon)

    def mix(group):
        for k in range(*GROUPS[group]):
            share = wnear[k] + dot(xt[:, far_lons], hh[far_lons, pl.ds(k * C, C)]) * FACTOR
            first, second = share[:, :128], share[:, 128:]
            wown[k] = jnp.where(core == 0, first, second)
            wsnd[k] = jnp.where(core == 0, second, first).astype(BF16)
        twin_copy(group).start()

    def along_x(step):
        to = lax.rem(x + step, 4)
        return to, lat + 2 * (lax.div(to, 2) - x_high), lon + 4 * (lax.rem(to, 2) - x_low)

    def plane_copy(group, dx, dy):
        k0, k1 = GROUPS[group]
        at = pl.ds(k0, k1 - k0)
        to_x, to_lat, to_lon = along_x(dx)
        to_y = lax.rem(y + dy, 4)
        slot = 4 * dx + dy
        return remote(
            s1.at[at, to_y, to_x], rplane.at[slot, at], send_plane.at[group, slot], recv_plane.at[group],
            to_lat, to_lon + to_y - y,
        )

    others = sorted(
        [(dx, dy) for dx in range(4) for dy in range(4) if dx or dy],
        key=lambda move: -min(move[0], 4 - move[0]) - min(move[1], 4 - move[1]),
    )

    def first(group):
        twin_copy(group).wait_recv()
        for k in range(*GROUPS[group]):
            s1[k] = (wown[k] + cx[k].astype(F32)).astype(BF16).reshape(4, 4, 16, 128)
        for dx, dy in others:
            plane_copy(group, dx, dy).start()

    part = 4 * y + x

    def granule(k):
        q = 16 * k + part
        to_z = lax.div(q, 18)
        b = lax.div(q - 18 * to_z, 16)
        copy = remote(
            s3.at[k], r3.at[b, z], send3.at[k], recv3.at[b], 4 * to_z + in_plane, lon
        )
        return to_z, b, copy

    def second(group):
        k0, k1 = GROUPS[group]
        arrived(rplane.at[pl.ds(1, 15), pl.ds(k0, k1 - k0)], recv_plane.at[group])
        for k in range(k0, k1):
            total = s1[k, y, x].astype(F32)
            for dx, dy in others:
                total = total + rplane[4 * dx + dy, k].astype(F32)
            s3[k] = total.astype(BF16)
        for k in range(k0, k1):
            to_z, b, copy = granule(k)

            @pl.when(to_z != z)
            def _():
                copy.start()

            @pl.when(to_z == z)
            def _():
                pltpu.make_async_copy(s3.at[k], r3.at[b, z], recv3.at[b]).start()

    def owned(b):
        q = 16 * lax.div(18 * z - part + 15, 16) + part + 16 * b
        owner = lax.div(q, 9)
        return q <= 18 * z + 17, owner - 2 * z, q - 9 * owner

    def final_copy(b, to_high, e, dc, step):
        at = pl.ds(pl.multiple_of(16 * e, 16), 16)
        to_lat = 4 * z + 2 * to_high + (1 - core if dc else core)
        return remote(s4.at[b], fin.at[core, at], fs_send.at[b, dc, step], fs_recv, to_lat, lon_at(step))

    def needed(e, to_core):
        return ((to_core == 0) & (e <= 4)) | ((to_core == 1) & (e >= 4))

    def spread_out():
        for b in range(2):
            valid, to_high, e = owned(b)

            @pl.when(valid)
            def _():
                arrived(r3.at[b], recv3.at[b])
                total = r3[b, 0].astype(F32)
                for step in range(1, N_Z):
                    total = total + r3[b, step].astype(F32)
                s4[b] = total

            for dc in range(2):
                @pl.when(valid & needed(e, 1 - core if dc else core))
                def _():
                    for step in range(N_LON):
                        if dc or step:
                            final_copy(b, to_high, e, dc, step).start()
                        else:
                            @pl.when(to_high == x_high)
                            def _():
                                at = pl.ds(pl.multiple_of(16 * e, 16), 16)
                                pltpu.make_async_copy(s4.at[b], fin.at[core, at], fs_recv).start()

                            @pl.when(to_high != x_high)
                            def _():
                                final_copy(b, to_high, e, 0, 0).start()

    def prepare_pull():
        w_copy.wait()

        def turn(k, carry):
            at = pl.ds(pl.multiple_of(k * C, C), C)
            wt[at, :] = wv[at, :].T
            return carry

        lax.fori_loop(0, K, turn, 0)

        circle_sum = gsel[...]
        high = circle_sum.astype(BF16)
        low = (circle_sum - high.astype(F32)).astype(BF16)
        parts = jnp.concatenate([high.astype(F32), low.astype(F32)], axis=0).astype(BF16)
        ztf[...] = jnp.zeros_like(ztf)
        for k in range(K):
            mixed = dot(parts, wt[pl.ds(k * C, C), :])
            mixed = mixed[:8] + mixed[8:]
            for q in range(2):
                ztf[pl.ds(16 * q + k, 1), :] = mixed[q:q + 1]

        circle_total = ztf[...]
        z_high = circle_total.astype(BF16)
        z_low = (circle_total - z_high.astype(F32)).astype(BF16)
        z_parts = jnp.concatenate([z_high, z_low], axis=0)
        zparts[...] = z_parts

    def pull(half):
        z_parts = zparts[...]
        grad = dot(hh[pl.ds(half * 2 * LONS, 2 * LONS), :], wt[...])
        for a in range(2):
            i2 = 2 * half + a
            twice = jnp.concatenate([yy[i2], yy[i2]], axis=0)
            ig_ref[i2] = (grad[a * LONS:(a + 1) * LONS] + dot(twice, z_parts, 0, 0)).astype(BF16)

    spread_far(*GROUPS[0])
    mix(0)
    spread_far(*GROUPS[1])
    mix(1)
    first(0)
    spread_far(*GROUPS[2])
    mix(2)
    first(1)
    spread_far(*GROUPS[3])
    mix(3)
    first(2)
    first(3)
    prepare_pull()
    pull(0)
    second(0)
    second(1)
    pull(1)
    second(2)
    second(3)
    spread_out()
    for move in level:
        halo("level", *move).wait_send()
    v_twin().wait_send()
    for move in to_twin:
        halo("twin", *move).wait_send()

    @pl.when(has_far)
    def _():
        v_far().wait_send()
        for move in to_far:
            halo("far", *move).wait_send()

    @pl.when(north)
    def _():
        y_halo(6).wait_send()

    @pl.when(south)
    def _():
        y_halo(0).wait_send()

    @pl.when(polar_dev)
    def _():
        for dc in range(2):
            for step in range(N_LON):
                if dc or step:
                    gs_copy(dc, step).wait_send()

    for group in range(len(GROUPS)):
        twin_copy(group).wait_send()
    for group in range(len(GROUPS)):
        for dx, dy in others:
            plane_copy(group, dx, dy).wait_send()
    for k in range(K):
        to_z, b, copy = granule(k)

        @pl.when(to_z != z)
        def _():
            copy.wait_send()

    some = fin.at[:, pl.ds(0, 80)]
    pltpu.make_async_copy(some, some, fs_recv).wait()
    rows = pl.ds(pl.multiple_of(72 * core, 8), 72)
    for half in range(2):
        wg_ref[:, pl.ds(128 * half, 128)] = fin[half, rows, :]

    for b in range(2):
        valid, to_high, e = owned(b)
        for dc in range(2):
            @pl.when(valid & needed(e, 1 - core if dc else core))
            def _():
                for step in range(N_LON):
                    if dc or step:
                        final_copy(b, to_high, e, dc, step).wait_send()
                    else:
                        @pl.when(to_high != x_high)
                        def _():
                            final_copy(b, to_high, e, 0, 0).wait_send()


def store(ig_ref, wg_ref, ig_hbm, wg_hbm, sem):
    copies = [
        pltpu.make_async_copy(ig_ref, ig_hbm, sem.at[0]),
        pltpu.make_async_copy(wg_ref, wg_hbm, sem.at[1]),
    ]
    for copy in copies:
        copy.start()
    for copy in copies:
        copy.wait()


def body(input_field, grad_out, weight, filt, zonal_weight, widths, offsets, polar_rows):
    dma = pltpu.SemaphoreType.DMA
    hbm = pl.BlockSpec(memory_space=pltpu.HBM)
    vmem = pl.BlockSpec(memory_space=pltpu.VMEM)
    groups = len(GROUPS)
    grads = pl.pallas_call(
        kernel,
        out_shape=(pltpu.VMEM((ROWS, LONS, C), BF16), pltpu.VMEM((72, C), F32)),
        in_specs=[hbm] * 8,
        out_specs=(vmem, vmem),
        scratch_shapes=[
            pltpu.VMEM((K, 3, ROWS, 2 * REACH + 1), BF16),
            pltpu.SMEM((ROWS,), jnp.int32), pltpu.SMEM((ROWS,), jnp.int32), pltpu.SMEM((4,), jnp.int32),
            pltpu.VMEM((8, LONS + 2 * REACH, C), BF16),
            pltpu.VMEM((2, LONS + 2 * REACH, C), BF16),
            pltpu.VMEM((ROWS, LONS, C), BF16),
            pltpu.VMEM((C, ROWS * LONS), BF16),
            pltpu.VMEM((K * C, C), BF16),
            pltpu.VMEM((K * C, C), BF16),
            pltpu.VMEM((CANDS, 128, 2 * REACH + 1), F32),
            pltpu.VMEM((8, 16, DEPTH), BF16),
            pltpu.VMEM((2, 16, DEPTH), BF16),
            pltpu.VMEM((2, 16, DEPTH), BF16),
            pltpu.VMEM((32, DEPTH), F32),
            pltpu.VMEM((32, 256), F32),
            pltpu.VMEM((ROWS, K * JB, DEPTH), BF16),
            pltpu.VMEM((2, K * JB, 256), BF16),
            pltpu.VMEM((8, K * JB, C), F32),
            pltpu.VMEM((ROWS * LONS, K * C), BF16),
            pltpu.VMEM((K, C, C), F32),
            pltpu.VMEM((K, 3, ROWS, LONS), BF16),
            pltpu.VMEM((16, K * LONS), F32),
            pltpu.VMEM((2, 256, 128), F32),
            pltpu.VMEM((8, 32, LONS), BF16),
            pltpu.VMEM((2, 32, LONS), BF16),
            pltpu.VMEM((ROWS, 32, LONS), BF16),
            pltpu.VMEM((32, C), F32),
            pltpu.VMEM((64, C), BF16),
            pltpu.VMEM((C, 32), F32),
            pltpu.VMEM((8, C), F32),
            pltpu.VMEM((N_LON, 8, C), F32),
            pltpu.VMEM((8, C), F32),
            pltpu.VMEM((K, C, 128), F32),
            pltpu.VMEM((K, C, 128), BF16),
            pltpu.VMEM((K, C, 128), BF16),
            pltpu.VMEM((K, 4, 4, 16, 128), BF16),
            pltpu.VMEM((16, K, 16, 128), BF16),
            pltpu.VMEM((K, 16, 128), BF16),
            pltpu.VMEM((2, N_Z, 16, 128), BF16),
            pltpu.VMEM((2, 16, 128), F32),
            pltpu.VMEM((2, 144, 128), F32),
            dma((8,)), dma((8,)), dma((8,)), dma((2,)), dma((2,)), dma, dma, dma((2, N_LON)), dma,
            dma((groups,)), dma((groups,)), dma((groups, 16)), dma((groups,)), dma((K,)), dma((2,)), dma((2, 2, N_LON)), dma,
        ],
        compiler_params=pltpu.CompilerParams(
            collective_id=0, has_side_effects=True, vmem_limit_bytes=48 * 1024 * 1024
        ),
        name="sphere_backward",
    )(*[
        pltpu.with_memory_space_constraint(array, pltpu.HBM)
        for array in (
            grad_out, input_field, weight, jnp.transpose(filt, (0, 2, 1, 3)),
            jnp.transpose(zonal_weight, (0, 2, 1, 3)), widths, offsets, polar_rows,
        )
    ])
    return tuple(pl.pallas_call(
        store,
        out_shape=(
            jax.ShapeDtypeStruct((ROWS, LONS, C), BF16),
            jax.ShapeDtypeStruct((72, C), F32),
        ),
        in_specs=[pl.BlockSpec(memory_space=pl.ANY)] * 2,
        out_specs=(pl.BlockSpec(memory_space=pl.ANY),) * 2,
        scratch_shapes=[dma((2,))],
        name="store",
    )(*[pltpu.with_memory_space_constraint(array, pltpu.VMEM) for array in grads]))


def solution(mesh):
    in_specs = (
        P("lat", "lon", None),
        P("lat", "lon", None),
        P(),
        P(None, "lat", None, None),
        P(None, "lat", None, None),
        P("lat"),
        P("lat"),
        P(),
    )
    out_specs = (P("lat", "lon", None), P("lat", None))
    return jax.shard_map(body, mesh=mesh, in_specs=in_specs, out_specs=out_specs, check_vma=False)
```
